32 devices in a mesh: dp: 8 (over z, x), mp: 4 (over y, core).
Axes of the slice: x: 2, y: 2, z: 4, core: 2. Of those that a mesh axis runs over, the one named last changes fastest.
Arguments:
- tokens: bfloat16 [64, 256, 512], P('dp', 'mp'), may hold values from -6 to 6
- lengths: int32 [64], P('dp'), may hold values from 0 to 250, as said below
- order_mask: int32 [64, 256], P('dp'), may hold values from 0 to 1, as said below
- norm_scale_pair: float32 [2, 512], replicated, may hold values from 0.5 to 1.5
- norm_offset_pair: float32 [2, 512], replicated, may hold values from -1.75 to 1.75
- w_qkv: bfloat16 [3, 512, 512], P(None, None, 'mp'), may hold values from -0.25 to 0.25
- qv_bias: float32 [2, 512], P(None, 'mp'), may hold values from -1.75 to 1.75
- order_bias: float32 [8], P('mp'), may hold values from -2 to 2
- w_out: bfloat16 [512, 512], P('mp'), may hold values from -2 to 2
- out_bias: float32 [2, 512], replicated, may hold values from -1.75 to 1.75
- w_up: bfloat16 [512, 2048], P(None, 'mp'), may hold values from -0.25 to 0.25
- up_bias: float32 [2048], P('mp'), may hold values from -1.75 to 1.75
- w_down: bfloat16 [2048, 512], P('mp'), may hold values from -0.125 to 0.125
- cotangent: bfloat16 [64, 256, 512], P('dp', 'mp'), may hold values from -6 to 6
Outputs:
- output: bfloat16 [64, 256, 512], P('dp', 'mp')
- token_gradient: float32 [64, 256, 512], P('dp', 'mp')
- grad_norm_gain: float32 [2, 512], replicated
- grad_norm_shift: float32 [2, 512], replicated
- grad_qkv: float32 [3, 512, 512], P(None, None, 'mp')
- grad_qv_bias: float32 [2, 512], P(None, 'mp')
- grad_order_bias: float32 [8], P('mp')
- grad_out: float32 [512, 512], P('mp')
- grad_out_bias: float32 [2, 512], replicated
- grad_up: float32 [512, 2048], P(None, 'mp')
- grad_up_bias: float32 [2048], P('mp')
- grad_down: float32 [2048, 512], P('mp')
The draws below stay inside these ranges and needn't reach their ends.
Inputs may be any that keep to these rules, and one draw needn't show every extreme that they name: `lengths`: each length is 0, 64, 128 or 250; within the rows of one device the rows of length 0 come last, and their number may differ from device to device. `order_mask`: in each row the slots that come first in a random order are marked, their number random.
All inputs are finite; a program needn't handle non-finite values.
Results may differ from the reference program's by a relative error of at most 0.03.
Values may be sent and summed in bfloat16 or wider, within the bound.
No kernel may reach another device: no remote copies, remote signals or barrier semaphores. Data moves between devices by JAX's collectives and lax.ppermute only.
A program may use at most 128 MiB of HBM per device.

```python
import jax
import jax.numpy as jnp
from jax import lax

D = 512
H = 8
HD = 64
FF = 2048
S = 256
ROWS_DEV = 8
ROWS = 64


def draw_lengths(key, part):
    key = jax.random.fold_in(key, 11)
    key_count, key_pick = jax.random.split(key, 2)
    devices = ROWS // ROWS_DEV
    counts = jax.random.randint(key_count, (devices,), (ROWS_DEV + 1) // 2, ROWS_DEV + 1)
    counts = counts.at[0].set(ROWS_DEV).at[devices - 1].set(ROWS_DEV - 1)
    picks = jax.random.randint(key_pick, (ROWS,), 0, 3)
    table = jnp.array([S // 4, S // 2, S - 6], dtype=jnp.int32)
    chosen = jnp.sum(jnp.where(picks[:, None] == jnp.arange(3)[None, :], table[None, :], 0), axis=1)
    chosen = chosen.at[0].set(S - 6)
    index = jnp.arange(ROWS, dtype=jnp.int32)
    owner = index // ROWS_DEV
    place = index % ROWS_DEV
    limit = jnp.sum(jnp.where(owner[:, None] == jnp.arange(devices)[None, :], counts[None, :], 0), axis=1)
    return jnp.where(place < limit, chosen, 0).astype(jnp.int32)


def draw_order_mask(key, part):
    key = jax.random.fold_in(key, 23)
    key_step, key_perm = jax.random.split(key, 2)
    steps_done = jax.random.randint(key_step, (ROWS,), 0, S + 1)
    ranks = jax.vmap(lambda k: jax.random.permutation(k, S))(jax.random.split(key_perm, ROWS))
    return (ranks < steps_done[:, None]).astype(jnp.int32)


def steps_of(own_key, shape, pieces, least, top_value):
    factor_of, own = 1.0, jax.random.fold_in(own_key, 6)
    for axis_at, parts in pieces:
        steps = jnp.exp(jax.random.uniform(jax.random.fold_in(own, axis_at), (parts,), jnp.float32, least / len(pieces), top_value / len(pieces)))
        factor_of = factor_of * jnp.repeat(steps, shape[axis_at] // parts).reshape([-1 if axis == axis_at else 1 for axis in range(len(shape))])
    return factor_of


def bell_draw(own_key, extent, deviation, most, shards=(), kind=jnp.bfloat16):
    drawn = deviation * jax.random.normal(own_key, extent, jnp.float32)
    if shards:
        drawn = drawn * steps_of(own_key, extent, shards, -0.22, 0.18)
    return jnp.clip(drawn, -most, most).astype(kind)


def setup_inputs(seed: int = 0) -> dict:
    key_list = jax.random.split(jax.random.key(seed), 15)
    tokens = bell_draw(key_list[0], (ROWS, S, D), 1.0, 6.0, ((0, 8), (1, 4)))
    lengths = draw_lengths(jax.random.fold_in(key_list[14], 71), 0)
    order_mask = draw_order_mask(jax.random.fold_in(key_list[14], 71), 0)
    norm_scale_pair = jnp.clip(1.0 + 0.1 * jax.random.normal(key_list[3], (2, D), jnp.float32), 0.5, 1.5)
    norm_offset_pair = bell_draw(key_list[4], (2, D), 0.3, 1.75, (), jnp.float32)
    w_qkv = bell_draw(key_list[5], (3, D, H * HD), D ** -0.5, 0.25, ((2, 4),))
    qv_bias = bell_draw(key_list[6], (2, H * HD), 0.3, 1.75, ((1, 4),), jnp.float32)
    order_bias = jnp.clip(jax.random.uniform(key_list[7], (H,), jnp.float32, -2.0, 2.0) * steps_of(key_list[7], (H,), ((0, 4),), -0.4, 0.0), -2.0, 2.0)
    w_out = bell_draw(key_list[8], (H * HD, D), (max(D // 64, 1)) ** -0.5, 2.0, ((0, 4),))
    out_bias = bell_draw(key_list[9], (2, D), 0.3, 1.75, (), jnp.float32)
    w_up = bell_draw(key_list[10], (D, FF), D ** -0.5, 0.25, ((1, 4),))
    up_bias = bell_draw(key_list[11], (FF,), 0.3, 1.75, ((0, 4),), jnp.float32)
    w_down = bell_draw(key_list[12], (FF, D), FF ** -0.5, 0.125, ((0, 4),))
    cotangent = bell_draw(key_list[13], (ROWS, S, D), 1.0, 6.0, ((0, 8), (1, 4)))
    return dict(tokens=tokens, lengths=lengths, order_mask=order_mask, norm_scale_pair=norm_scale_pair, norm_offset_pair=norm_offset_pair, w_qkv=w_qkv, qv_bias=qv_bias, order_bias=order_bias, w_out=w_out, out_bias=out_bias, w_up=w_up, up_bias=up_bias, w_down=w_down, cotangent=cotangent)


@jax.custom_vjp
def low(v):
    return lax.optimization_barrier(v.astype(jnp.bfloat16)).astype(jnp.float32)

@jax.custom_vjp
def low_back(v):
    return v

def low_keep(v):
    return (low(v), None)

def low_pass(kept, output_gradient):
    return (output_gradient,)

def back_keep(v):
    return (v, None)

def back_low(kept, output_gradient):
    return (low(output_gradient),)
low.defvjp(low_keep, low_pass)
low_back.defvjp(back_keep, back_low)

def layer_normalizer(v):
    centre = v - lax.optimization_barrier(jnp.mean(v, -1, keepdims=True))
    return centre * lax.rsqrt(lax.optimization_barrier(jnp.mean(centre * centre, -1, keepdims=True)) + 1e-05)

def block(xg, keep_g, order_g, params):
    gains, shifts, wqkv, qvb, obias, wo, outb, wup, upb, wdown = params
    high = lax.Precision.HIGHEST
    count = xg.shape[0]
    first_attention = low(layer_normalizer(xg) * gains[0] + shifts[0])
    query = low_back(low(jnp.einsum('rsd,de->rse', first_attention, wqkv[0], precision=high) + qvb[0]))
    keyed = low_back(low(jnp.einsum('rsd,de->rse', first_attention, wqkv[1], precision=high)))
    value = low_back(low(jnp.einsum('rsd,de->rse', first_attention, wqkv[2], precision=high) + qvb[1]))
    query = query.reshape(count, S, H, HD)
    keyed = keyed.reshape(count, S, H, HD)
    value = value.reshape(count, S, H, HD)
    scores = jnp.einsum('rqhe,rkhe->rhqk', query, keyed, precision=high) * HD ** (-0.5)
    scores = scores + obias[None, :, None, None] * order_g[:, None, None, :]
    scores = low_back(scores)
    scores = jnp.where(keep_g[:, None, None, :] > 0.5, scores, -1e+30)
    probs = jax.nn.softmax(scores, axis=-1)
    attended = jnp.einsum('rhqk,rkhe->rqhe', low(probs), value, precision=high).reshape(count, S, H * HD)
    attended = low_back(low(attended * keep_g[:, :, None]))
    branch = low_back(jnp.einsum('rse,ed->rsd', attended, wo, precision=high) + outb[0])
    first_residual = xg + branch
    second_activation = low(layer_normalizer(first_residual) * gains[1] + shifts[1])
    pre = low_back(jnp.einsum('rsd,df->rsf', second_activation, wup, precision=high) + upb)
    hidden = low(jax.nn.gelu(pre, approximate=True))
    mixed = low_back(jnp.einsum('rsf,fd->rsd', hidden, wdown, precision=high) + outb[1])
    return first_residual + mixed

def reference(tokens, lengths, order_mask, norm_scale_pair, norm_offset_pair, w_qkv, qv_bias, order_bias, w_out, out_bias, w_up, up_bias, w_down, cotangent):
    params = tuple((p.astype(jnp.float32) for p in (norm_scale_pair, norm_offset_pair, w_qkv, qv_bias, order_bias, w_out, out_bias, w_up, up_bias, w_down)))
    input_single_float = tokens.astype(jnp.float32)
    keep = (jnp.arange(S, dtype=jnp.int32)[None, :] < lengths[:, None]).astype(jnp.float32)
    order_f = order_mask.astype(jnp.float32)
    groups = ROWS // ROWS_DEV

    def layer(xin, weights):

        def one(items):
            return block(items[0], items[1], items[2], weights)
        step = jax.checkpoint(one)
        result = lax.map(step, (xin.reshape(groups, ROWS_DEV, S, D), keep.reshape(groups, ROWS_DEV, S), order_f.reshape(groups, ROWS_DEV, S)))
        return result.reshape(ROWS, S, D)
    output, pull = jax.vjp(layer, input_single_float, params)
    d_input, grads = pull(cotangent.astype(jnp.float32))
    return (output.astype(jnp.bfloat16), d_input, grads[0], grads[1], grads[2], grads[3], grads[4], grads[5], grads[6], grads[7], grads[8], grads[9])
```

```python
import jax
import jax.numpy as jnp
from jax import lax
from jax.sharding import PartitionSpec as P

HD = 64
F32 = jnp.float32
BF16 = jnp.bfloat16


def swap(v, axis, bit, size):
    return lax.ppermute(v, axis, [(i, i ^ bit) for i in range(size)])


def bits_of(size):
    return [1 << b for b in range(size.bit_length() - 1)]


def normalize(v):
    centre = v - jnp.mean(v, -1, keepdims=True)
    rstd = lax.rsqrt(jnp.mean(centre * centre, -1, keepdims=True) + 1e-05)
    return centre * rstd, rstd


def norm_back(g, normed, rstd, gain):
    e = g * gain
    return rstd * (
        e - jnp.mean(e, -1, keepdims=True) - normed * jnp.mean(e * normed, -1, keepdims=True)
    )


def gelu_fn(v):
    return jax.nn.gelu(v, approximate=True)


def make_body(n_dp, n_mp):
    def gather_mp(v):
        blocks = {0: v}
        for bit in reversed(bits_of(n_mp)):
            for k in list(blocks):
                blocks[k ^ bit] = swap(blocks[k], "mp", bit, n_mp)
        return [blocks[k] for k in range(n_mp)]

    def body(
        tokens,
        lengths,
        order_mask,
        norm_scale_pair,
        norm_offset_pair,
        w_qkv,
        qv_bias,
        order_bias,
        w_out,
        out_bias,
        w_up,
        up_bias,
        w_down,
        cotangent,
    ):
        rows, share, width = tokens.shape
        slots = order_mask.shape[1]
        own_rows = rows // n_mp
        me = lax.axis_index("mp")
        dpi = lax.axis_index("dp")
        factor = HD**-0.5

        def to_rows(v):
            parts = []
            for k in range(n_mp):
                part = lax.dynamic_slice_in_dim(v, (me ^ k) * own_rows, own_rows, 0)
                parts.append(part if k == 0 else swap(part, "mp", k, n_mp))
            return jnp.concatenate(parts, 1)

        def from_rows(v):
            parts = []
            for k in range(n_mp):
                part = v[:, k * share : (k + 1) * share]
                parts.append(part if k == 0 else swap(part, "mp", k, n_mp))
            stacked = jnp.stack(parts)
            natural = jnp.take(stacked, me ^ jnp.arange(n_mp), axis=0)
            return natural.reshape(rows, share, width)

        x_bf = to_rows(tokens)
        w_qkv_all = jnp.concatenate(gather_mp(w_qkv), 2)
        small = jnp.concatenate([qv_bias.reshape(-1), up_bias, order_bias])
        smalls = gather_mp(small)
        lane = qv_bias.shape[1]
        hid = up_bias.shape[0]
        qv_bias_all = jnp.concatenate([s[: 2 * lane].reshape(2, lane) for s in smalls], 1)
        up_bias_all = jnp.concatenate([s[2 * lane : 2 * lane + hid] for s in smalls])
        order_bias_all = jnp.concatenate([s[2 * lane + hid :] for s in smalls])
        w_out_all = jnp.concatenate(gather_mp(w_out), 0)
        dy_bf = to_rows(cotangent)
        w_up_all = jnp.concatenate(gather_mp(w_up), 1)
        w_down_all = jnp.concatenate(gather_mp(w_down), 0)

        slot_of = jnp.concatenate([(me ^ k) * share + jnp.arange(share) for k in range(n_mp)])
        own_len = lax.dynamic_slice_in_dim(lengths, me * own_rows, own_rows, 0)
        own_order = jnp.take(
            lax.dynamic_slice_in_dim(order_mask, me * own_rows, own_rows, 0), slot_of, axis=1
        )
        keep = slot_of[None, :] < own_len[:, None]
        keep_f = keep.astype(F32)
        heads = w_out_all.shape[0] // HD

        x = x_bf.astype(F32)
        n1, rstd1 = normalize(x)
        a1 = (n1 * norm_scale_pair[0] + norm_offset_pair[0]).astype(BF16)
        proj = jnp.einsum("rsd,tde->trse", a1, w_qkv_all, preferred_element_type=F32)
        split = (own_rows, slots, heads, HD)
        query = (proj[0] + qv_bias_all[0]).astype(BF16).reshape(split)
        keyed = proj[1].astype(BF16).reshape(split)
        value = (proj[2] + qv_bias_all[1]).astype(BF16).reshape(split)
        raw = jnp.einsum("rqhe,rkhe->rhqk", query, keyed, preferred_element_type=F32) * factor
        raw = raw + order_bias_all[None, :, None, None] * own_order.astype(F32)[:, None, None, :]
        scores = jnp.where(keep[:, None, None, :], raw, -1e30)
        expo = jnp.exp(scores - jnp.max(scores, -1, keepdims=True))
        probs = expo / jnp.sum(expo, -1, keepdims=True)
        probs_bf = probs.astype(BF16)
        attended = jnp.einsum("rhqk,rkhe->rqhe", probs_bf, value, preferred_element_type=F32)
        attended = (attended.reshape(own_rows, slots, heads * HD) * keep_f[:, :, None]).astype(BF16)
        x1 = x + jnp.dot(attended, w_out_all, preferred_element_type=F32) + out_bias[0]
        n2, rstd2 = normalize(x1)
        a2 = (n2 * norm_scale_pair[1] + norm_offset_pair[1]).astype(BF16)
        pre = jnp.dot(a2, w_up_all, preferred_element_type=F32) + up_bias_all
        gelu_out, gelu_pull = jax.vjp(gelu_fn, pre)
        hidden = gelu_out.astype(BF16)
        mixed = jnp.dot(hidden, w_down_all, preferred_element_type=F32)
        output = from_rows((x1 + mixed + out_bias[1]).astype(BF16))

        dy = dy_bf.astype(F32)
        g_down = jnp.einsum("rsf,rsd->fd", hidden, dy_bf, preferred_element_type=F32)
        d_hidden = jnp.dot(dy_bf, w_down_all.T, preferred_element_type=F32)
        d_pre = gelu_pull(d_hidden)[0].astype(BF16)
        g_up = jnp.einsum("rsf,rsd->fd", d_pre, a2, preferred_element_type=F32)
        g_up_bias = jnp.sum(d_pre.astype(F32), (0, 1))
        d_mid = jnp.dot(d_pre, w_up_all.T, preferred_element_type=F32)
        dx1 = dy + norm_back(d_mid, n2, rstd2, norm_scale_pair[1])
        d_att = dx1.astype(BF16)
        g_out = jnp.einsum("rse,rsd->ed", attended, d_att, preferred_element_type=F32)
        d_o = jnp.dot(d_att, w_out_all.T, preferred_element_type=F32).astype(BF16)
        d_o = (d_o * keep_f[:, :, None].astype(BF16)).reshape(split)
        d_value = jnp.einsum("rhqk,rqhe->rkhe", probs_bf, d_o, preferred_element_type=F32)
        d_probs = jnp.einsum("rqhe,rkhe->rhqk", d_o, value, preferred_element_type=F32)
        d_scores = probs * (d_probs - jnp.sum(probs * d_probs, -1, keepdims=True))
        d_scores = jnp.where(keep[:, None, None, :], d_scores, 0.0).astype(BF16)
        g_order = jnp.einsum(
            "rhqk,rk->h", d_scores, own_order.astype(BF16), preferred_element_type=F32
        )
        d_query = jnp.einsum("rhqk,rkhe->rqhe", d_scores, keyed, preferred_element_type=F32)
        d_key = jnp.einsum("rhqk,rqhe->rkhe", d_scores, query, preferred_element_type=F32)
        stacked = jnp.stack(
            [
                (d_query * factor).astype(BF16),
                (d_key * factor).astype(BF16),
                d_value.astype(BF16),
            ]
        ).reshape(3, own_rows, slots, heads * HD)
        g_qkv = jnp.einsum("trse,rsd->ted", stacked, a1, preferred_element_type=F32)
        g_q_bias = jnp.sum(stacked[0].astype(F32), (0, 1))
        g_v_bias = jnp.sum(stacked[2].astype(F32), (0, 1))
        d_in = jnp.einsum("trse,tde->rsd", stacked, w_qkv_all, preferred_element_type=F32)
        token_gradient = dx1 + norm_back(d_in, n1, rstd1, norm_scale_pair[0])
        token_gradient = from_rows(token_gradient.astype(BF16)).astype(F32)

        shared = jnp.stack(
            [
                jnp.sum(d_in * n1, (0, 1)),
                jnp.sum(d_mid * n2, (0, 1)),
                jnp.sum(d_in, (0, 1)),
                jnp.sum(d_mid, (0, 1)),
                jnp.sum(d_att.astype(F32), (0, 1)),
                jnp.sum(dy, (0, 1)),
            ]
        )

        mp_bits, dp_bits = bits_of(n_mp), bits_of(n_dp)
        dp_sub = jnp.zeros((1,), jnp.int32)
        for bit in reversed(dp_bits):
            dp_sub = jnp.concatenate([dp_sub, dp_sub + bit])
        mp_order = [0]
        for bit in reversed(mp_bits):
            mp_order = mp_order + [k + bit for k in mp_order]

        def reduce(parts):
            m = parts[0].shape[0]
            cut = [p.astype(BF16).reshape(n_dp, m // n_dp, -1) for p in parts]
            full = jnp.stack([jnp.take(cut[k], dpi ^ dp_sub, axis=0) for k in mp_order])
            steps = [("mp", bit, n_mp) for bit in mp_bits] + [("dp", bit, n_dp) for bit in dp_bits]
            v = full.reshape([2] * len(steps) + list(full.shape[2:]))
            for axis, bit, size in steps:
                v = (v[0].astype(F32) + swap(v[1], axis, bit, size).astype(F32)).astype(BF16)
            v = v[None]
            for bit in reversed(dp_bits):
                v = jnp.concatenate([v, swap(v, "dp", bit, n_dp)])
            place = jnp.argsort(dpi ^ dp_sub)
            return jnp.take(v, place, axis=0).reshape(m, -1).astype(F32)

        def blocks_of(v, axis):
            return jnp.split(v, n_mp, axis)

        r_down = reduce(blocks_of(g_down, 0))
        r_up = reduce(blocks_of(g_up, 0)).T
        r_att = reduce(
            [
                jnp.concatenate([q.reshape(-1, width), o])
                for q, o in zip(blocks_of(g_qkv, 1), blocks_of(g_out, 0))
            ]
        )
        r_qkv = r_att[: 3 * lane].reshape(3, lane, width).transpose(0, 2, 1)
        r_out = r_att[3 * lane :]

        per_head = order_bias.shape[0]
        owned = jnp.stack(
            [
                jnp.concatenate([a, b, c, d])
                for a, b, c, d in zip(
                    blocks_of(g_q_bias, 0),
                    blocks_of(g_v_bias, 0),
                    blocks_of(g_up_bias, 0),
                    blocks_of(g_order, 0),
                )
            ]
        )
        owned = jnp.stack([owned[k] for k in mp_order])
        flat = shared.reshape(-1)
        count = flat.shape[0]
        for bit in mp_bits:
            half = owned.shape[0] // 2
            got = swap(jnp.concatenate([flat, owned[half:].reshape(-1)]), "mp", bit, n_mp)
            flat = flat + got[:count]
            owned = owned[:half] + got[count:].reshape(half, -1)
        flat = jnp.concatenate([flat, owned[0]])
        for bit in dp_bits:
            flat = flat + swap(flat, "dp", bit, n_dp)
        shared = flat[:count].reshape(6, width)
        owned = flat[count:]
        return (
            output,
            token_gradient,
            shared[0:2],
            shared[2:4],
            r_qkv,
            owned[: 2 * lane].reshape(2, lane),
            owned[2 * lane + hid :],
            r_out,
            shared[4:6],
            r_up,
            owned[2 * lane : 2 * lane + hid],
            r_down,
        )

    return body


def solution(mesh):
    return jax.shard_map(
        make_body(mesh.shape["dp"], mesh.shape["mp"]),
        mesh=mesh,
        in_specs=(
            P("dp", "mp", None),
            P("dp"),
            P("dp", None),
            P(),
            P(),
            P(None, None, "mp"),
            P(None, "mp"),
            P("mp"),
            P("mp", None),
            P(),
            P(None, "mp"),
            P("mp"),
            P("mp", None),
            P("dp", "mp", None),
        ),
        out_specs=(
            P("dp", "mp", None),
            P("dp", "mp", None),
            P(),
            P(),
            P(None, None, "mp"),
            P(None, "mp"),
            P("mp"),
            P("mp", None),
            P(),
            P(None, "mp"),
            P("mp"),
            P("mp", None),
        ),
        check_vma=False,
    )
```

```python
import jax
import jax.numpy as jnp
from jax import lax
from jax.experimental import pallas as pl
from jax.experimental.pallas import tpu as pltpu
from jax.sharding import PartitionSpec as P

HD = 64
PAIR = 2 * HD
LANES = 128
F32 = jnp.float32
BF16 = jnp.bfloat16
VMEM_LIMIT = 48 * 2**20
GELU_C = 0.7978845608028654
GELU_A = 0.044715
VEC = 8


def swap(v, axis, bit, size):
    return lax.ppermute(v, axis, [(i, i ^ bit) for i in range(size)])


def shape(dims, kind):
    return jax.ShapeDtypeStruct(tuple(dims), kind)


def run(name, fn, ins, outs, scratch=(), flops=0, smem=()):
    n_in, n_out = len(ins), len(outs)

    def kernel(*refs):
        fn(refs[:n_in], refs[n_in : n_in + n_out], refs[n_in + n_out :])

    moved = sum(v.size * v.dtype.itemsize for v in list(ins) + list(outs))
    return pl.pallas_call(
        kernel,
        out_shape=tuple(outs),
        in_specs=[
            pl.BlockSpec(memory_space=pltpu.SMEM if i in smem else pltpu.VMEM)
            for i in range(n_in)
        ],
        out_specs=tuple(pl.BlockSpec(memory_space=pltpu.VMEM) for _ in outs),
        scratch_shapes=list(scratch),
        compiler_params=pltpu.CompilerParams(vmem_limit_bytes=VMEM_LIMIT),
        cost_estimate=pl.CostEstimate(flops=int(flops), bytes_accessed=int(moved), transcendentals=0),
        name=name,
    )(*ins)


def dot(a, b):
    return jnp.dot(a, b, preferred_element_type=F32)


def dot_nt(a, b):
    return lax.dot_general(a, b, (((1,), (1,)), ((), ())), preferred_element_type=F32)


def dot_tn(a, b):
    return lax.dot_general(a, b, (((0,), (0,)), ((), ())), preferred_element_type=F32)


def normalize(v):
    centre = v - jnp.mean(v, -1, keepdims=True)
    rstd = lax.rsqrt(jnp.mean(centre * centre, -1, keepdims=True) + 1e-05)
    return centre * rstd, rstd


def norm_back(g, normed, rstd, gain):
    e = g * gain
    return rstd * (
        e - jnp.mean(e, -1, keepdims=True) - normed * jnp.mean(e * normed, -1, keepdims=True)
    )


def rows_of(start, size):
    return pl.ds(pl.multiple_of(start * size, size), size)


def place(dst, lanes, pieces, x_bit):
    if len(pieces) == 1:
        dst[:, lanes] = pieces[0][...]
        return
    half = dst.shape[0] // 2
    a, b = pieces[0][...], pieces[1][...]
    dst[:half, lanes] = jnp.where(x_bit == 0, a, b)
    dst[half:, lanes] = jnp.where(x_bit == 0, b, a)


def place_rows(dst, start, size, pieces, x_bit):
    if len(pieces) == 1:
        dst[start : start + size] = pieces[0][...]
        return
    half = size // 2
    a, b = pieces[0][...], pieces[1][...]
    dst[start : start + half] = jnp.where(x_bit == 0, a, b)
    dst[start + half : start + size] = jnp.where(x_bit == 0, b, a)


def take(refs, counts):
    out, at = [], 0
    for c in counts:
        out.append(refs[at : at + c])
        at += c
    assert at == len(refs)
    return out


def make_body(n_dp, n_mp):
    n_z = n_dp // 2
    groups = [[0, 1], list(range(2, n_mp))]

    def body(
        tokens,
        lengths,
        order_mask,
        norm_scale_pair,
        norm_offset_pair,
        w_qkv,
        qv_bias,
        order_bias,
        w_out,
        out_bias,
        w_up,
        up_bias,
        w_down,
        cotangent,
    ):
        rows, share, width = tokens.shape
        slots = order_mask.shape[1]
        own = rows // n_mp
        count = own * slots
        lane = qv_bias.shape[1]
        per = order_bias.shape[0]
        hid = up_bias.shape[0]
        hid_rows = hid // LANES
        piece = shape((own, share, width), BF16)
        sub = width // n_dp
        factor = HD**-0.5

        def mp_swap(v, bit):
            return swap(v, "mp", bit, n_mp)

        def dp_swap(v, bit):
            return swap(v, "dp", bit, n_dp)

        def gather_mp(v, first):
            halves = {0: [first]}
            for k in range(2, n_mp, 2):
                over_y = mp_swap(first, k)
                halves[k] = [over_y, dp_swap(over_y, 1)]
            blocks = {0: [v], 1: [mp_swap(v, 1)]}
            for k in range(2, n_mp, 2):
                blocks[k] = halves[k]
                blocks[k + 1] = [mp_swap(h, 1) for h in halves[k]]
            return [blocks[k] for k in range(n_mp)]

        def cut_tokens(ins, outs, _):
            me = lax.axis_index("mp")
            for k in range(n_mp):
                outs[k][...] = ins[0][pl.ds((me ^ k) * own, own)]

        token_parts = run("cut_tokens", cut_tokens, [tokens], [piece] * n_mp)
        token_parts = [
            v if k == 0 else mp_swap(v, k) for k, v in enumerate(token_parts)
        ]

        def first_halves(ins, outs, _):
            x_bit = lax.axis_index("dp") & 1
            for src, dst in zip(ins, outs):
                dst[...] = src[rows_of(x_bit, dst.shape[0])]

        flat_qkv = w_qkv.reshape(-1, lane)
        flats = [flat_qkv, w_out, w_up, w_down]
        firsts = run(
            "first_halves",
            first_halves,
            flats,
            [shape((v.shape[0] // 2, v.shape[1]), BF16) for v in flats],
        )
        small = jnp.concatenate(
            [
                jnp.pad(qv_bias, ((0, 0), (0, LANES - lane))),
                up_bias.reshape(hid_rows, LANES),
                jnp.pad(order_bias, (0, LANES - per))[None],
                jnp.zeros((VEC - 3 - hid_rows % VEC, LANES), F32),
            ]
        )
        smalls = [small] + [mp_swap(small, k) for k in range(1, n_mp)]
        cot_parts = run("cut_cotangent", cut_tokens, [cotangent], [piece] * n_mp)
        b_qkv = gather_mp(flat_qkv, firsts[0])
        b_out = gather_mp(w_out, firsts[1])
        cot_parts = [v if k == 0 else mp_swap(v, k) for k, v in enumerate(cot_parts)]
        b_up = gather_mp(w_up, firsts[2])
        b_down = gather_mp(w_down, firsts[3])

        def flat(blocks, group):
            return [p for k in group for p in blocks[k]], [len(blocks[k]) for k in group]

        def place_group(dst, pieces, counts, size, x_bit):
            for j, ps in enumerate(take(pieces, counts)):
                place(dst, slice(j * size, (j + 1) * size), ps, x_bit)

        def order_row(om_ref, me, r):
            v = om_ref[pl.ds(me * own + r, 1), :].astype(F32)
            v = jnp.broadcast_to(v, (8, slots))
            at = lax.broadcasted_iota(jnp.int32, (8, slots), 1)
            step = share
            while step < slots:
                turned = jnp.where(
                    (at & step) == 0, pltpu.roll(v, slots - step, 1), pltpu.roll(v, step, 1)
                )
                v = jnp.where((me * share) & step, turned, v)
                step *= 2
            return v[:1]

        def keep_row(me, length):
            at = lax.broadcasted_iota(jnp.int32, (1, slots), 1)
            return (at ^ (me * share)) < length

        def keep_column(me, length):
            at = lax.broadcasted_iota(jnp.int32, (slots, 1), 0)
            return ((at ^ (me * share)) < length).astype(F32)

        def head_mask(pair_value, h):
            at = lax.broadcasted_iota(jnp.int32, pair_value.shape, 1)
            return jnp.where((at >= HD) == (h % 2 == 1), pair_value, jnp.zeros_like(pair_value))

        def assemble(dst, parts):
            for r in range(own):
                for k in range(n_mp):
                    dst[r * slots + k * share : r * slots + (k + 1) * share] = parts[k][r]

        def attend(group, first):
            wide = lane * len(group)
            heads = wide // HD
            pieces, counts = flat(b_qkv, group)

            def fn(ins, outs, scratch):
                me, x_bit = lax.axis_index("mp"), lax.axis_index("dp") & 1
                weights = scratch[0]
                if first:
                    head, tail = ins[: n_mp + 4], ins[n_mp + 4 :]
                    lens, om, gains, shifts = head[n_mp:]
                    x_ref, a1_ref, qkv_ref, p_ref, att_ref = outs
                    assemble(x_ref, head[:n_mp])
                    normed, _ = normalize(x_ref[...].astype(F32))
                    a1_ref[...] = (normed * gains[0:1] + shifts[0:1]).astype(BF16)
                else:
                    lens, om, a1_ref = ins[:3]
                    tail = ins[3:]
                    qkv_ref, p_ref, att_ref = outs
                place_group(weights, tail[: len(pieces)], counts, lane, x_bit)
                biases = tail[len(pieces) :]
                a1 = a1_ref[...]
                for t in range(3):
                    y = dot(a1, weights[t * width : (t + 1) * width])
                    if t != 1:
                        y = y + jnp.concatenate(
                            [b[t // 2 : t // 2 + 1, :lane] for b in biases], 1
                        )
                    qkv_ref[t] = y.astype(BF16)
                for r in range(own):
                    length = lens[me * own + r]
                    order = order_row(om, me, r)
                    kept = keep_row(me, length)
                    column = keep_column(me, length)
                    here = slice(r * slots, (r + 1) * slots)
                    for pair in range(heads // 2):
                        cols = slice(pair * PAIR, (pair + 1) * PAIR)
                        q = qkv_ref[0, here, cols] * jnp.asarray(factor, BF16)
                        key = qkv_ref[1, here, cols]
                        val = qkv_ref[2, here, cols]
                        acc = None
                        for h in (2 * pair, 2 * pair + 1):
                            b = biases[h // per]
                            ob = b[2 + hid_rows : 3 + hid_rows, h % per : h % per + 1]
                            row = jnp.where(kept, ob * order, -1e30)
                            s = dot_nt(head_mask(q, h), key) + row
                            e = jnp.exp(s - jnp.max(s, -1, keepdims=True))
                            p = (e * (1.0 / jnp.sum(e, -1, keepdims=True))).astype(BF16)
                            p_ref[r * heads + h] = p
                            term = dot(p, head_mask(val, h))
                            acc = term if acc is None else acc + term
                        att_ref[here, cols] = (acc * column).astype(BF16)

            ins = (
                token_parts + [lengths, order_mask, norm_scale_pair, norm_offset_pair]
                if first
                else [lengths, order_mask, a1]
            )
            lead = [shape((count, width), BF16)] * 2 if first else []
            return run(
                "attend",
                fn,
                ins + pieces + [smalls[k] for k in group],
                lead
                + [
                    shape((3, count, wide), BF16),
                    shape((own * heads, slots, slots), BF16),
                    shape((count, wide), BF16),
                ],
                [pltpu.VMEM((3 * width, wide), BF16)],
                flops=2 * count * width * 3 * wide + 4 * count * slots * wide * 4,
                smem=(n_mp if first else 0,),
            )

        x, a1, qkv0, p0, att0 = attend(groups[0], True)
        qkv1, p1, att1 = attend(groups[1], False)

        def scatter(dst, src, block, dpi):
            for xi in range(2):
                for zi in range(n_z):
                    here = rows_of(dpi ^ (xi + 2 * zi), sub)
                    dst[block, xi, zi] = src[here, :]

        def mlp_block(k, j, a2, a2t, dy, dyt, wu, wd, bias, mixed, d_mid, gs, outs, dpi):
            up = jnp.concatenate([bias[2 + i : 3 + i, :] for i in range(hid_rows)], 1)
            pre = dot(a2[...], wu[...]) + up
            square = pre * pre
            t = jnp.tanh(pre * (GELU_C + (GELU_C * GELU_A) * square))
            half = 0.5 + 0.5 * t
            hidden = (pre * half).astype(BF16)
            slope = half + (pre * (1.0 - t * t)) * (
                0.5 * GELU_C + (1.5 * GELU_C * GELU_A) * square
            )
            d_hidden = dot_nt(dy[...], wd[...])
            d_pre = (slope * d_hidden).astype(BF16)
            mixed[...] += dot(hidden, wd[...])
            d_mid[...] += dot_nt(d_pre, wu[...])
            down_ref, up_ref = outs[k % 2], outs[2 + k % 2]
            g_down, g_up = gs.at[2 * j], gs.at[2 * j + 1]
            g_down[...] = dot(dyt[...], hidden).astype(BF16)
            scatter(down_ref, g_down, j // 2, dpi)
            g_up[...] = dot(a2t[...], d_pre).astype(BF16)
            scatter(up_ref, g_up, j // 2, dpi)
            outs[4][j] = jnp.sum(d_pre.astype(F32), 0, keepdims=True)

        def grad_shapes(n_blocks, m, c):
            half = n_blocks // 2
            return [shape((half, 2, n_z, m, c), BF16)] * 2

        full = shape((count, width), F32)
        full_bf = shape((count, width), BF16)
        turned = shape((width, count), BF16)
        g0, g1 = groups
        out_pieces, out_counts = flat(b_out, range(n_mp))

        def mlp_outs(n_blocks):
            return (
                grad_shapes(n_blocks, sub, hid)
                + grad_shapes(n_blocks, sub, hid)
                + [shape((n_blocks, 1, hid), F32)]
            )

        up0, up0_counts = flat(b_up, g0)
        down0, down0_counts = flat(b_down, g0)

        def mlp_first(ins, outs, scratch):
            x_bit, dpi = lax.axis_index("dp") & 1, lax.axis_index("dp")
            sizes = [6, len(out_pieces), n_mp, len(up0), len(down0), len(g0)]
            lead, wo_p, dy_p, wu_p, wd_p, biases = take(ins, sizes)
            x_ref, att0_ref, att1_ref, gains, shifts, ob = lead
            x1, a2, a2t, dy, dyt, mixed, d_mid = outs[:7]
            wo, gs = scratch
            for j, ps in enumerate(take(wo_p, out_counts)):
                place_rows(wo, j * lane, lane, ps, x_bit)
            cut = lane * len(g0)
            v = x_ref[...].astype(F32) + (
                dot(att0_ref[...], wo[:cut]) + dot(att1_ref[...], wo[cut:]) + ob[0:1]
            )
            x1[...] = v
            normed, _ = normalize(v)
            act = (normed * gains[1:2] + shifts[1:2]).astype(BF16)
            a2[...] = act
            a2t[...] = act.T
            assemble(dy, dy_p)
            dyt[...] = dy[...].T
            mixed[...] = jnp.zeros_like(mixed)
            d_mid[...] = jnp.zeros_like(d_mid)
            for j, k in enumerate(g0):
                mlp_block(
                    k, j, a2, a2t, dy, dyt, wu_p[j], wd_p[j], biases[j], mixed, d_mid, gs, outs[7:], dpi
                )

        block_flops = 12 * count * width * hid
        x1, a2, a2t, dy, dyt, mixed, d_mid, kd0, sd0, ku0, su0, gub0 = run(
            "mlp_first",
            mlp_first,
            [x, att0, att1, norm_scale_pair, norm_offset_pair, out_bias]
            + out_pieces
            + cot_parts
            + up0
            + down0
            + [smalls[k] for k in g0],
            [full, full_bf, turned, full_bf, turned, full, full] + mlp_outs(len(g0)),
            [pltpu.VMEM((width, width), BF16), pltpu.VMEM((2 * len(g0), width, hid), BF16)],
            flops=block_flops * len(g0) + 2 * count * width * width,
        )

        up1, up1_counts = flat(b_up, g1)
        down1, down1_counts = flat(b_down, g1)

        def mlp_second(ins, outs, scratch):
            x_bit, dpi = lax.axis_index("dp") & 1, lax.axis_index("dp")
            lead, wu_p, wd_p, biases = take(ins, [9, len(up1), len(down1), len(g1)])
            x1, a2, a2t, dy, dyt, mixed_in, d_mid_in, gains, ob = lead
            out_parts, (dx1, d_att, vec) = outs[:n_mp], outs[n_mp : n_mp + 3]
            mixed, d_mid, wus, wds, gs = scratch
            mixed[...] = mixed_in[...]
            d_mid[...] = d_mid_in[...]
            wu_p, wd_p = take(wu_p, up1_counts), take(wd_p, down1_counts)
            for j, k in enumerate(g1):
                wu, wd = wus.at[j], wds.at[j]
                place(wu, slice(0, hid), wu_p[j], x_bit)
                place(wd, slice(0, width), wd_p[j], x_bit)
                mlp_block(
                    k, j, a2, a2t, dy, dyt, wu, wd, biases[j], mixed, d_mid, gs, outs[n_mp + 3 :], dpi
                )
            v = x1[...]
            final = (v + (mixed[...] + ob[1:2])).astype(BF16)
            for r in range(own):
                for k in range(n_mp):
                    at = r * slots + k * share
                    out_parts[k][r] = final[at : at + share]
            normed, rstd = normalize(v)
            g = d_mid[...]
            dyf = dy[...].astype(F32)
            d = dyf + norm_back(g, normed, rstd, gains[1:2])
            dx1[...] = d
            low = d.astype(BF16)
            d_att[...] = low
            vec[0:1] = jnp.sum(g * normed, 0, keepdims=True)
            vec[1:2] = jnp.sum(g, 0, keepdims=True)
            vec[2:3] = jnp.sum(low.astype(F32), 0, keepdims=True)
            vec[3:4] = jnp.sum(dyf, 0, keepdims=True)

        second = run(
            "mlp_second",
            mlp_second,
            [x1, a2, a2t, dy, dyt, mixed, d_mid, norm_scale_pair, out_bias]
            + up1
            + down1
            + [smalls[k] for k in g1],
            [piece] * n_mp + [full, full_bf, shape((4, width), F32)] + mlp_outs(len(g1)),
            [
                pltpu.VMEM((count, width), F32),
                pltpu.VMEM((count, width), F32),
                pltpu.VMEM((len(g1), width, hid), BF16),
                pltpu.VMEM((len(g1), hid, width), BF16),
                pltpu.VMEM((2 * len(g1), width, hid), BF16),
            ],
            flops=block_flops * len(g1),
        )
        out_parts, (dx1, d_att, vec, kd1, sd1, ku1, su1, gub1) = second[:n_mp], second[n_mp:]

        vec_rows = n_dp * VEC
        qkv_pieces, qkv_counts = flat(b_qkv, range(n_mp))
        chunk = 4 * sub + 2 * VEC

        def attend_back(ins, outs, scratch):
            me, dpi = lax.axis_index("mp"), lax.axis_index("dp")
            x_bit = dpi & 1
            sizes = [3, 4, 2, 2, 2, 3, len(qkv_pieces), len(out_pieces)]
            (lens, om, gains), (x_ref, a1_ref, dx1, d_att), qkvs, ps, atts, (vec, gub_a, gub_b), wq_p, wo_p = take(ins, sizes)
            parts = outs[:n_mp]
            grads = outs[n_mp:]
            wqs, wos, dqkvs, gqs = scratch[:2], scratch[2:4], scratch[4:6], scratch[6:8]
            d_in, vec_f, shared = scratch[8:]
            wq_p, wo_p = take(wq_p, qkv_counts), take(wo_p, out_counts)
            a1t = a1_ref[...].T
            d_att_v = d_att[...]
            d_att_t = d_att_v.T
            d_in[...] = jnp.zeros_like(d_in)
            order_sums = {}
            for gi, group in enumerate(groups):
                wide = lane * len(group)
                heads = wide // HD
                qkv_ref, p_ref, att_ref = qkvs[gi], ps[gi], atts[gi]
                wq, wo, dqkv, gq = wqs[gi], wos[gi], dqkvs[gi], gqs[gi]
                for j, k in enumerate(group):
                    place(wq, slice(j * lane, (j + 1) * lane), wq_p[k], x_bit)
                    place_rows(wo, j * lane, lane, wo_p[k], x_bit)
                d_o = dot_nt(d_att_v, wo[:wide]).astype(BF16)
                for r in range(own):
                    length = lens[me * own + r]
                    order = order_row(om, me, r)
                    kept = keep_row(me, length)
                    column = keep_column(me, length).astype(BF16)
                    here = slice(r * slots, (r + 1) * slots)
                    for pair in range(heads // 2):
                        cols = slice(pair * PAIR, (pair + 1) * PAIR)
                        q = qkv_ref[0, here, cols] * jnp.asarray(factor, BF16)
                        key = qkv_ref[1, here, cols] * jnp.asarray(factor, BF16)
                        val = qkv_ref[2, here, cols]
                        do = d_o[here, cols] * column
                        dq = dk = dv = 0.0
                        for h in (2 * pair, 2 * pair + 1):
                            p_low = p_ref[r * heads + h]
                            p = p_low.astype(F32)
                            do_h = head_mask(do, h)
                            d_p = dot_nt(do_h, val)
                            inner = jnp.sum(p * d_p, -1, keepdims=True)
                            d_s = jnp.where(kept, p * (d_p - inner), 0.0).astype(BF16)
                            sums = dot(jnp.ones((8, slots), BF16), d_s)[:1] * order
                            name = (group[h // per], h % per)
                            old = order_sums.get(name)
                            order_sums[name] = sums if old is None else old + sums
                            dq = dq + dot(d_s, head_mask(key, h))
                            dk = dk + dot_tn(d_s, head_mask(q, h))
                            dv = dv + dot_tn(p_low, do_h)
                        dqkv[0, here, cols] = dq.astype(BF16)
                        dqkv[1, here, cols] = dk.astype(BF16)
                        dqkv[2, here, cols] = dv.astype(BF16)
                total = None
                for t in range(3):
                    g = dqkv[t, :, :wide]
                    gq[t, :, :wide] = dot(a1t, g).astype(BF16)
                    term = dot_nt(g, wq[t * width : (t + 1) * width, :wide])
                    total = term if total is None else total + term
                d_in[...] += total
                gq[3, :, :wide] = dot(d_att_t, att_ref[...]).astype(BF16)
                for j, k in enumerate(group):
                    dst = grads[2 * gi + k % 2]
                    cols = slice(j * lane, (j + 1) * lane)
                    for xi in range(2):
                        for zi in range(n_z):
                            at = rows_of(dpi ^ (xi + 2 * zi), sub)
                            for t in range(4):
                                dst[j // 2, xi, zi, t * sub : (t + 1) * sub] = gq[t, at, cols]
                    rows_q = jnp.sum(dqkv[0, :, cols].astype(F32), 0, keepdims=True)
                    rows_v = jnp.sum(dqkv[2, :, cols].astype(F32), 0, keepdims=True)
                    vec_f[k] = jnp.zeros((vec_rows, lane), F32)
                    at = 6 * width // lane
                    vec_f[k, at : at + 1] = rows_q
                    vec_f[k, at + 1 : at + 2] = rows_v
                    gub = (gub_a, gub_b)[gi][j]
                    for i in range(hid // lane):
                        vec_f[k, at + 2 + i : at + 3 + i] = gub[:, i * lane : (i + 1) * lane]
                    lanes = lax.broadcasted_iota(jnp.int32, (1, lane), 1)
                    row = jnp.zeros((1, lane), F32)
                    for i in range(per):
                        row = row + jnp.where(
                            lanes == i, jnp.sum(order_sums[(k, i)], -1, keepdims=True), 0.0
                        )
                    vec_f[k, at + 2 + hid // lane : at + 3 + hid // lane] = row
            normed, rstd = normalize(x_ref[...].astype(F32))
            g = d_in[...]
            final = (dx1[...] + norm_back(g, normed, rstd, gains[0:1])).astype(BF16)
            for r in range(own):
                for k in range(n_mp):
                    at = r * slots + k * share
                    parts[k][r] = final[at : at + share]
            shared[0:1] = jnp.sum(g * normed, 0, keepdims=True)
            shared[1:2] = vec[0:1]
            shared[2:3] = jnp.sum(g, 0, keepdims=True)
            shared[3:4] = vec[1:2]
            shared[4:5] = vec[2:3]
            shared[5:6] = vec[3:4]
            per_row = width // lane
            for gi, group in enumerate(groups):
                for j, k in enumerate(group):
                    for i in range(6):
                        for c in range(per_row):
                            at = i * per_row + c
                            vec_f[k, at : at + 1] = shared[i : i + 1, c * lane : (c + 1) * lane]
                    dst = grads[2 * gi + k % 2]
                    for xi in range(2):
                        for zi in range(n_z):
                            v = vec_f[k, rows_of(dpi ^ (xi + 2 * zi), VEC)]
                            dst[j // 2, xi, zi, 4 * sub :] = two_parts(v)

        def two_parts(v):
            high = v.astype(BF16)
            low = (v - high.astype(F32)).astype(BF16)
            return jnp.concatenate([high.astype(F32), low.astype(F32)], 0).astype(BF16)

        back = run(
            "attend_back",
            attend_back,
            [lengths, order_mask, norm_scale_pair]
            + [x, a1, dx1, d_att]
            + [qkv0, qkv1, p0, p1, att0, att1]
            + [vec, gub0, gub1]
            + qkv_pieces
            + out_pieces,
            [piece] * n_mp + grad_shapes(len(g0), chunk, lane) + grad_shapes(len(g1), chunk, lane),
            [
                *[pltpu.VMEM((3 * width, lane * len(g)), BF16) for g in groups],
                *[pltpu.VMEM((lane * len(g), width), BF16) for g in groups],
                *[pltpu.VMEM((3, count, lane * len(g)), BF16) for g in groups],
                *[pltpu.VMEM((4, width, lane * len(g)), BF16) for g in groups],
                pltpu.VMEM((count, width), F32),
                pltpu.VMEM((n_mp, vec_rows, lane), F32),
                pltpu.VMEM((8, width), F32),
            ],
            flops=2 * count * width * width * 8 + 24 * count * slots * width,
            smem=(0,),
        )
        grad_parts, (ka0, sa0, ka1, sa1) = back[:n_mp], back[n_mp:]

        def add_all(values, vectors):
            total = values[0].astype(F32)
            for v in values[1:]:
                total = total + v.astype(F32)
            if not vectors:
                return total.astype(BF16)
            m = total.shape[-2]
            head = total[..., : m - 2 * VEC, :]
            v = total[..., m - 2 * VEC : m - VEC, :] + total[..., m - VEC :, :]
            high = v.astype(BF16).astype(F32)
            return jnp.concatenate([head, high, v - high], -2).astype(BF16)

        def reduce(keep0, send0, keep1, send1, vectors):
            m, c = keep0.shape[-2:]

            def split_x(ins, outs, _):
                for n in range(ins[0].shape[0]):
                    for xi in range(2):
                        for zi in range(n_z):
                            outs[xi][n, zi] = add_all(
                                [ins[0][n, xi, zi], ins[1][n, xi, zi]], vectors
                            )

            def core_step(keep, send):
                got = mp_swap(send, 1)
                part = shape((keep.shape[0], n_z, m, c), BF16)
                kept, sent = run("add_core", split_x, [keep, got], [part, part])
                return kept, dp_swap(sent, 1)

            kept1, got1 = core_step(keep1, send1)

            def for_y(ins, outs, _):
                for n, o in enumerate(outs):
                    for zi in range(n_z):
                        o[zi] = add_all([ins[0][n, zi], ins[1][n, zi]], vectors)

            n_y = keep1.shape[0]
            over_y = run("add_x", for_y, [kept1, got1], [shape((n_z, m, c), BF16)] * n_y)
            over_y = [mp_swap(v, 2 * (n + 1)) for n, v in enumerate(over_y)]
            kept0, got0 = core_step(keep0, send0)

            def for_z(ins, outs, _):
                for zi, o in enumerate(outs):
                    o[...] = add_all(
                        [ins[0][0, zi], ins[1][0, zi]] + [v[zi] for v in ins[2:]], vectors
                    )

            over_z = run("add_y", for_z, [kept0, got0] + over_y, [shape((m, c), BF16)] * n_z)
            got = [dp_swap(v, 2 * zi) for zi, v in enumerate(over_z) if zi]

            def last(ins, outs, _):
                outs[0][...] = add_all([v[...] for v in ins], vectors)

            (done,) = run("add_z", last, [over_z[0]] + got, [shape((m, c), BF16)])
            same_x = [done] + [dp_swap(done, 2 * zi) for zi in range(1, n_z)]
            other_x = [dp_swap(v, 1) for v in same_x]
            return same_x + other_x

        def places(dpi):
            return [dpi ^ (xi + 2 * zi) for xi in range(2) for zi in range(n_z)]

        def turn(ins, outs, scratch):
            for at, v in zip(places(lax.axis_index("dp")), ins):
                scratch[0][rows_of(at, sub)] = v[...].astype(F32)
            outs[0][...] = scratch[0][...].T

        def straight(ins, outs, _):
            for at, v in zip(places(lax.axis_index("dp")), ins):
                outs[0][rows_of(at, sub)] = v[...].astype(F32)

        def unpack(ins, outs, scratch):
            r_qkv, r_out, small_out, shared = outs
            turned_out, vec_f = scratch
            for at, v in zip(places(lax.axis_index("dp")), ins):
                here = rows_of(at, sub)
                for t in range(3):
                    r_qkv[t, here] = v[t * sub : (t + 1) * sub].astype(F32)
                turned_out[here] = v[3 * sub : 4 * sub].astype(F32)
                pairs = v[4 * sub :].astype(F32)
                vec_f[rows_of(at, VEC)] = pairs[:VEC] + pairs[VEC:]
            r_out[...] = turned_out[...].T
            per_row = width // lane
            for i in range(6):
                shared[i : i + 1] = jnp.concatenate(
                    [vec_f[i * per_row + c : i * per_row + c + 1] for c in range(per_row)], 1
                )
            at = 6 * per_row
            small_out[...] = vec_f[at : at + small_out.shape[0]]

        (r_down,) = run(
            "finish_down",
            turn,
            reduce(kd0, sd0, kd1, sd1, False),
            [shape((hid, width), F32)],
            [pltpu.VMEM((width, hid), F32)],
        )
        (r_up,) = run(
            "finish_up", straight, reduce(ku0, su0, ku1, su1, False), [shape((width, hid), F32)]
        )
        r_qkv, r_out, small_out, shared = run(
            "finish_attention",
            unpack,
            reduce(ka0, sa0, ka1, sa1, True),
            [
                shape((3, width, lane), F32),
                shape((lane, width), F32),
                shape((3 + hid // lane, lane), F32),
                shape((6, width), F32),
            ],
            [pltpu.VMEM((width, lane), F32), pltpu.VMEM((vec_rows, lane), F32)],
        )

        def gather_rows(ins, outs, _):
            me = lax.axis_index("mp")
            for k in range(n_mp):
                outs[0][pl.ds((me ^ k) * own, own)] = ins[k][...].astype(outs[0].dtype)

        def send_back(parts, kind):
            parts = [v if k == 0 else mp_swap(v, k) for k, v in enumerate(parts)]
            return run("gather_rows", gather_rows, parts, [shape((rows, share, width), kind)])[0]

        output = send_back(out_parts, BF16)
        token_gradient = send_back(grad_parts, F32)
        return (
            output,
            token_gradient,
            shared[0:2],
            shared[2:4],
            r_qkv,
            small_out[:2],
            small_out[2 + hid // lane, :per],
            r_out,
            shared[4:6],
            r_up,
            small_out[2 : 2 + hid // lane].reshape(-1),
            r_down,
        )

    return body


def solution(mesh):
    return jax.shard_map(
        make_body(mesh.shape["dp"], mesh.shape["mp"]),
        mesh=mesh,
        in_specs=(
            P("dp", "mp", None),
            P("dp"),
            P("dp", None),
            P(),
            P(),
            P(None, None, "mp"),
            P(None, "mp"),
            P("mp"),
            P("mp", None),
            P(),
            P(None, "mp"),
            P("mp"),
            P("mp", None),
            P("dp", "mp", None),
        ),
        out_specs=(
            P("dp", "mp", None),
            P("dp", "mp", None),
            P(),
            P(),
            P(None, None, "mp"),
            P(None, "mp"),
            P("mp"),
            P("mp", None),
            P(),
            P(None, "mp"),
            P("mp"),
            P("mp", None),
        ),
        check_vma=False,
    )
```

```python
import jax
import jax.numpy as jnp
from jax import lax
from jax.experimental import pallas as pl
from jax.experimental.pallas import tpu as pltpu
from jax.sharding import PartitionSpec as P

HD = 64
PAIR = 2 * HD
LANES = 128
F32 = jnp.float32
BF16 = jnp.bfloat16
VMEM_LIMIT = 28 * 2**20
GELU_C = 0.7978845608028654
GELU_A = 0.044715
VEC = 8


def swap(v, axis, bit, size):
    return lax.ppermute(v, axis, [(i, i ^ bit) for i in range(size)])


def bits_of(size):
    return [1 << b for b in range(size.bit_length() - 1)]


def shape(dims, kind):
    return jax.ShapeDtypeStruct(tuple(dims), kind)


def together(*lists):
    out = lax.optimization_barrier(tuple(tuple(v) for v in lists))
    return [list(v) for v in out]


def run(name, fn, ins, outs, scratch=(), smem=(), after=(), hbm=()):
    n_in, n_out, n_all = len(ins), len(outs), len(ins) + len(after)

    def kernel(*refs):
        fn(refs[:n_in], refs[n_all : n_all + n_out], refs[n_all + n_out :])

    return pl.pallas_call(
        kernel,
        out_shape=tuple(outs),
        in_specs=[
            pl.BlockSpec(
                memory_space=pltpu.SMEM if i in smem else pl.ANY if i in hbm else pltpu.VMEM
            )
            for i in range(n_in)
        ]
        + [pl.BlockSpec(memory_space=pl.ANY) for _ in after],
        out_specs=tuple(pl.BlockSpec(memory_space=pltpu.VMEM) for _ in outs),
        scratch_shapes=list(scratch),
        compiler_params=pltpu.CompilerParams(vmem_limit_bytes=VMEM_LIMIT),
        cost_estimate=pl.CostEstimate(flops=1, bytes_accessed=1, transcendentals=0),
        name=name,
    )(*ins, *after)


def dot(a, b):
    return jnp.dot(a, b, preferred_element_type=F32)


def dot_nt(a, b):
    return lax.dot_general(a, b, (((1,), (1,)), ((), ())), preferred_element_type=F32)


def dot_tn(a, b):
    return lax.dot_general(a, b, (((0,), (0,)), ((), ())), preferred_element_type=F32)


def normalize(v):
    centre = v - jnp.mean(v, -1, keepdims=True)
    rstd = lax.rsqrt(jnp.mean(centre * centre, -1, keepdims=True) + 1e-05)
    return centre * rstd, rstd


def norm_back(g, normed, rstd, gain):
    e = g * gain
    return rstd * (
        e - jnp.mean(e, -1, keepdims=True) - normed * jnp.mean(e * normed, -1, keepdims=True)
    )


def rows_of(start, size):
    return pl.ds(pl.multiple_of(start * size, size), size)


def whole(pieces, x_bit):
    if len(pieces) == 1:
        return pieces[0][...]
    a, b = pieces[0][...], pieces[1][...]
    first = x_bit == 0
    return jnp.concatenate([jnp.where(first, a, b), jnp.where(first, b, a)], 0)


def take(refs, counts):
    out, at = [], 0
    for c in counts:
        out.append(refs[at : at + c])
        at += c
    assert at == len(refs)
    return out


def three_parts(v):
    high = v.astype(BF16).astype(F32)
    rest = v - high
    middle = rest.astype(BF16).astype(F32)
    return jnp.concatenate([high, middle, rest - middle, jnp.zeros_like(v)], 0).astype(BF16)


def two_parts(v):
    high = v.astype(BF16).astype(F32)
    return jnp.concatenate([high, v - high], 0).astype(BF16)


def make_body(n_dp, n_mp):
    groups = [[0, 1], list(range(2, n_mp))]
    y_peers = list(range(2, n_mp, 2))
    def body(
        tokens,
        lengths,
        order_mask,
        norm_scale_pair,
        norm_offset_pair,
        w_qkv,
        qv_bias,
        order_bias,
        w_out,
        out_bias,
        w_up,
        up_bias,
        w_down,
        cotangent,
    ):
        rows, share, width = tokens.shape
        slots = order_mask.shape[1]
        own = rows // n_mp
        count = own * slots
        lane = qv_bias.shape[1]
        per = order_bias.shape[0]
        hid = up_bias.shape[0]
        hid_rows = hid // lane
        cols = width // lane
        piece = shape((own, share, width), BF16)
        sub = width // n_dp
        factor = HD**-0.5
        o_at, s_at = 3 * width, 4 * width
        bundle_rows = 4 * width + 4 * VEC

        def mp_swap(v, bit):
            return swap(v, "mp", bit, n_mp)

        def dp_swap(v, bit):
            return swap(v, "dp", bit, n_dp)

        def spread(parts):
            return [mp_swap(v, k + 1) for k, v in enumerate(parts)]

        def over_y(v):
            return [mp_swap(v, k) for k in y_peers]

        def spread_y(parts):
            return [mp_swap(v, k) for k, v in zip(y_peers, parts)]

        def cut_rows(ins, outs, scratch):
            me = lax.axis_index("mp")
            copies = [
                pltpu.make_async_copy(
                    v.at[pl.ds((me ^ k) * own, own)],
                    outs[i * n_mp + k],
                    scratch[0].at[i, k],
                )
                for i, v in enumerate(ins)
                for k in range(n_mp)
            ]
            for c in copies:
                c.start()
            for c in copies:
                c.wait()

        rows_cut = run(
            "cut_rows",
            cut_rows,
            [tokens, cotangent],
            [piece] * (2 * n_mp),
            [pltpu.SemaphoreType.DMA((2, n_mp))],
            hbm=(0, 1),
        )
        token_parts, cot_parts = list(rows_cut[:n_mp]), list(rows_cut[n_mp:])

        def pack(ins, outs, scratch):
            x_bit = lax.axis_index("dp") & 1
            bundle, half = outs
            copy = pltpu.make_async_copy(ins[0], bundle.at[pl.ds(0, o_at)], scratch[0])
            copy.start()
            for c in range(cols):
                bundle[o_at + c * lane : o_at + (c + 1) * lane] = ins[1][
                    :, c * lane : (c + 1) * lane
                ]
            small = jnp.concatenate(
                [
                    ins[2][...],
                    ins[3][...],
                    jnp.concatenate([ins[4][...], jnp.zeros((1, lane - per), F32)], 1),
                    jnp.zeros((VEC - 3 - hid_rows, lane), F32),
                ],
                0,
            )
            bundle[s_at:] = three_parts(small)
            copy.wait()
            half[...] = bundle[rows_of(x_bit, bundle_rows // 2)]

        bundle, bundle_half = run(
            "pack",
            pack,
            [
                w_qkv.reshape(-1, lane),
                w_out,
                qv_bias,
                up_bias.reshape(hid_rows, lane),
                order_bias.reshape(1, per),
            ],
            [shape((bundle_rows, lane), BF16), shape((bundle_rows // 2, lane), BF16)],
            [pltpu.SemaphoreType.DMA(())],
            hbm=(0,),
            after=[token_parts[0]],
        )
        def cut_halves(ins, outs, scratch):
            dpi = lax.axis_index("dp")
            copies = [
                pltpu.make_async_copy(
                    src.at[rows_of(bit, src.shape[0] // 2)],
                    outs[0].at[n] if joined else outs[n],
                    scratch[0].at[n],
                )
                for n, (src, bit) in enumerate(zip(ins, (dpi & 1, (dpi >> 1) & 1)))
            ]
            for c in copies:
                c.start()
            for c in copies:
                c.wait()

        joined = w_up.shape == w_down.shape
        half_shapes = [shape((v.shape[0] // 2, v.shape[1]), BF16) for v in (w_up, w_down)]
        half_parts = run(
            "cut_halves",
            cut_halves,
            [w_up, w_down],
            [shape((2,) + half_shapes[0].shape, BF16)] if joined else half_shapes,
            [pltpu.SemaphoreType.DMA((2,))],
            hbm=(0, 1),
            after=[bundle_half],
        )

        sends, (bundle, bundle_half) = together(token_parts[1:], [bundle, bundle_half])
        token_parts = token_parts[:1] + spread(sends)
        bundle_core, bundle_y = mp_swap(bundle, 1), over_y(bundle_half)

        bundle_y, halves, token_parts, near = together(
            bundle_y, half_parts, token_parts, [w_up, w_down]
        )
        bundle_x = [dp_swap(v, 1) for v in bundle_y]
        bundle_yc = [mp_swap(v, 1) for v in bundle_y]
        halves_y = [over_y(v) for v in halves]
        near_core = [mp_swap(v, 1) for v in near]

        def far(first, second, first_core, second_core):
            return [
                v
                for n in range(len(y_peers))
                for v in (first[n], second[n], first_core[n], second_core[n])
            ]

        def order_row(om_ref, me, r):
            v = om_ref[pl.ds(me * own + r, 1), :].astype(F32)
            v = jnp.broadcast_to(v, (8, slots))
            at = lax.broadcasted_iota(jnp.int32, (8, slots), 1)
            step = share
            while step < slots:
                turned = jnp.where(
                    (at & step) == 0, pltpu.roll(v, slots - step, 1), pltpu.roll(v, step, 1)
                )
                v = jnp.where((me * share) & step, turned, v)
                step *= 2
            return v[:1]

        def keep_row(me, length):
            at = lax.broadcasted_iota(jnp.int32, (1, slots), 1)
            return (at ^ (me * share)) < length

        def keep_column(me, length):
            at = lax.broadcasted_iota(jnp.int32, (slots, 1), 0)
            return ((at ^ (me * share)) < length).astype(F32)

        def head_mask(pair_value, h):
            at = lax.broadcasted_iota(jnp.int32, pair_value.shape, 1)
            return jnp.where((at >= HD) == (h % 2 == 1), pair_value, jnp.zeros_like(pair_value))

        def assemble(dst, parts):
            for r in range(own):
                for k in range(n_mp):
                    dst[r * slots + k * share : r * slots + (k + 1) * share] = parts[k][r]

        def cut_slots(dst, lead, value):
            for r in range(own):
                for k in range(n_mp):
                    at = r * slots + k * share
                    dst[k][lead + r] = value[at : at + share]

        def attend(group, first, pieces):
            wide = lane * len(group)
            heads = wide // HD
            counts = [len(pieces) // len(group)] * len(group)

            def fn(ins, outs, scratch):
                me, x_bit = lax.axis_index("mp"), lax.axis_index("dp") & 1
                qkv_ref, p_ref, att_ref, weights, wo, smalls = outs[-6:]
                if first:
                    lens, om, gains, shifts = ins[n_mp : n_mp + 4]
                    x_ref, a1_ref = outs[:2]
                    assemble(x_ref, ins[:n_mp])
                    normed, _ = normalize(x_ref[...].astype(F32))
                    a1_ref[...] = (normed * gains[0:1] + shifts[0:1]).astype(BF16)
                else:
                    lens, om, a1_ref = ins[:3]
                for j, ps in enumerate(take(ins[-len(pieces) :], counts)):
                    v = whole(ps, x_bit)
                    weights[:, j * lane : (j + 1) * lane] = v[:o_at]
                    for c in range(cols):
                        wo[j * lane : (j + 1) * lane, c * lane : (c + 1) * lane] = v[
                            o_at + c * lane : o_at + (c + 1) * lane
                        ]
                    parts = v[s_at:].astype(F32)
                    smalls[j] = parts[:VEC] + parts[VEC : 2 * VEC] + parts[2 * VEC : 3 * VEC]
                a1 = a1_ref[...]
                for t in range(3):
                    y = dot(a1, weights[t * width : (t + 1) * width])
                    if t != 1:
                        i = t // 2
                        y = y + jnp.concatenate(
                            [smalls[j, i : i + 1] for j in range(len(group))], 1
                        )
                    qkv_ref[t] = y.astype(BF16)
                for r in range(own):
                    length = lens[me * own + r]
                    order = order_row(om, me, r)
                    kept = keep_row(me, length)
                    column = keep_column(me, length)
                    here = slice(r * slots, (r + 1) * slots)
                    for pair in range(heads // 2):
                        at = slice(pair * PAIR, (pair + 1) * PAIR)
                        q = qkv_ref[0, here, at] * jnp.asarray(factor, BF16)
                        key = qkv_ref[1, here, at]
                        val = qkv_ref[2, here, at]
                        acc = None
                        for h in (2 * pair, 2 * pair + 1):
                            o = 2 + hid_rows
                            ob = smalls[h // per, o : o + 1, h % per : h % per + 1]
                            row = jnp.where(kept, ob * order, -1e30)
                            s = dot_nt(head_mask(q, h), key) + row
                            e = jnp.exp(s - jnp.max(s, -1, keepdims=True))
                            p = (e * (1.0 / jnp.sum(e, -1, keepdims=True))).astype(BF16)
                            p_ref[r * heads + h] = p
                            term = dot(p, head_mask(val, h))
                            acc = term if acc is None else acc + term
                        att_ref[here, at] = (acc * column).astype(BF16)

            ins = (
                token_parts + [lengths, order_mask, norm_scale_pair, norm_offset_pair]
                if first
                else [lengths, order_mask, a1]
            )
            lead = [shape((count, width), BF16)] * 2 if first else []
            return run(
                "attend",
                fn,
                ins + pieces,
                lead
                + [
                    shape((3, count, wide), BF16),
                    shape((own * heads, slots, slots), BF16),
                    shape((count, wide), BF16),
                    shape((3 * width, wide), BF16),
                    shape((wide, width), BF16),
                    shape((len(group), VEC, lane), F32),
                ],
                smem=(n_mp if first else 0,),
            )

        x, a1, qkv0, p0, att0, wq0, wo0, small0 = attend(groups[0], True, [bundle, bundle_core])

        bundle_x, (att0,) = together(bundle_x, [att0])
        bundle_xc = [mp_swap(v, 1) for v in bundle_x]
        qkv1, p1, att1, wq1, wo1, small1 = attend(
            groups[1], False, far(bundle_y, bundle_x, bundle_yc, bundle_xc)
        )

        def take_apart(ins, outs, _):
            for n, o in enumerate(outs):
                o[...] = ins[0][n]

        if joined:
            pairs = [run("take_apart", take_apart, [v], half_shapes, after=[att1]) for v in halves_y[0]]
            halves_y = list(zip(*pairs))
        up_y, down_y, (att1,), sends = together(*halves_y, [att1], cot_parts[1:])
        up_x, down_z = [dp_swap(v, 1) for v in up_y], [dp_swap(v, 2) for v in down_y]
        up_yc, down_yc = ([mp_swap(v, 1) for v in vs] for vs in (up_y, down_y))
        cot_parts = cot_parts[:1] + spread(sends)

        up_x, down_z, cot_parts = together(up_x, down_z, cot_parts)
        up_xc, down_zc = ([mp_swap(v, 1) for v in vs] for vs in (up_x, down_z))

        def scatter(dst, src, block, which, dpi):
            for p in range(n_dp):
                dst[block, which, p] = src[rows_of(dpi ^ p, sub), :]

        def mlp_block(
            j, a2, a2t, dy, dyt, wu, wd, bias, mixed, d_mid, gs, dst, block, bias_sums, dpi
        ):
            up = jnp.concatenate([bias[2 + i : 3 + i] for i in range(hid_rows)], 1)
            pre = dot(a2[...], wu) + up
            square = pre * pre
            t = jnp.tanh(pre * (GELU_C + (GELU_C * GELU_A) * square))
            half = 0.5 + 0.5 * t
            hidden = (pre * half).astype(BF16)
            slope = half + (pre * (1.0 - t * t)) * (
                0.5 * GELU_C + (1.5 * GELU_C * GELU_A) * square
            )
            d_hidden = dot_nt(dy[...], wd)
            d_pre = (slope * d_hidden).astype(BF16)
            mixed[...] += dot(hidden, wd)
            d_mid[...] += dot_nt(d_pre, wu)
            g_down, g_up = gs.at[2 * j], gs.at[2 * j + 1]
            g_down[...] = dot(dyt[...], hidden).astype(BF16)
            scatter(dst, g_down, block, 0, dpi)
            g_up[...] = dot(a2t[...], d_pre).astype(BF16)
            scatter(dst, g_up, block, 1, dpi)
            bias_sums[j] = jnp.sum(d_pre.astype(F32), 0, keepdims=True)

        def mlp_outs(n_blocks, n_arrays):
            both = shape((n_blocks // n_arrays, 2, n_dp, sub, hid), BF16)
            return [both] * n_arrays + [shape((n_blocks, 1, hid), F32)]

        full = shape((count, width), F32)
        full_bf = shape((count, width), BF16)
        turned = shape((width, count), BF16)
        g0, g1 = groups

        def mlp_first(ins, outs, scratch):
            dpi = lax.axis_index("dp")
            lead, dy_p, wu_p, wd_p = take(ins, [9, n_mp, len(g0), len(g0)])
            x_ref, att0_ref, att1_ref, wo0_ref, wo1_ref, smalls, gains, shifts, ob = lead
            x1, a2, a2t, dy, dyt, mixed, d_mid = outs[:7]
            v = x_ref[...].astype(F32) + (
                dot(att0_ref[...], wo0_ref[...]) + dot(att1_ref[...], wo1_ref[...]) + ob[0:1]
            )
            x1[...] = v
            normed, _ = normalize(v)
            act = (normed * gains[1:2] + shifts[1:2]).astype(BF16)
            a2[...] = act
            a2t[...] = act.T
            assemble(dy, dy_p)
            dyt[...] = dy[...].T
            mixed[...] = jnp.zeros_like(mixed)
            d_mid[...] = jnp.zeros_like(d_mid)
            for j, k in enumerate(g0):
                mlp_block(
                    j,
                    a2,
                    a2t,
                    dy,
                    dyt,
                    wu_p[j][...],
                    wd_p[j][...],
                    smalls[j],
                    mixed,
                    d_mid,
                    scratch[0],
                    outs[7 + k % 2],
                    0,
                    outs[9],
                    dpi,
                )

        x1, a2, a2t, dy, dyt, mixed, d_mid, keep0, send0, gub0 = run(
            "mlp_first",
            mlp_first,
            [x, att0, att1, wo0, wo1, small0, norm_scale_pair, norm_offset_pair, out_bias]
            + cot_parts
            + [near[0], near_core[0], near[1], near_core[1]],
            [full, full_bf, turned, full_bf, turned, full, full] + mlp_outs(len(g0), 2),
            [pltpu.VMEM((2 * len(g0), width, hid), BF16)],
        )

        got0 = mp_swap(send0, 1)

        up1 = far(up_y, up_x, up_yc, up_xc)
        down1 = far(down_y, down_z, down_yc, down_zc)

        def mlp_far(j, last):
            ks = g1[j::2]
            n_w = 2 * len(ks)

            def fn(ins, outs, scratch):
                dpi = lax.axis_index("dp")
                lead, wu_p, wd_p = take(ins, [10, n_w, n_w])
                x1, a2, a2t, dy, dyt, mixed_in, d_mid_in, smalls, gains, ob = lead
                mixed, d_mid, gs = scratch if last else (*outs[:2], scratch[0])
                mixed[...] = mixed_in[...]
                d_mid[...] = d_mid_in[...]
                grads, bias_sums = outs[-2:]
                for n, k in enumerate(ks):
                    mlp_block(
                        n,
                        a2,
                        a2t,
                        dy,
                        dyt,
                        whole(wu_p[2 * n : 2 * n + 2], dpi & 1),
                        whole(wd_p[2 * n : 2 * n + 2], (dpi >> 1) & 1),
                        smalls[2 * n + j],
                        mixed,
                        d_mid,
                        gs,
                        grads,
                        n,
                        bias_sums,
                        dpi,
                    )
                if not last:
                    return
                output, dx1, d_att, vec = outs[:4]
                v = x1[...]
                output[...] = (v + (mixed[...] + ob[1:2])).astype(BF16)
                normed, rstd = normalize(v)
                g = d_mid[...]
                dyf = dy[...].astype(F32)
                d = dyf + norm_back(g, normed, rstd, gains[1:2])
                dx1[...] = d
                low = d.astype(BF16)
                d_att[...] = low
                vec[0:1] = jnp.sum(g * normed, 0, keepdims=True)
                vec[1:2] = jnp.sum(g, 0, keepdims=True)
                vec[2:3] = jnp.sum(low.astype(F32), 0, keepdims=True)
                vec[3:4] = jnp.sum(dyf, 0, keepdims=True)

            sums = [pltpu.VMEM((count, width), F32)] * 2
            return run(
                "mlp_far",
                fn,
                [x1, a2, a2t, dy, dyt, mixed, d_mid, small1, norm_scale_pair, out_bias]
                + [v for n in range(len(ks)) for v in up1[4 * n + 2 * j : 4 * n + 2 * j + 2]]
                + [v for n in range(len(ks)) for v in down1[4 * n + 2 * j : 4 * n + 2 * j + 2]],
                ([full_bf, full, full_bf, shape((4, width), F32)] if last else [full, full])
                + mlp_outs(len(ks), 1),
                (sums if last else []) + [pltpu.VMEM((2 * len(ks), width, hid), BF16)],
            )

        mixed, d_mid, send1, gub1_odd = mlp_far(1, False)
        send1, mixed = together([send1, mixed])[0]
        got1 = mp_swap(send1, 1)
        out_rows, dx1, d_att, vec, keep1, gub1_even = mlp_far(0, True)

        def add_all(values, vectors=False):
            total = values[0].astype(F32)
            for v in values[1:]:
                total = total + v.astype(F32)
            if not vectors:
                return total.astype(BF16)
            m = total.shape[-2]
            head = total[: m - 2 * VEC]
            v = total[m - 2 * VEC : m - VEC] + total[m - VEC :]
            high = v.astype(BF16).astype(F32)
            return jnp.concatenate([head, high, v - high], 0).astype(BF16)

        n_y = len(y_peers)

        def split(places, bit):
            return [i for i, p in enumerate(places) if not p & bit], [
                i for i, p in enumerate(places) if p & bit
            ]

        def add_split(parts, places, bit, vectors=False):
            picks = split(places, bit)

            def fn(ins, outs, _):
                for dst, pick in zip(outs, picks):
                    for at, i in enumerate(pick):
                        dst[at] = add_all([v[i] for v in ins], vectors)

            half = shape((len(picks[0]),) + parts[0].shape[1:], BF16)
            kept, sent = run("add_split", fn, parts, [half, half])
            return kept, sent, [places[i] for i in picks[0]]

        def add_whole(parts, vectors=False):
            def fn(ins, outs, _):
                for i in range(outs[0].shape[0]):
                    outs[0][i] = add_all([v[i] for v in ins], vectors)

            return run("add_whole", fn, parts, [shape(parts[0].shape, BF16)])[0]

        every = list(range(n_dp))
        no_x, with_x = split(every, 1)
        last_bits = [b for b in bits_of(n_dp) if b > 2]

        def add_core_mlp(ins, outs, _):
            keep0, got0, keep1, got1 = ins
            kept, sent, mine = outs[:3]
            for n in range(1 + n_y):
                a, b, i = (keep0, got0, 0) if n == 0 else (keep1, got1, n - 1)
                for dst, pick in ((kept, no_x), (sent, with_x)):
                    for at, p in enumerate(pick):
                        dst[n, at] = add_all([a[i, 0, p], b[i, 0, p]])
                up = mine if n == 0 else outs[3 + n - 1]
                for p in every:
                    up[p] = add_all([a[i, 1, p], b[i, 1, p]])

        kept_d, sent_d, mine_u, *others_u = run(
            "add_core_mlp",
            add_core_mlp,
            [keep0, got0, keep1, got1],
            [shape((1 + n_y, n_dp // 2, sub, hid), BF16)] * 2
            + [shape((n_dp, sub, hid), BF16)] * (1 + n_y),
        )
        (sent_d, d_att), others_u = together([sent_d, d_att], others_u)
        got_d = dp_swap(sent_d, 1)
        got_u = spread_y(others_u)

        vec_rows = n_dp * VEC
        chunk = 4 * sub + 2 * VEC

        def attend_back(ins, outs, scratch):
            me, dpi = lax.axis_index("mp"), lax.axis_index("dp")
            (lens, om, gains), fulls, qkvs, ps, atts, wqs, wos, vecs = take(
                ins, [3, 5, 2, 2, 2, 2, 2, 4]
            )
            x_ref, a1_ref, dx1, d_att, out_ref = fulls
            vec, gub_near, gub_even, gub_odd = vecs
            parts = outs[:n_mp]
            grads = outs[n_mp:]
            dqkvs, gqs = scratch[:2], scratch[2:4]
            d_in, vec_f, shared = scratch[4:]
            a1t = a1_ref[...].T
            d_att_v = d_att[...]
            d_att_t = d_att_v.T
            d_in[...] = jnp.zeros_like(d_in)
            cut_slots(parts, 0, out_ref[...])
            order_sums = {}
            for gi, group in enumerate(groups):
                wide = lane * len(group)
                heads = wide // HD
                qkv_ref, p_ref, att_ref = qkvs[gi], ps[gi], atts[gi]
                wq, wo, dqkv, gq = wqs[gi], wos[gi], dqkvs[gi], gqs[gi]
                d_o = dot_nt(d_att_v, wo[...]).astype(BF16)
                for r in range(own):
                    length = lens[me * own + r]
                    order = order_row(om, me, r)
                    kept = keep_row(me, length)
                    column = keep_column(me, length).astype(BF16)
                    here = slice(r * slots, (r + 1) * slots)
                    for pair in range(heads // 2):
                        at = slice(pair * PAIR, (pair + 1) * PAIR)
                        q = qkv_ref[0, here, at] * jnp.asarray(factor, BF16)
                        key = qkv_ref[1, here, at] * jnp.asarray(factor, BF16)
                        val = qkv_ref[2, here, at]
                        do = d_o[here, at] * column
                        dq = dk = dv = 0.0
                        for h in (2 * pair, 2 * pair + 1):
                            p_low = p_ref[r * heads + h]
                            p = p_low.astype(F32)
                            do_h = head_mask(do, h)
                            d_p = dot_nt(do_h, val)
                            inner = jnp.sum(p * d_p, -1, keepdims=True)
                            d_s = jnp.where(kept, p * (d_p - inner), 0.0).astype(BF16)
                            sums = dot(jnp.ones((8, slots), BF16), d_s)[:1] * order
                            name = (group[h // per], h % per)
                            old = order_sums.get(name)
                            order_sums[name] = sums if old is None else old + sums
                            dq = dq + dot(d_s, head_mask(key, h))
                            dk = dk + dot_tn(d_s, head_mask(q, h))
                            dv = dv + dot_tn(p_low, do_h)
                        dqkv[0, here, at] = dq.astype(BF16)
                        dqkv[1, here, at] = dk.astype(BF16)
                        dqkv[2, here, at] = dv.astype(BF16)
                total = None
                for t in range(3):
                    g = dqkv[t]
                    gq[t] = dot(a1t, g).astype(BF16)
                    term = dot_nt(g, wq[t * width : (t + 1) * width])
                    total = term if total is None else total + term
                d_in[...] += total
                gq[3] = dot(d_att_t, att_ref[...]).astype(BF16)
                for j, k in enumerate(group):
                    dst = grads[2 * gi + k % 2]
                    at = slice(j * lane, (j + 1) * lane)
                    for p in range(n_dp):
                        here = rows_of(dpi ^ p, sub)
                        for t in range(4):
                            dst[j // 2, p, t * sub : (t + 1) * sub] = gq[t, here, at]
                    vec_f[k] = jnp.zeros((vec_rows, lane), F32)
                    base = 6 * cols
                    for n, t in enumerate((0, 2)):
                        vec_f[k, base + n : base + n + 1] = jnp.sum(
                            dqkv[t, :, at].astype(F32), 0, keepdims=True
                        )
                    gub = gub_near[j] if gi == 0 else (gub_even, gub_odd)[j % 2][j // 2]
                    for i in range(hid_rows):
                        vec_f[k, base + 2 + i : base + 3 + i] = gub[:, i * lane : (i + 1) * lane]
                    lanes = lax.broadcasted_iota(jnp.int32, (1, lane), 1)
                    row = jnp.zeros((1, lane), F32)
                    for i in range(per):
                        row = row + jnp.where(
                            lanes == i, jnp.sum(order_sums[(k, i)], -1, keepdims=True), 0.0
                        )
                    vec_f[k, base + 2 + hid_rows : base + 3 + hid_rows] = row
            normed, rstd = normalize(x_ref[...].astype(F32))
            g = d_in[...]
            cut_slots(
                parts, own, (dx1[...] + norm_back(g, normed, rstd, gains[0:1])).astype(BF16)
            )
            shared[0:1] = jnp.sum(g * normed, 0, keepdims=True)
            shared[1:2] = vec[0:1]
            shared[2:3] = jnp.sum(g, 0, keepdims=True)
            shared[3:4] = vec[1:2]
            shared[4:5] = vec[2:3]
            shared[5:6] = vec[3:4]
            for gi, group in enumerate(groups):
                for j, k in enumerate(group):
                    for i in range(6):
                        for c in range(cols):
                            at = i * cols + c
                            vec_f[k, at : at + 1] = shared[i : i + 1, c * lane : (c + 1) * lane]
                    dst = grads[2 * gi + k % 2]
                    for p in range(n_dp):
                        v = vec_f[k, rows_of(dpi ^ p, VEC)]
                        dst[j // 2, p, 4 * sub :] = two_parts(v)

        def grad_shapes(n_blocks):
            return [shape((n_blocks // 2, n_dp, chunk, lane), BF16)] * 2

        back = run(
            "attend_back",
            attend_back,
            [lengths, order_mask, norm_scale_pair]
            + [x, a1, dx1, d_att, out_rows]
            + [qkv0, qkv1, p0, p1, att0, att1, wq0, wq1, wo0, wo1]
            + [vec, gub0, gub1_even, gub1_odd],
            [shape((2 * own, share, width), BF16)] * n_mp + grad_shapes(len(g0)) + grad_shapes(len(g1)),
            [
                *[pltpu.VMEM((3, count, lane * len(g)), BF16) for g in groups],
                *[pltpu.VMEM((4, width, lane * len(g)), BF16) for g in groups],
                pltpu.VMEM((count, width), F32),
                pltpu.VMEM((n_mp, vec_rows, lane), F32),
                pltpu.VMEM((8, width), F32),
            ],
            smem=(0,),
        )
        row_parts, (ka0, sa0, ka1, sa1) = back[:n_mp], back[n_mp:]

        def add_x(ins, outs, _):
            for n in range(1 + n_y):
                for i in range(n_dp // 2):
                    outs[n][i] = add_all([ins[0][n, i], ins[1][n, i]])

        mine_d, *others_d = run(
            "add_x", add_x, [kept_d, got_d], [shape((n_dp // 2, sub, hid), BF16)] * (1 + n_y)
        )
        kept_u, sent_u, at_u = add_split([mine_u] + got_u, every, 2)
        others_d, (sent_u,), sends = together(others_d, [sent_u], [sa0, sa1])
        got_d = spread_y(others_d)
        got_u = dp_swap(sent_u, 2)
        ga0, ga1 = (mp_swap(v, 1) for v in sends)

        def add_core_att(ins, outs, _):
            keep0, got0, keep1, got1 = ins
            for n in range(1 + n_y):
                a, b, i = (keep0, got0, 0) if n == 0 else (keep1, got1, n - 1)
                for p in every:
                    outs[n][p] = add_all([a[i, p], b[i, p]], True)

        mine_a, *others_a = run(
            "add_core_att",
            add_core_att,
            [ka0, ga0, ka1, ga1],
            [shape((n_dp, chunk, lane), BF16)] * (1 + n_y),
        )
        kept_d, sent_d, at_d = add_split([mine_d] + got_d, no_x, 2)
        kept_u, sent_u, at_u = add_split([kept_u, got_u], at_u, 1)
        (sent_d, sent_u), others_a = together([sent_d, sent_u], others_a)
        got_d, got_u, got_a = dp_swap(sent_d, 2), dp_swap(sent_u, 1), spread_y(others_a)

        def join_split(parts_d, parts_u, places, bit):
            picks = split(places, bit)

            def fn(ins, outs, _):
                for n, mine in enumerate(take(ins, [len(parts_d), len(parts_u)])):
                    for dst, pick in zip(outs, picks):
                        for at, i in enumerate(pick):
                            dst[at, n] = add_all([v[i] for v in mine])

            half = shape((len(picks[0]), 2, sub, hid), BF16)
            kept, sent = run("join_split", fn, parts_d + parts_u, [half, half])
            return kept, sent, [places[i] for i in picks[0]]

        both, sent, at_both = join_split([kept_d, got_d], [kept_u, got_u], at_d, last_bits[0])
        got = dp_swap(sent, last_bits[0])
        for bit in last_bits[1:]:
            both, sent, at_both = add_split([both, got], at_both, bit)
            got = dp_swap(sent, bit)
        both = add_whole([both, got])
        kept_a, sent_a, at_a = add_split([mine_a] + got_a, every, 1, True)

        (both, sent_a), sends = together([both, sent_a], row_parts[1:])
        got = dp_swap(both, last_bits[-1])
        got_a = dp_swap(sent_a, 1)
        row_parts = list(row_parts[:1]) + spread(sends)
        for bit in reversed(last_bits):
            if bit != last_bits[-1]:
                got = dp_swap(both, bit)
            if bit != last_bits[0]:
                both, at_both = jnp.concatenate([both, got]), at_both + [p ^ bit for p in at_both]
        at_both = at_both + [p ^ last_bits[0] for p in at_both]

        def part(ins, outs, _):
            half = ins[0].shape[0]
            for n, o in enumerate(outs):
                for i in range(half):
                    o[i] = ins[0][i, n]
                    o[half + i] = ins[1][i, n]

        down, up = run("part", part, [both, got], [shape((len(at_both), sub, hid), BF16)] * 2)
        kept_a, sent_a, at_a = add_split([kept_a, got_a], at_a, 2, True)
        (down, up, sent_a), row_parts[2:3] = together([down, up, sent_a], row_parts[2:3])
        got_d, got_u, got_a = dp_swap(down, 2), dp_swap(up, 1), dp_swap(sent_a, 2)
        down, at_down = jnp.concatenate([down, got_d]), at_both + [p ^ 2 for p in at_both]
        up, at_up = jnp.concatenate([up, got_u]), at_both + [p ^ 1 for p in at_both]
        kept_a, sent_a, at_a = add_split([kept_a, got_a], at_a, last_bits[0], True)
        (down, up, sent_a), row_parts[3:4] = together([down, up, sent_a], row_parts[3:4])
        got_d, got_u, got_a = dp_swap(down, 1), dp_swap(up, 2), dp_swap(sent_a, last_bits[0])
        for bit in last_bits[1:]:
            kept_a, sent_a, at_a = add_split([kept_a, got_a], at_a, bit, True)
            got_a = dp_swap(sent_a, bit)
        att = add_whole([kept_a, got_a], True)
        for bit in [*reversed(last_bits), 2]:
            if bit == 2:
                (att, got_d, got_u), row_parts = together([att, got_d, got_u], row_parts)
            att = jnp.concatenate([att, dp_swap(att, bit)])
            at_a = at_a + [p ^ bit for p in at_a]
        got_a = dp_swap(att, 1)

        def finish_mlp(ins, outs, scratch):
            dpi = lax.axis_index("dp")
            for n, p in enumerate(at_down):
                for v, at in zip(ins[:2], (p, p ^ 1)):
                    scratch[0][rows_of(dpi ^ at, sub)] = v[n].astype(F32)
            for n, p in enumerate(at_up):
                for v, at in zip(ins[2:], (p, p ^ 2)):
                    outs[1][rows_of(dpi ^ at, sub)] = v[n].astype(F32)
            outs[0][...] = scratch[0][...].T

        r_down, r_up = run(
            "finish_mlp",
            finish_mlp,
            [down, got_d, up, got_u],
            [shape((hid, width), F32), shape((width, hid), F32)],
            [pltpu.VMEM((width, hid), F32)],
        )

        def finish_att(ins, outs, scratch):
            r_qkv, r_out, gain, shift, outb, qvb, upb, order = outs
            turned_out, vec_f = scratch
            dpi = lax.axis_index("dp")
            for src, n, p in [(0, n, p) for n, p in enumerate(at_a)] + [
                (1, n, p ^ 1) for n, p in enumerate(at_a)
            ]:
                v = ins[src][n]
                at = dpi ^ p
                here = rows_of(at, sub)
                for t in range(3):
                    r_qkv[t, here] = v[t * sub : (t + 1) * sub].astype(F32)
                turned_out[here] = v[3 * sub : 4 * sub].astype(F32)
                pairs = v[4 * sub :].astype(F32)
                vec_f[rows_of(at, VEC)] = pairs[:VEC] + pairs[VEC:]
            r_out[...] = turned_out[...].T
            for i in range(6):
                dst = (gain, shift, outb)[i // 2]
                dst[i % 2 : i % 2 + 1] = jnp.concatenate(
                    [vec_f[i * cols + c : i * cols + c + 1] for c in range(cols)], 1
                )
            base = 6 * cols
            qvb[...] = vec_f[base : base + 2]
            upb[...] = jnp.concatenate(
                [vec_f[base + 2 + i : base + 3 + i] for i in range(hid_rows)], 1
            )
            order[...] = vec_f[base + 2 + hid_rows : base + 3 + hid_rows, :per]

        pair_shape = shape((2, width), F32)
        def gather_rows(ins, outs, _):
            me = lax.axis_index("mp")
            for k in range(n_mp):
                here = pl.ds((me ^ k) * own, own)
                outs[0][here] = ins[k][:own]
                outs[1][here] = ins[k][own:].astype(F32)

        output, token_gradient = run(
            "gather_rows",
            gather_rows,
            row_parts,
            [shape((rows, share, width), BF16), shape((rows, share, width), F32)],
        )
        r_qkv, r_out, gain, shift, outb, qvb, upb, order = run(
            "finish_att",
            finish_att,
            [att, got_a],
            [
                shape((3, width, lane), F32),
                shape((lane, width), F32),
                pair_shape,
                pair_shape,
                pair_shape,
                shape((2, lane), F32),
                shape((1, hid), F32),
                shape((1, per), F32),
            ],
            [pltpu.VMEM((width, lane), F32), pltpu.VMEM((vec_rows, lane), F32)],
            after=[r_up, output],
        )

        return (
            output,
            token_gradient,
            gain,
            shift,
            r_qkv,
            qvb,
            order.reshape(per),
            r_out,
            outb,
            r_up,
            upb.reshape(hid),
            r_down,
        )

    return body


def solution(mesh):
    return jax.shard_map(
        make_body(mesh.shape["dp"], mesh.shape["mp"]),
        mesh=mesh,
        in_specs=(
            P("dp", "mp", None),
            P("dp"),
            P("dp", None),
            P(),
            P(),
            P(None, None, "mp"),
            P(None, "mp"),
            P("mp"),
            P("mp", None),
            P(),
            P(None, "mp"),
            P("mp"),
            P("mp", None),
            P("dp", "mp", None),
        ),
        out_specs=(
            P("dp", "mp", None),
            P("dp", "mp", None),
            P(),
            P(),
            P(None, None, "mp"),
            P(None, "mp"),
            P("mp"),
            P("mp", None),
            P(),
            P(None, "mp"),
            P("mp"),
            P("mp", None),
        ),
        check_vma=False,
    )
```

```python
import jax
import jax.numpy as jnp
from jax import lax
from jax.experimental import pallas as pl
from jax.experimental.pallas import tpu as pltpu
from jax.sharding import PartitionSpec as P

HD = 64
PAIR = 2 * HD
LANES = 128
F32 = jnp.float32
BF16 = jnp.bfloat16
VMEM_LIMIT = 28 * 2**20
VMEM_MOST = 60 * 2**20
GELU_C = 0.7978845608028654
GELU_A = 0.044715
VEC = 8


def swap(v, axis, bit, size):
    return lax.ppermute(v, axis, [(i, i ^ bit) for i in range(size)])


def bits_of(size):
    return [1 << b for b in range(size.bit_length() - 1)]


def shape(dims, kind):
    return jax.ShapeDtypeStruct(tuple(dims), kind)


def together(*lists):
    out = lax.optimization_barrier(tuple(tuple(v) for v in lists))
    return [list(v) for v in out]


def run(name, fn, ins, outs, scratch=(), smem=(), after=(), hbm=(), limit=VMEM_LIMIT):
    n_in, n_out, n_all = len(ins), len(outs), len(ins) + len(after)

    def kernel(*refs):
        fn(refs[:n_in], refs[n_all : n_all + n_out], refs[n_all + n_out :])

    return pl.pallas_call(
        kernel,
        out_shape=tuple(outs),
        in_specs=[
            pl.BlockSpec(
                memory_space=pltpu.SMEM if i in smem else pl.ANY if i in hbm else pltpu.VMEM
            )
            for i in range(n_in)
        ]
        + [pl.BlockSpec(memory_space=pl.ANY) for _ in after],
        out_specs=tuple(pl.BlockSpec(memory_space=pltpu.VMEM) for _ in outs),
        scratch_shapes=list(scratch),
        compiler_params=pltpu.CompilerParams(vmem_limit_bytes=limit),
        cost_estimate=pl.CostEstimate(flops=1, bytes_accessed=1, transcendentals=0),
        name=name,
    )(*ins, *after)


def dot(a, b):
    return jnp.dot(a, b, preferred_element_type=F32)


def dot_nt(a, b):
    return lax.dot_general(a, b, (((1,), (1,)), ((), ())), preferred_element_type=F32)


def dot_tn(a, b):
    return lax.dot_general(a, b, (((0,), (0,)), ((), ())), preferred_element_type=F32)


def normalize(v):
    centre = v - jnp.mean(v, -1, keepdims=True)
    rstd = lax.rsqrt(jnp.mean(centre * centre, -1, keepdims=True) + 1e-05)
    return centre * rstd, rstd


def norm_back(g, normed, rstd, gain):
    e = g * gain
    return rstd * (
        e - jnp.mean(e, -1, keepdims=True) - normed * jnp.mean(e * normed, -1, keepdims=True)
    )


def rows_of(start, size):
    return pl.ds(pl.multiple_of(start * size, size), size)


def whole(pieces, x_bit):
    if len(pieces) == 1:
        return pieces[0][...]
    a, b = pieces[0][...], pieces[1][...]
    first = x_bit == 0
    return jnp.concatenate([jnp.where(first, a, b), jnp.where(first, b, a)], 0)


def take(refs, counts):
    out, at = [], 0
    for c in counts:
        out.append(refs[at : at + c])
        at += c
    assert at == len(refs)
    return out


def three_parts(v):
    high = v.astype(BF16).astype(F32)
    rest = v - high
    middle = rest.astype(BF16).astype(F32)
    return jnp.concatenate([high, middle, rest - middle, jnp.zeros_like(v)], 0).astype(BF16)


def two_parts(v):
    high = v.astype(BF16).astype(F32)
    return jnp.concatenate([high, v - high], 0).astype(BF16)


def make_body(n_dp, n_mp):
    groups = [[0, 1], list(range(2, n_mp))]
    y_peers = list(range(2, n_mp, 2))
    def body(
        tokens,
        lengths,
        order_mask,
        norm_scale_pair,
        norm_offset_pair,
        w_qkv,
        qv_bias,
        order_bias,
        w_out,
        out_bias,
        w_up,
        up_bias,
        w_down,
        cotangent,
    ):
        rows, share, width = tokens.shape
        slots = order_mask.shape[1]
        own = rows // n_mp
        count = own * slots
        lane = qv_bias.shape[1]
        per = order_bias.shape[0]
        hid = up_bias.shape[0]
        hid_rows = hid // lane
        cols = width // lane
        piece = shape((own, share, width), BF16)
        sub = width // n_dp
        factor = HD**-0.5
        o_at, s_at = 3 * width, 4 * width
        bundle_rows = 4 * width + 4 * VEC

        def mp_swap(v, bit):
            return swap(v, "mp", bit, n_mp)

        def dp_swap(v, bit):
            return swap(v, "dp", bit, n_dp)

        def send_rows(core, pairs):
            return [mp_swap(core, 1)] + spread_y(pairs)

        def pass_rows(pairs):
            half = pairs[0].shape[0] // 2
            passed = [mp_swap(v[half:], 1) for v in pairs]
            return [p for pair in zip(pairs, passed) for p in pair]

        def over_y(v):
            return [mp_swap(v, k) for k in y_peers]

        def spread_y(parts):
            return [mp_swap(v, k) for k, v in zip(y_peers, parts)]

        row_shapes = [piece] * 2 + [shape((2 * own, share, width), BF16)] * len(y_peers)

        def cut_copies(src, outs, sems):
            me = lax.axis_index("mp")
            copies = []
            for k in range(n_mp):
                dst = outs[k] if k < 2 else outs[k // 2 + 1].at[pl.ds((k % 2) * own, own)]
                here = src.at[pl.ds((me ^ k) * own, own)]
                copies.append(pltpu.make_async_copy(here, dst, sems.at[k]))
            for c in copies:
                c.start()
            return copies

        def begin(ins, outs, scratch):
            x_bit = lax.axis_index("dp") & 1
            bundle, half = outs[-2:]
            copies = cut_copies(ins[0], outs, scratch[0])
            copies.append(
                pltpu.make_async_copy(ins[1], bundle.at[pl.ds(0, o_at)], scratch[1])
            )
            copies[-1].start()
            for c in range(cols):
                bundle[o_at + c * lane : o_at + (c + 1) * lane] = ins[2][
                    :, c * lane : (c + 1) * lane
                ]
            small = jnp.concatenate(
                [
                    ins[3][...],
                    ins[4][...],
                    jnp.concatenate([ins[5][...], jnp.zeros((1, lane - per), F32)], 1),
                    jnp.zeros((VEC - 3 - hid_rows, lane), F32),
                ],
                0,
            )
            bundle[s_at:] = three_parts(small)
            for c in copies:
                c.wait()
            half[...] = bundle[rows_of(x_bit, bundle_rows // 2)]

        *token_parts, bundle, bundle_half = run(
            "begin",
            begin,
            [
                tokens,
                w_qkv.reshape(-1, lane),
                w_out,
                qv_bias,
                up_bias.reshape(hid_rows, lane),
                order_bias.reshape(1, per),
            ],
            row_shapes
            + [shape((bundle_rows, lane), BF16), shape((bundle_rows // 2, lane), BF16)],
            [pltpu.SemaphoreType.DMA((n_mp,)), pltpu.SemaphoreType.DMA(())],
            hbm=(0, 1),
            limit=VMEM_MOST,
        )

        def cut_rest(ins, outs, scratch):
            dpi = lax.axis_index("dp")
            copies = cut_copies(ins[0], outs, scratch[0])
            halves = outs[len(row_shapes) :]
            for n, (src, bit) in enumerate(zip(ins[1:], (dpi & 1, (dpi >> 1) & 1))):
                here = src.at[rows_of(bit, src.shape[0] // 2)]
                dst = halves[0].at[n] if joined else halves[n]
                copies.append(pltpu.make_async_copy(here, dst, scratch[1].at[n]))
                copies[-1].start()
            for c in copies:
                c.wait()

        joined = w_up.shape == w_down.shape
        half_shapes = [shape((v.shape[0] // 2, v.shape[1]), BF16) for v in (w_up, w_down)]
        rest = run(
            "cut_rest",
            cut_rest,
            [cotangent, w_up, w_down],
            row_shapes
            + ([shape((2,) + half_shapes[0].shape, BF16)] if joined else half_shapes),
            [pltpu.SemaphoreType.DMA((n_mp,)), pltpu.SemaphoreType.DMA((2,))],
            hbm=(0, 1, 2),
            after=[bundle_half],
        )
        cot_parts, half_parts = list(rest[: len(row_shapes)]), rest[len(row_shapes) :]

        sends, (bundle, bundle_half) = together(token_parts[1:], [bundle, bundle_half])
        token_parts = token_parts[:1] + send_rows(sends[0], sends[1:])
        bundle_core, bundle_y = mp_swap(bundle, 1), over_y(bundle_half)

        bundle_y, token_parts, cot_parts = together(bundle_y, token_parts, cot_parts)
        halves_y = [over_y(v) for v in half_parts]
        token_parts = token_parts[:2] + pass_rows(token_parts[2:])
        bundle_y, token_parts = together(bundle_y, token_parts)
        bundle_x = [dp_swap(v, 1) for v in bundle_y]
        bundle_yc = [mp_swap(v, 1) for v in bundle_y]

        def far(first, second, first_core, second_core):
            return [
                v
                for n in range(len(y_peers))
                for v in (first[n], second[n], first_core[n], second_core[n])
            ]

        def order_row(om_ref, me, r):
            v = om_ref[pl.ds(me * own + r, 1), :].astype(F32)
            v = jnp.broadcast_to(v, (8, slots))
            at = lax.broadcasted_iota(jnp.int32, (8, slots), 1)
            step = share
            while step < slots:
                turned = jnp.where(
                    (at & step) == 0, pltpu.roll(v, slots - step, 1), pltpu.roll(v, step, 1)
                )
                v = jnp.where((me * share) & step, turned, v)
                step *= 2
            return v[:1]

        def keep_row(me, length):
            at = lax.broadcasted_iota(jnp.int32, (1, slots), 1)
            return (at ^ (me * share)) < length

        def keep_column(me, length):
            at = lax.broadcasted_iota(jnp.int32, (slots, 1), 0)
            return ((at ^ (me * share)) < length).astype(F32)

        def head_mask(pair_value, h):
            at = lax.broadcasted_iota(jnp.int32, pair_value.shape, 1)
            return jnp.where((at >= HD) == (h % 2 == 1), pair_value, jnp.zeros_like(pair_value))

        def assemble(dst, parts):
            for r in range(own):
                for k in range(n_mp):
                    dst[r * slots + k * share : r * slots + (k + 1) * share] = parts[k][r]

        def cut_slots(dst, lead, value):
            for r in range(own):
                for k in range(n_mp):
                    at = r * slots + k * share
                    to, first = (dst[k], 0) if k < 2 else (dst[k // 2 + 1], (k % 2) * 2 * own)
                    to[first + lead + r] = value[at : at + share]

        def attend(group, first, pieces):
            wide = lane * len(group)
            heads = wide // HD
            counts = [len(pieces) // len(group)] * len(group)

            def fn(ins, outs, scratch):
                me, x_bit = lax.axis_index("mp"), lax.axis_index("dp") & 1
                qkv_ref, p_ref, att_ref, weights, wo, smalls = outs[-6:]
                if first:
                    lens, om, gains, shifts = ins[n_mp : n_mp + 4]
                    x_ref, a1_ref = outs[:2]
                    assemble(x_ref, ins[:n_mp])
                    normed, _ = normalize(x_ref[...].astype(F32))
                    a1_ref[...] = (normed * gains[0:1] + shifts[0:1]).astype(BF16)
                else:
                    lens, om, a1_ref = ins[:3]
                for j, ps in enumerate(take(ins[-len(pieces) :], counts)):
                    v = whole(ps, x_bit)
                    weights[:, j * lane : (j + 1) * lane] = v[:o_at]
                    for c in range(cols):
                        wo[j * lane : (j + 1) * lane, c * lane : (c + 1) * lane] = v[
                            o_at + c * lane : o_at + (c + 1) * lane
                        ]
                    parts = v[s_at:].astype(F32)
                    smalls[j] = parts[:VEC] + parts[VEC : 2 * VEC] + parts[2 * VEC : 3 * VEC]
                a1 = a1_ref[...]
                for t in range(3):
                    y = dot(a1, weights[t * width : (t + 1) * width])
                    if t != 1:
                        i = t // 2
                        y = y + jnp.concatenate(
                            [smalls[j, i : i + 1] for j in range(len(group))], 1
                        )
                    qkv_ref[t] = y.astype(BF16)
                for r in range(own):
                    length = lens[me * own + r]
                    order = order_row(om, me, r)
                    kept = keep_row(me, length)
                    column = keep_column(me, length)
                    here = slice(r * slots, (r + 1) * slots)
                    for pair in range(heads // 2):
                        at = slice(pair * PAIR, (pair + 1) * PAIR)
                        q = qkv_ref[0, here, at] * jnp.asarray(factor, BF16)
                        key = qkv_ref[1, here, at]
                        val = qkv_ref[2, here, at]
                        acc = None
                        for h in (2 * pair, 2 * pair + 1):
                            o = 2 + hid_rows
                            ob = smalls[h // per, o : o + 1, h % per : h % per + 1]
                            row = jnp.where(kept, ob * order, -1e30)
                            s = dot_nt(head_mask(q, h), key) + row
                            e = jnp.exp(s - jnp.max(s, -1, keepdims=True))
                            p = (e * (1.0 / jnp.sum(e, -1, keepdims=True))).astype(BF16)
                            p_ref[r * heads + h] = p
                            term = dot(p, head_mask(val, h))
                            acc = term if acc is None else acc + term
                        att_ref[here, at] = (acc * column).astype(BF16)

            ins = (
                token_parts + [lengths, order_mask, norm_scale_pair, norm_offset_pair]
                if first
                else [lengths, order_mask, a1]
            )
            lead = [shape((count, width), BF16)] * 2 if first else []
            return run(
                "attend",
                fn,
                ins + pieces,
                lead
                + [
                    shape((3, count, wide), BF16),
                    shape((own * heads, slots, slots), BF16),
                    shape((count, wide), BF16),
                    shape((3 * width, wide), BF16),
                    shape((wide, width), BF16),
                    shape((len(group), VEC, lane), F32),
                ],
                smem=(n_mp if first else 0,),
            )

        x, a1, qkv0, p0, att0, wq0, wo0, small0 = attend(groups[0], True, [bundle, bundle_core])

        bundle_x, (att0,), near = together(bundle_x, [att0], [w_up, w_down])
        bundle_xc = [mp_swap(v, 1) for v in bundle_x]
        near_core = [mp_swap(v, 1) for v in near]
        qkv1, p1, att1, wq1, wo1, small1 = attend(
            groups[1], False, far(bundle_y, bundle_x, bundle_yc, bundle_xc)
        )

        def take_apart(ins, outs, _):
            for n, o in enumerate(outs):
                o[...] = ins[0][n]

        if joined:
            pairs = [run("take_apart", take_apart, [v], half_shapes, after=[att1]) for v in halves_y[0]]
            halves_y = list(zip(*pairs))
        up_y, down_y, (att1,), near_core, sends = together(
            *halves_y, [att1], near_core, cot_parts[1:]
        )
        up_x, down_z = [dp_swap(v, 1) for v in up_y], [dp_swap(v, 2) for v in down_y]
        cot_parts = cot_parts[:1] + send_rows(sends[0], sends[1:])
        cot_parts = cot_parts[:2] + pass_rows(cot_parts[2:])

        def scatter(dst, src, block, which, dpi):
            for p in range(n_dp):
                dst[block, which, p] = src[rows_of(dpi ^ p, sub), :]

        def mlp_forward(a2, wu, wd, bias, mixed):
            up = jnp.concatenate([bias[2 + i : 3 + i] for i in range(hid_rows)], 1)
            pre = dot(a2[...], wu) + up
            square = pre * pre
            t = jnp.tanh(pre * (GELU_C + (GELU_C * GELU_A) * square))
            half = 0.5 + 0.5 * t
            hidden = (pre * half).astype(BF16)
            slope = half + (pre * (1.0 - t * t)) * (
                0.5 * GELU_C + (1.5 * GELU_C * GELU_A) * square
            )
            mixed[...] += dot(hidden, wd)
            return hidden, slope

        def mlp_backward(hidden, slope, a2t, dy, dyt, wu, wd, d_mid, gs, dst, block, bias_sum, dpi):
            d_hidden = dot_nt(dy[...], wd)
            d_pre = (slope * d_hidden).astype(BF16)
            d_mid[...] += dot_nt(d_pre, wu)
            g_down, g_up = gs.at[0], gs.at[1]
            g_down[...] = dot(dyt[...], hidden).astype(BF16)
            scatter(dst, g_down, block, 0, dpi)
            g_up[...] = dot(a2t[...], d_pre).astype(BF16)
            scatter(dst, g_up, block, 1, dpi)
            bias_sum[...] = jnp.sum(d_pre.astype(F32), 0, keepdims=True)

        def mlp_outs(n_blocks, n_arrays):
            both = shape((n_blocks // n_arrays, 2, n_dp, sub, hid), BF16)
            return [both] * n_arrays + [shape((n_blocks, 1, hid), F32)]

        full = shape((count, width), F32)
        full_bf = shape((count, width), BF16)
        turned = shape((width, count), BF16)
        g0, g1 = groups

        def mlp_near_forward(ins, outs, _):
            lead, wu_p, wd_p = take(ins, [9, len(g0), len(g0)])
            x_ref, att0_ref, att1_ref, wo0_ref, wo1_ref, smalls, gains, shifts, ob = lead
            x1, a2, a2t, mixed, hidden, slope = outs
            v = x_ref[...].astype(F32) + (
                dot(att0_ref[...], wo0_ref[...]) + dot(att1_ref[...], wo1_ref[...]) + ob[0:1]
            )
            x1[...] = v
            normed, _ = normalize(v)
            act = (normed * gains[1:2] + shifts[1:2]).astype(BF16)
            a2[...] = act
            a2t[...] = act.T
            mixed[...] = jnp.zeros_like(mixed)
            for j in range(len(g0)):
                hidden[j], slope[j] = mlp_forward(
                    a2, wu_p[j][...], wd_p[j][...], smalls.at[j], mixed
                )

        near_up, near_down = [near[0], near_core[0]], [near[1], near_core[1]]
        x1, a2, a2t, mixed, hidden, slope = run(
            "mlp_near_forward",
            mlp_near_forward,
            [x, att0, att1, wo0, wo1, small0, norm_scale_pair, norm_offset_pair, out_bias]
            + near_up
            + near_down,
            [full, full_bf, turned, full]
            + [shape((len(g0), count, hid), BF16), shape((len(g0), count, hid), F32)],
        )

        def mlp_near_backward(ins, outs, scratch):
            dpi = lax.axis_index("dp")
            (hidden, slope, a2t), dy_p, wu_p, wd_p = take(ins, [3, n_mp, len(g0), len(g0)])
            dy, dyt, d_mid = outs[:3]
            assemble(dy, dy_p)
            dyt[...] = dy[...].T
            d_mid[...] = jnp.zeros_like(d_mid)
            for j, k in enumerate(g0):
                mlp_backward(
                    hidden[j],
                    slope[j],
                    a2t,
                    dy,
                    dyt,
                    wu_p[j][...],
                    wd_p[j][...],
                    d_mid,
                    scratch[j],
                    outs[3 + k % 2],
                    0,
                    outs[5].at[j],
                    dpi,
                )

        dy, dyt, d_mid, keep0, send0, gub0 = run(
            "mlp_near_backward",
            mlp_near_backward,
            [hidden, slope, a2t] + cot_parts + near_up + near_down,
            [full_bf, turned, full] + mlp_outs(len(g0), 2),
            [pltpu.VMEM((2, width, hid), BF16)] * len(g0),
        )

        far_parts = together(up_y, up_x, down_y, down_z, [mixed])
        up_y, up_x, down_y, down_z, (mixed,) = far_parts
        up_yc, up_xc, down_yc, down_zc = (
            [mp_swap(v, 1) for v in vs] for vs in (up_y, up_x, down_y, down_z)
        )
        got0 = mp_swap(send0, 1)

        up1 = far(up_y, up_x, up_yc, up_xc)
        down1 = far(down_y, down_z, down_yc, down_zc)

        def mlp_far(j, last):
            ks = g1[j::2]
            n_w = 2 * len(ks)

            def fn(ins, outs, scratch):
                dpi = lax.axis_index("dp")
                lead, wu_p, wd_p = take(ins, [10, n_w, n_w])
                x1, a2, a2t, dy, dyt, mixed_in, d_mid_in, smalls, gains, ob = lead
                (mixed, d_mid), gs = (scratch[:2], scratch[2:]) if last else (outs[:2], scratch)
                mixed[...] = mixed_in[...]
                d_mid[...] = d_mid_in[...]
                grads, bias_sums = outs[-2:]
                for n in range(len(ks)):
                    wu = whole(wu_p[2 * n : 2 * n + 2], dpi & 1)
                    wd = whole(wd_p[2 * n : 2 * n + 2], (dpi >> 1) & 1)
                    hidden, slope = mlp_forward(a2, wu, wd, smalls.at[2 * n + j], mixed)
                    mlp_backward(
                        hidden,
                        slope,
                        a2t,
                        dy,
                        dyt,
                        wu,
                        wd,
                        d_mid,
                        gs[n],
                        grads,
                        n,
                        bias_sums.at[n],
                        dpi,
                    )
                if not last:
                    return
                output, dx1, d_att, vec = outs[:4]
                v = x1[...]
                output[...] = (v + (mixed[...] + ob[1:2])).astype(BF16)
                normed, rstd = normalize(v)
                g = d_mid[...]
                dyf = dy[...].astype(F32)
                d = dyf + norm_back(g, normed, rstd, gains[1:2])
                dx1[...] = d
                low = d.astype(BF16)
                d_att[...] = low
                vec[0:1] = jnp.sum(g * normed, 0, keepdims=True)
                vec[1:2] = jnp.sum(g, 0, keepdims=True)
                vec[2:3] = jnp.sum(low.astype(F32), 0, keepdims=True)
                vec[3:4] = jnp.sum(dyf, 0, keepdims=True)

            sums = [pltpu.VMEM((count, width), F32)] * 2
            return run(
                "mlp_far",
                fn,
                [x1, a2, a2t, dy, dyt, mixed, d_mid, small1, norm_scale_pair, out_bias]
                + [v for n in range(len(ks)) for v in up1[4 * n + 2 * j : 4 * n + 2 * j + 2]]
                + [v for n in range(len(ks)) for v in down1[4 * n + 2 * j : 4 * n + 2 * j + 2]],
                ([full_bf, full, full_bf, shape((4, width), F32)] if last else [full, full])
                + mlp_outs(len(ks), 1),
                (sums if last else []) + [pltpu.VMEM((2, width, hid), BF16)] * len(ks),
            )

        mixed, d_mid, send1, gub1_odd = mlp_far(1, False)
        send1, mixed = together([send1, mixed])[0]
        got1 = mp_swap(send1, 1)
        out_rows, dx1, d_att, vec, keep1, gub1_even = mlp_far(0, True)

        def add_all(values, vectors=False):
            total = values[0].astype(F32)
            for v in values[1:]:
                total = total + v.astype(F32)
            if not vectors:
                return total.astype(BF16)
            m = total.shape[-2]
            head = total[: m - 2 * VEC]
            v = total[m - 2 * VEC : m - VEC] + total[m - VEC :]
            high = v.astype(BF16).astype(F32)
            return jnp.concatenate([head, high, v - high], 0).astype(BF16)

        n_y = len(y_peers)

        def split(places, bit):
            return [i for i, p in enumerate(places) if not p & bit], [
                i for i, p in enumerate(places) if p & bit
            ]

        def add_split(parts, places, bit, vectors=False, after=(), two=False, halves=()):
            picks = split(places, bit)
            n_parts, n_half = len(parts), len(places) // 2

            def fn(ins, outs, _):
                for pick, dsts in zip(picks, (outs[:1], outs[1:])):
                    for at, i in enumerate(pick):
                        values = [v[i] for v in ins[:n_parts]]
                        if halves:
                            values.append(ins[n_parts + i // n_half][i % n_half])
                        size = dsts[0].shape[0]
                        dsts[at // size][at % size] = add_all(values, vectors)

            n, rest = len(picks[0]), parts[0].shape[1:]
            sizes = [n] + ([n // 2] * 2 if two else [n])
            kept, *sent = run(
                "add_split",
                fn,
                list(parts) + list(halves),
                [shape((k,) + rest, BF16) for k in sizes],
                after=after,
            )
            return kept, sent if two else sent[0], [places[i] for i in picks[0]]

        def add_whole(parts, vectors=False):
            def fn(ins, outs, _):
                for i in range(outs[0].shape[0]):
                    outs[0][i] = add_all([v[i] for v in ins], vectors)

            return run("add_whole", fn, parts, [shape(parts[0].shape, BF16)])[0]

        def meet(mine, got, places, bit, vectors):
            def fn(ins, outs, _):
                for i, p in enumerate(places):
                    outs[0][i] = add_all([ins[0][i], ins[1][places.index(p ^ bit)]], vectors)

            return run("meet", fn, [mine, got], [shape(mine.shape, BF16)])[0]

        every = list(range(n_dp))
        no_x, with_x = split(every, 1)
        last_bits = [b for b in bits_of(n_dp) if b > 2]

        def add_core_mlp(ins, outs, _):
            keep0, got0, keep1, got1 = ins
            kept, sent, mine = outs[:3]
            for n in range(1 + n_y):
                a, b, i = (keep0, got0, 0) if n == 0 else (keep1, got1, n - 1)
                for dst, pick in ((kept, no_x), (sent, with_x)):
                    for at, p in enumerate(pick):
                        dst[n, at] = add_all([a[i, 0, p], b[i, 0, p]])
                up = mine if n == 0 else outs[3 + n - 1]
                for p in every:
                    up[p] = add_all([a[i, 1, p], b[i, 1, p]])

        kept_d, sent_d, mine_u, *others_u = run(
            "add_core_mlp",
            add_core_mlp,
            [keep0, got0, keep1, got1],
            [shape((1 + n_y, n_dp // 2, sub, hid), BF16)] * 2
            + [shape((n_dp, sub, hid), BF16)] * (1 + n_y),
        )
        (sent_d, d_att), others_u = together([sent_d, d_att], others_u)
        got_d = dp_swap(sent_d, 1)
        got_u = spread_y(others_u)

        vec_rows = n_dp * VEC
        chunk = 4 * sub + 2 * VEC

        def attend_back(ins, outs, scratch):
            me, dpi = lax.axis_index("mp"), lax.axis_index("dp")
            (lens, om, gains), fulls, qkvs, ps, atts, wqs, wos, vecs = take(
                ins, [3, 5, 2, 2, 2, 2, 2, 4]
            )
            x_ref, a1_ref, dx1, d_att, out_ref = fulls
            vec, gub_near, gub_even, gub_odd = vecs
            parts, grads = outs[:-4], outs[-4:]
            dqkvs, gqs = scratch[:2], scratch[2:4]
            d_in, vec_f, shared = scratch[4:]
            a1t = a1_ref[...].T
            d_att_v = d_att[...]
            d_att_t = d_att_v.T
            d_in[...] = jnp.zeros_like(d_in)
            cut_slots(parts, 0, out_ref[...])
            order_sums = {}
            for gi, group in enumerate(groups):
                wide = lane * len(group)
                heads = wide // HD
                qkv_ref, p_ref, att_ref = qkvs[gi], ps[gi], atts[gi]
                wq, wo, dqkv, gq = wqs[gi], wos[gi], dqkvs[gi], gqs[gi]
                d_o = dot_nt(d_att_v, wo[...]).astype(BF16)
                for r in range(own):
                    length = lens[me * own + r]
                    order = order_row(om, me, r)
                    kept = keep_row(me, length)
                    column = keep_column(me, length).astype(BF16)
                    here = slice(r * slots, (r + 1) * slots)
                    for pair in range(heads // 2):
                        at = slice(pair * PAIR, (pair + 1) * PAIR)
                        q = qkv_ref[0, here, at] * jnp.asarray(factor, BF16)
                        key = qkv_ref[1, here, at] * jnp.asarray(factor, BF16)
                        val = qkv_ref[2, here, at]
                        do = d_o[here, at] * column
                        dq = dk = dv = 0.0
                        for h in (2 * pair, 2 * pair + 1):
                            p_low = p_ref[r * heads + h]
                            p = p_low.astype(F32)
                            do_h = head_mask(do, h)
                            d_p = dot_nt(do_h, val)
                            inner = jnp.sum(p * d_p, -1, keepdims=True)
                            d_s = jnp.where(kept, p * (d_p - inner), 0.0).astype(BF16)
                            sums = dot(jnp.ones((8, slots), BF16), d_s)[:1] * order
                            name = (group[h // per], h % per)
                            old = order_sums.get(name)
                            order_sums[name] = sums if old is None else old + sums
                            dq = dq + dot(d_s, head_mask(key, h))
                            dk = dk + dot_tn(d_s, head_mask(q, h))
                            dv = dv + dot_tn(p_low, do_h)
                        dqkv[0, here, at] = dq.astype(BF16)
                        dqkv[1, here, at] = dk.astype(BF16)
                        dqkv[2, here, at] = dv.astype(BF16)
                total = None
                for t in range(3):
                    g = dqkv[t]
                    gq[t] = dot(a1t, g).astype(BF16)
                    term = dot_nt(g, wq[t * width : (t + 1) * width])
                    total = term if total is None else total + term
                d_in[...] += total
                gq[3] = dot(d_att_t, att_ref[...]).astype(BF16)
                for j, k in enumerate(group):
                    dst = grads[2 * gi + k % 2]
                    at = slice(j * lane, (j + 1) * lane)
                    for p in range(n_dp):
                        here = rows_of(dpi ^ p, sub)
                        for t in range(4):
                            dst[j // 2, p, t * sub : (t + 1) * sub] = gq[t, here, at]
                    vec_f[k] = jnp.zeros((vec_rows, lane), F32)
                    base = 6 * cols
                    for n, t in enumerate((0, 2)):
                        vec_f[k, base + n : base + n + 1] = jnp.sum(
                            dqkv[t, :, at].astype(F32), 0, keepdims=True
                        )
                    gub = gub_near[j] if gi == 0 else (gub_even, gub_odd)[j % 2][j // 2]
                    for i in range(hid_rows):
                        vec_f[k, base + 2 + i : base + 3 + i] = gub[:, i * lane : (i + 1) * lane]
                    lanes = lax.broadcasted_iota(jnp.int32, (1, lane), 1)
                    row = jnp.zeros((1, lane), F32)
                    for i in range(per):
                        row = row + jnp.where(
                            lanes == i, jnp.sum(order_sums[(k, i)], -1, keepdims=True), 0.0
                        )
                    vec_f[k, base + 2 + hid_rows : base + 3 + hid_rows] = row
            normed, rstd = normalize(x_ref[...].astype(F32))
            g = d_in[...]
            cut_slots(
                parts, own, (dx1[...] + norm_back(g, normed, rstd, gains[0:1])).astype(BF16)
            )
            shared[0:1] = jnp.sum(g * normed, 0, keepdims=True)
            shared[1:2] = vec[0:1]
            shared[2:3] = jnp.sum(g, 0, keepdims=True)
            shared[3:4] = vec[1:2]
            shared[4:5] = vec[2:3]
            shared[5:6] = vec[3:4]
            for gi, group in enumerate(groups):
                for j, k in enumerate(group):
                    for i in range(6):
                        for c in range(cols):
                            at = i * cols + c
                            vec_f[k, at : at + 1] = shared[i : i + 1, c * lane : (c + 1) * lane]
                    dst = grads[2 * gi + k % 2]
                    for p in range(n_dp):
                        v = vec_f[k, rows_of(dpi ^ p, VEC)]
                        dst[j // 2, p, 4 * sub :] = two_parts(v)

        def grad_shapes(n_blocks):
            return [shape((n_blocks // 2, n_dp, chunk, lane), BF16)] * 2

        back = run(
            "attend_back",
            attend_back,
            [lengths, order_mask, norm_scale_pair]
            + [x, a1, dx1, d_att, out_rows]
            + [qkv0, qkv1, p0, p1, att0, att1, wq0, wq1, wo0, wo1]
            + [vec, gub0, gub1_even, gub1_odd],
            [shape((2 * s.shape[0],) + s.shape[1:], BF16) for s in row_shapes]
            + grad_shapes(len(g0))
            + grad_shapes(len(g1)),
            [
                *[pltpu.VMEM((3, count, lane * len(g)), BF16) for g in groups],
                *[pltpu.VMEM((4, width, lane * len(g)), BF16) for g in groups],
                pltpu.VMEM((count, width), F32),
                pltpu.VMEM((n_mp, vec_rows, lane), F32),
                pltpu.VMEM((8, width), F32),
            ],
            smem=(0,),
        )
        row_parts, (ka0, sa0, ka1, sa1) = back[:-4], back[-4:]

        def add_x(ins, outs, _):
            for n in range(1 + n_y):
                for i in range(n_dp // 2):
                    outs[n][i] = add_all([ins[0][n, i], ins[1][n, i]])

        mine_d, *others_d = run(
            "add_x", add_x, [kept_d, got_d], [shape((n_dp // 2, sub, hid), BF16)] * (1 + n_y)
        )
        kept_u, sent_u, at_u = add_split([mine_u] + got_u, every, 2)
        others_d, (sent_u,), sends = together(others_d, [sent_u], [sa0, sa1])
        got_d = spread_y(others_d)
        got_u = dp_swap(sent_u, 2)
        ga0, ga1 = (mp_swap(v, 1) for v in sends)

        def add_core_att(ins, outs, _):
            keep0, got0, keep1, got1 = ins
            for n in range(1 + n_y):
                a, b, i = (keep0, got0, 0) if n == 0 else (keep1, got1, n - 1)
                for p in every:
                    outs[n][p] = add_all([a[i, p], b[i, p]], True)

        mine_a, *others_a = run(
            "add_core_att",
            add_core_att,
            [ka0, ga0, ka1, ga1],
            [shape((n_dp, chunk, lane), BF16)] * (1 + n_y),
        )
        kept_d, sent_d, at_d = add_split([mine_d] + got_d, no_x, 2)
        kept_u, sent_u, at_u = add_split([kept_u, got_u], at_u, 1)
        (sent_d, sent_u), others_a = together([sent_d, sent_u], others_a)
        got_d, got_u, got_a = dp_swap(sent_d, 2), dp_swap(sent_u, 1), spread_y(others_a)

        def join(ins, outs, _):
            for n, mine in enumerate((ins[:2], ins[2:])):
                for i in range(outs[0].shape[0]):
                    outs[0][i, n] = add_all([v[i] for v in mine])

        (both,) = run(
            "join",
            join,
            [kept_d, got_d, kept_u, got_u],
            [shape((len(at_d), 2, sub, hid), BF16)],
        )
        at_both = at_d
        for bit in last_bits[:-1]:
            kept, sent, at_both = add_split([both], at_both, bit)
            both = add_whole([kept, dp_swap(sent, bit)])
        got = dp_swap(both, last_bits[-1])
        kept_a, sent_a, at_a = add_split([mine_a] + got_a, every, 1, True, two=True)
        got_a = [dp_swap(v, 1) for v in sent_a]
        both = meet(both, got, at_both, last_bits[-1], False)
        for bit in reversed(last_bits[:-1]):
            both, at_both = jnp.concatenate([both, dp_swap(both, bit)]), at_both + [
                p ^ bit for p in at_both
            ]

        def part(ins, outs, _):
            for n, o in enumerate(outs):
                for i in range(len(at_both)):
                    o[i] = ins[0][i, n]

        down, up = run("part", part, [both], [shape((len(at_both), sub, hid), BF16)] * 2)
        kept_a, sent_a, at_a = add_split([kept_a], at_a, 2, True, [down], halves=got_a)

        row_parts = list(row_parts)
        row_parts[1:] = send_rows(row_parts[1], row_parts[2:])
        down, up, sent_a = together([down, up, sent_a])[0]
        got_d, got_u, got_a = dp_swap(down, 2), dp_swap(up, 1), dp_swap(sent_a, 2)
        down, at_down = jnp.concatenate([down, got_d]), at_both + [p ^ 2 for p in at_both]
        up, at_up = jnp.concatenate([up, got_u]), at_both + [p ^ 1 for p in at_both]
        if len(last_bits) > 1:
            kept_a, sent_a, at_a = add_split([kept_a, got_a], at_a, last_bits[0], True)
        else:
            kept_a = sent_a = add_whole([kept_a, got_a], True)
        got_d, got_u, got_a = dp_swap(down, 1), dp_swap(up, 2), dp_swap(sent_a, last_bits[0])
        for bit in last_bits[1:]:
            if bit != last_bits[-1]:
                kept_a, sent_a, at_a = add_split([kept_a, got_a], at_a, bit, True)
            else:
                kept_a = sent_a = add_whole([kept_a, got_a], True)
            got_a = dp_swap(sent_a, bit)
        att = meet(kept_a, got_a, at_a, last_bits[-1], True)
        for bit in [*reversed(last_bits[:-1]), 2]:
            if bit == 2:
                (att, got_d, got_u), row_parts = together([att, got_d, got_u], row_parts)
                row_parts = row_parts[:2] + pass_rows(row_parts[2:])
            att = jnp.concatenate([att, dp_swap(att, bit)])
            at_a = at_a + [p ^ bit for p in at_a]
        got_a = dp_swap(att, 1)

        def finish_mlp(ins, outs, scratch):
            dpi = lax.axis_index("dp")
            for n, p in enumerate(at_down):
                for v, at in zip(ins[:2], (p, p ^ 1)):
                    scratch[0][rows_of(dpi ^ at, sub)] = v[n].astype(F32)
            for n, p in enumerate(at_up):
                for v, at in zip(ins[2:], (p, p ^ 2)):
                    outs[1][rows_of(dpi ^ at, sub)] = v[n].astype(F32)
            outs[0][...] = scratch[0][...].T
            outs[2][...] = jnp.zeros((8, LANES), F32)

        mark = shape((8, LANES), F32)
        r_down, r_up, mlp_mark = run(
            "finish_mlp",
            finish_mlp,
            [down, got_d, up, got_u],
            [shape((hid, width), F32), shape((width, hid), F32), mark],
            [pltpu.VMEM((width, hid), F32)],
        )

        def finish_att(ins, outs, scratch):
            r_qkv, r_out, gain, shift, outb, qvb, upb, order = outs
            turned_out, vec_f = scratch
            dpi = lax.axis_index("dp")
            for src, n, p in [(0, n, p) for n, p in enumerate(at_a)] + [
                (1, n, p ^ 1) for n, p in enumerate(at_a)
            ]:
                v = ins[src][n]
                at = dpi ^ p
                here = rows_of(at, sub)
                for t in range(3):
                    r_qkv[t, here] = v[t * sub : (t + 1) * sub].astype(F32)
                turned_out[here] = v[3 * sub : 4 * sub].astype(F32)
                pairs = v[4 * sub :].astype(F32)
                vec_f[rows_of(at, VEC)] = pairs[:VEC] + pairs[VEC:]
            r_out[...] = turned_out[...].T
            for i in range(6):
                dst = (gain, shift, outb)[i // 2]
                dst[i % 2 : i % 2 + 1] = jnp.concatenate(
                    [vec_f[i * cols + c : i * cols + c + 1] for c in range(cols)], 1
                )
            base = 6 * cols
            qvb[...] = vec_f[base : base + 2]
            upb[...] = jnp.concatenate(
                [vec_f[base + 2 + i : base + 3 + i] for i in range(hid_rows)], 1
            )
            order[...] = vec_f[base + 2 + hid_rows : base + 3 + hid_rows, :per]

        pair_shape = shape((2, width), F32)
        def gather_rows(ins, outs, _):
            me = lax.axis_index("mp")
            for k in range(n_mp):
                here = pl.ds((me ^ k) * own, own)
                outs[0][here] = ins[k][:own]
                outs[1][here] = ins[k][own : 2 * own].astype(F32)
            outs[2][...] = jnp.zeros((8, LANES), F32)

        output, token_gradient, rows_mark = run(
            "gather_rows",
            gather_rows,
            row_parts,
            [shape((rows, share, width), BF16), shape((rows, share, width), F32), mark],
        )
        r_qkv, r_out, gain, shift, outb, qvb, upb, order = run(
            "finish_att",
            finish_att,
            [att, got_a],
            [
                shape((3, width, lane), F32),
                shape((lane, width), F32),
                pair_shape,
                pair_shape,
                pair_shape,
                shape((2, lane), F32),
                shape((1, hid), F32),
                shape((1, per), F32),
            ],
            [pltpu.VMEM((width, lane), F32), pltpu.VMEM((vec_rows, lane), F32)],
            after=[mlp_mark, rows_mark],
        )

        return (
            output,
            token_gradient,
            gain,
            shift,
            r_qkv,
            qvb,
            order.reshape(per),
            r_out,
            outb,
            r_up,
            upb.reshape(hid),
            r_down,
        )

    return body


def solution(mesh):
    return jax.shard_map(
        make_body(mesh.shape["dp"], mesh.shape["mp"]),
        mesh=mesh,
        in_specs=(
            P("dp", "mp", None),
            P("dp"),
            P("dp", None),
            P(),
            P(),
            P(None, None, "mp"),
            P(None, "mp"),
            P("mp"),
            P("mp", None),
            P(),
            P(None, "mp"),
            P("mp"),
            P("mp", None),
            P("dp", "mp", None),
        ),
        out_specs=(
            P("dp", "mp", None),
            P("dp", "mp", None),
            P(),
            P(),
            P(None, None, "mp"),
            P(None, "mp"),
            P("mp"),
            P("mp", None),
            P(),
            P(None, "mp"),
            P("mp"),
            P("mp", None),
        ),
        check_vma=False,
    )
```

```python
import jax
import jax.numpy as jnp
from jax import lax
from jax.experimental import pallas as pl
from jax.experimental.pallas import tpu as pltpu
from jax.sharding import PartitionSpec as P

HD = 64
PAIR = 2 * HD
LANES = 128
F32 = jnp.float32
BF16 = jnp.bfloat16
VMEM_LIMIT = 28 * 2**20
VMEM_MOST = 60 * 2**20
GELU_C = 0.7978845608028654
GELU_A = 0.044715
VEC = 8


def swap(v, axis, bit, size):
    return lax.ppermute(v, axis, [(i, i ^ bit) for i in range(size)])


def bits_of(size):
    return [1 << b for b in range(size.bit_length() - 1)]


def shape(dims, kind):
    return jax.ShapeDtypeStruct(tuple(dims), kind)


def together(*lists):
    out = lax.optimization_barrier(tuple(tuple(v) for v in lists))
    return [list(v) for v in out]


def run(name, fn, ins, outs, scratch=(), smem=(), after=(), hbm=(), limit=VMEM_LIMIT):
    n_in, n_out, n_all = len(ins), len(outs), len(ins) + len(after)

    def kernel(*refs):
        fn(refs[:n_in], refs[n_all : n_all + n_out], refs[n_all + n_out :])

    return pl.pallas_call(
        kernel,
        out_shape=tuple(outs),
        in_specs=[
            pl.BlockSpec(
                memory_space=pltpu.SMEM if i in smem else pl.ANY if i in hbm else pltpu.VMEM
            )
            for i in range(n_in)
        ]
        + [pl.BlockSpec(memory_space=pl.ANY) for _ in after],
        out_specs=tuple(pl.BlockSpec(memory_space=pltpu.VMEM) for _ in outs),
        scratch_shapes=list(scratch),
        compiler_params=pltpu.CompilerParams(vmem_limit_bytes=limit),
        cost_estimate=pl.CostEstimate(flops=1, bytes_accessed=1, transcendentals=0),
        name=name,
    )(*ins, *after)


def dot(a, b):
    return jnp.dot(a, b, preferred_element_type=F32)


def dot_nt(a, b):
    return lax.dot_general(a, b, (((1,), (1,)), ((), ())), preferred_element_type=F32)


def dot_tn(a, b):
    return lax.dot_general(a, b, (((0,), (0,)), ((), ())), preferred_element_type=F32)


def normalize(v):
    centre = v - jnp.mean(v, -1, keepdims=True)
    rstd = lax.rsqrt(jnp.mean(centre * centre, -1, keepdims=True) + 1e-05)
    return centre * rstd, rstd


def norm_back(g, normed, rstd, gain):
    e = g * gain
    return rstd * (
        e - jnp.mean(e, -1, keepdims=True) - normed * jnp.mean(e * normed, -1, keepdims=True)
    )


def rows_of(start, size):
    return pl.ds(pl.multiple_of(start * size, size), size)


def whole(pieces, x_bit):
    if len(pieces) == 1:
        return pieces[0][...]
    a, b = pieces[0][...], pieces[1][...]
    first = x_bit == 0
    return jnp.concatenate([jnp.where(first, a, b), jnp.where(first, b, a)], 0)


def take(refs, counts):
    out, at = [], 0
    for c in counts:
        out.append(refs[at : at + c])
        at += c
    assert at == len(refs)
    return out


def three_parts(v):
    high = v.astype(BF16).astype(F32)
    rest = v - high
    middle = rest.astype(BF16).astype(F32)
    return jnp.concatenate([high, middle, rest - middle, jnp.zeros_like(v)], 0).astype(BF16)


def two_parts(v):
    high = v.astype(BF16).astype(F32)
    return jnp.concatenate([high, v - high], 0).astype(BF16)


def make_body(n_dp, n_mp):
    groups = [[0, 1], list(range(2, n_mp))]
    y_peers = list(range(2, n_mp, 2))
    def body(
        tokens,
        lengths,
        order_mask,
        norm_scale_pair,
        norm_offset_pair,
        w_qkv,
        qv_bias,
        order_bias,
        w_out,
        out_bias,
        w_up,
        up_bias,
        w_down,
        cotangent,
    ):
        rows, share, width = tokens.shape
        slots = order_mask.shape[1]
        own = rows // n_mp
        count = own * slots
        lane = qv_bias.shape[1]
        per = order_bias.shape[0]
        hid = up_bias.shape[0]
        hid_rows = hid // lane
        cols = width // lane
        piece = shape((own, share, width), BF16)
        sub = width // n_dp
        factor = HD**-0.5
        o_at, s_at = 3 * width, 4 * width
        bundle_rows = 4 * width + 4 * VEC

        def mp_swap(v, bit):
            return swap(v, "mp", bit, n_mp)

        def dp_swap(v, bit):
            return swap(v, "dp", bit, n_dp)

        def send_rows(core, pairs):
            return [mp_swap(core, 1)] + spread_y(pairs)

        def pass_rows(pairs):
            half = pairs[0].shape[0] // 2
            passed = [mp_swap(v[half:], 1) for v in pairs]
            return [p for pair in zip(pairs, passed) for p in pair]

        def over_y(v):
            return [mp_swap(v, k) for k in y_peers]

        def spread_y(parts):
            return [mp_swap(v, k) for k, v in zip(y_peers, parts)]

        row_shapes = [piece] * 2 + [shape((2 * own, share, width), BF16)] * len(y_peers)

        def cut_copies(src, outs, sems):
            me = lax.axis_index("mp")
            copies = []
            for k in range(n_mp):
                dst = outs[k] if k < 2 else outs[k // 2 + 1].at[pl.ds((k % 2) * own, own)]
                here = src.at[pl.ds((me ^ k) * own, own)]
                copies.append(pltpu.make_async_copy(here, dst, sems.at[k]))
            for c in copies:
                c.start()
            return copies

        def begin(ins, outs, scratch):
            x_bit = lax.axis_index("dp") & 1
            bundle, half = outs[-2:]
            copies = cut_copies(ins[0], outs, scratch[0])
            copies.append(
                pltpu.make_async_copy(ins[1], bundle.at[pl.ds(0, o_at)], scratch[1])
            )
            copies[-1].start()
            for c in range(cols):
                bundle[o_at + c * lane : o_at + (c + 1) * lane] = ins[2][
                    :, c * lane : (c + 1) * lane
                ]
            small = jnp.concatenate(
                [
                    ins[3][...],
                    ins[4][...],
                    jnp.concatenate([ins[5][...], jnp.zeros((1, lane - per), F32)], 1),
                    jnp.zeros((VEC - 3 - hid_rows, lane), F32),
                ],
                0,
            )
            bundle[s_at:] = three_parts(small)
            for c in copies:
                c.wait()
            half[...] = bundle[rows_of(x_bit, bundle_rows // 2)]

        *token_parts, bundle, bundle_half = run(
            "begin",
            begin,
            [
                tokens,
                w_qkv.reshape(-1, lane),
                w_out,
                qv_bias,
                up_bias.reshape(hid_rows, lane),
                order_bias.reshape(1, per),
            ],
            row_shapes
            + [shape((bundle_rows, lane), BF16), shape((bundle_rows // 2, lane), BF16)],
            [pltpu.SemaphoreType.DMA((n_mp,)), pltpu.SemaphoreType.DMA(())],
            hbm=(0, 1),
            limit=VMEM_MOST,
        )

        def cut_rest(ins, outs, scratch):
            dpi = lax.axis_index("dp")
            copies = cut_copies(ins[0], outs, scratch[0])
            halves = outs[len(row_shapes) :]
            for n, (src, bit) in enumerate(zip(ins[1:], (dpi & 1, (dpi >> 1) & 1))):
                here = src.at[rows_of(bit, src.shape[0] // 2)]
                dst = halves[0].at[n] if joined else halves[n]
                copies.append(pltpu.make_async_copy(here, dst, scratch[1].at[n]))
                copies[-1].start()
            for c in copies:
                c.wait()

        joined = w_up.shape == w_down.shape
        half_shapes = [shape((v.shape[0] // 2, v.shape[1]), BF16) for v in (w_up, w_down)]
        rest = run(
            "cut_rest",
            cut_rest,
            [cotangent, w_up, w_down],
            row_shapes
            + ([shape((2,) + half_shapes[0].shape, BF16)] if joined else half_shapes),
            [pltpu.SemaphoreType.DMA((n_mp,)), pltpu.SemaphoreType.DMA((2,))],
            hbm=(0, 1, 2),
            after=[bundle_half],
        )
        cot_parts, half_parts = list(rest[: len(row_shapes)]), rest[len(row_shapes) :]

        sends, (bundle, bundle_half) = together(token_parts[1:], [bundle, bundle_half])
        token_parts = token_parts[:1] + send_rows(sends[0], sends[1:])
        bundle_core, bundle_y = mp_swap(bundle, 1), over_y(bundle_half)

        near = [w_up, w_down]
        near_core = [mp_swap(v, 1) for v in near]
        bundle_y, (bundle_core,), token_parts[:2], half_parts, cot_parts, near_core = together(
            bundle_y, [bundle_core], token_parts[:2], half_parts, cot_parts, near_core
        )
        halves_y = [over_y(v) for v in half_parts]
        bundle_x = [dp_swap(v, 1) for v in bundle_y]
        bundle_yc = [mp_swap(v, 1) for v in bundle_y]
        token_parts = token_parts[:2] + pass_rows(token_parts[2:])

        def far(first, second, first_core, second_core):
            return [
                v
                for n in range(len(y_peers))
                for v in (first[n], second[n], first_core[n], second_core[n])
            ]

        def order_row(om_ref, me, r):
            v = om_ref[pl.ds(me * own + r, 1), :].astype(F32)
            v = jnp.broadcast_to(v, (8, slots))
            at = lax.broadcasted_iota(jnp.int32, (8, slots), 1)
            step = share
            while step < slots:
                turned = jnp.where(
                    (at & step) == 0, pltpu.roll(v, slots - step, 1), pltpu.roll(v, step, 1)
                )
                v = jnp.where((me * share) & step, turned, v)
                step *= 2
            return v[:1]

        def keep_row(me, length):
            at = lax.broadcasted_iota(jnp.int32, (1, slots), 1)
            return (at ^ (me * share)) < length

        def keep_column(me, length):
            at = lax.broadcasted_iota(jnp.int32, (slots, 1), 0)
            return ((at ^ (me * share)) < length).astype(F32)

        def head_mask(pair_value, h):
            at = lax.broadcasted_iota(jnp.int32, pair_value.shape, 1)
            return jnp.where((at >= HD) == (h % 2 == 1), pair_value, jnp.zeros_like(pair_value))

        def assemble(dst, parts):
            for r in range(own):
                for k in range(n_mp):
                    dst[r * slots + k * share : r * slots + (k + 1) * share] = parts[k][r]

        def cut_slots(dst, lead, value):
            for r in range(own):
                for k in range(n_mp):
                    at = r * slots + k * share
                    to, first = (dst[k], 0) if k < 2 else (dst[k // 2 + 1], (k % 2) * 2 * own)
                    to[first + lead + r] = value[at : at + share]

        def attend(group, first, pieces):
            wide = lane * len(group)
            heads = wide // HD
            counts = [len(pieces) // len(group)] * len(group)

            def fn(ins, outs, scratch):
                me, x_bit = lax.axis_index("mp"), lax.axis_index("dp") & 1
                qkv_ref, p_ref, att_ref, weights, wo, smalls = outs[-6:]
                if first:
                    lens, om, gains, shifts = ins[n_mp : n_mp + 4]
                    x_ref, a1_ref = outs[:2]
                    assemble(x_ref, ins[:n_mp])
                    normed, _ = normalize(x_ref[...].astype(F32))
                    a1_ref[...] = (normed * gains[0:1] + shifts[0:1]).astype(BF16)
                else:
                    lens, om, a1_ref = ins[:3]
                for j, ps in enumerate(take(ins[-len(pieces) :], counts)):
                    v = whole(ps, x_bit)
                    weights[:, j * lane : (j + 1) * lane] = v[:o_at]
                    for c in range(cols):
                        wo[j * lane : (j + 1) * lane, c * lane : (c + 1) * lane] = v[
                            o_at + c * lane : o_at + (c + 1) * lane
                        ]
                    parts = v[s_at:].astype(F32)
                    smalls[j] = parts[:VEC] + parts[VEC : 2 * VEC] + parts[2 * VEC : 3 * VEC]
                a1 = a1_ref[...]
                for t in range(3):
                    y = dot(a1, weights[t * width : (t + 1) * width])
                    if t != 1:
                        i = t // 2
                        y = y + jnp.concatenate(
                            [smalls[j, i : i + 1] for j in range(len(group))], 1
                        )
                    qkv_ref[t] = y.astype(BF16)
                for r in range(own):
                    length = lens[me * own + r]
                    order = order_row(om, me, r)
                    kept = keep_row(me, length)
                    column = keep_column(me, length)
                    here = slice(r * slots, (r + 1) * slots)
                    for pair in range(heads // 2):
                        at = slice(pair * PAIR, (pair + 1) * PAIR)
                        q = qkv_ref[0, here, at] * jnp.asarray(factor, BF16)
                        key = qkv_ref[1, here, at]
                        val = qkv_ref[2, here, at]
                        acc = None
                        for h in (2 * pair, 2 * pair + 1):
                            o = 2 + hid_rows
                            ob = smalls[h // per, o : o + 1, h % per : h % per + 1]
                            row = jnp.where(kept, ob * order, -1e30)
                            s = dot_nt(head_mask(q, h), key) + row
                            e = jnp.exp(s - jnp.max(s, -1, keepdims=True))
                            p = (e * (1.0 / jnp.sum(e, -1, keepdims=True))).astype(BF16)
                            p_ref[r * heads + h] = p
                            term = dot(p, head_mask(val, h))
                            acc = term if acc is None else acc + term
                        att_ref[here, at] = (acc * column).astype(BF16)

            ins = (
                token_parts + [lengths, order_mask, norm_scale_pair, norm_offset_pair]
                if first
                else [lengths, order_mask, a1]
            )
            lead = [shape((count, width), BF16)] * 2 if first else []
            return run(
                "attend",
                fn,
                ins + pieces,
                lead
                + [
                    shape((3, count, wide), BF16),
                    shape((own * heads, slots, slots), BF16),
                    shape((count, wide), BF16),
                    shape((3 * width, wide), BF16),
                    shape((wide, width), BF16),
                    shape((len(group), VEC, lane), F32),
                ],
                smem=(n_mp if first else 0,),
            )

        x, a1, qkv0, p0, att0, wq0, wo0, small0 = attend(groups[0], True, [bundle, bundle_core])

        bundle_x, (att0,), sends = together(bundle_x, [att0], cot_parts[1:])
        cot_parts = cot_parts[:1] + send_rows(sends[0], sends[1:])
        bundle_xc = [mp_swap(v, 1) for v in bundle_x]
        qkv1, p1, att1, wq1, wo1, small1 = attend(
            groups[1], False, far(bundle_y, bundle_x, bundle_yc, bundle_xc)
        )

        def take_apart(ins, outs, _):
            for n, o in enumerate(outs):
                o[...] = ins[0][n]

        if joined:
            pairs = [run("take_apart", take_apart, [v], half_shapes, after=[att1]) for v in halves_y[0]]
            halves_y = list(zip(*pairs))
        up_y, down_y, (att1,), cot_parts[1:2] = together(*halves_y, [att1], cot_parts[1:2])
        up_x, down_z = [dp_swap(v, 1) for v in up_y], [dp_swap(v, 2) for v in down_y]
        up_yc, down_yc = ([mp_swap(v, 1) for v in vs] for vs in (up_y, down_y))

        def scatter(dst, src, block, which, dpi):
            for p in range(n_dp):
                dst[block, which, p] = src[rows_of(dpi ^ p, sub), :]

        def mlp_forward(a2, wu, wd, bias, mixed):
            up = jnp.concatenate([bias[2 + i : 3 + i] for i in range(hid_rows)], 1)
            pre = dot(a2[...], wu) + up
            square = pre * pre
            t = jnp.tanh(pre * (GELU_C + (GELU_C * GELU_A) * square))
            half = 0.5 + 0.5 * t
            hidden = (pre * half).astype(BF16)
            slope = half + (pre * (1.0 - t * t)) * (
                0.5 * GELU_C + (1.5 * GELU_C * GELU_A) * square
            )
            mixed[...] += dot(hidden, wd)
            return hidden, slope

        def mlp_backward(hidden, slope, a2t, dy, dyt, wu, wd, d_mid, gs, dst, block, bias_sum, dpi):
            d_hidden = dot_nt(dy[...], wd)
            d_pre = (slope * d_hidden).astype(BF16)
            d_mid[...] += dot_nt(d_pre, wu)
            g_down, g_up = gs.at[0], gs.at[1]
            g_down[...] = dot(dyt[...], hidden).astype(BF16)
            scatter(dst, g_down, block, 0, dpi)
            g_up[...] = dot(a2t[...], d_pre).astype(BF16)
            scatter(dst, g_up, block, 1, dpi)
            bias_sum[...] = jnp.sum(d_pre.astype(F32), 0, keepdims=True)

        def mlp_outs(n_blocks, n_arrays):
            both = shape((n_blocks // n_arrays, 2, n_dp, sub, hid), BF16)
            return [both] * n_arrays + [shape((n_blocks, 1, hid), F32)]

        full = shape((count, width), F32)
        full_bf = shape((count, width), BF16)
        turned = shape((width, count), BF16)
        g0, g1 = groups

        def mlp_near_forward(ins, outs, _):
            lead, wu_p, wd_p = take(ins, [9, len(g0), len(g0)])
            x_ref, att0_ref, att1_ref, wo0_ref, wo1_ref, smalls, gains, shifts, ob = lead
            x1, a2, a2t, mixed, hidden, slope = outs
            v = x_ref[...].astype(F32) + (
                dot(att0_ref[...], wo0_ref[...]) + dot(att1_ref[...], wo1_ref[...]) + ob[0:1]
            )
            x1[...] = v
            normed, _ = normalize(v)
            act = (normed * gains[1:2] + shifts[1:2]).astype(BF16)
            a2[...] = act
            a2t[...] = act.T
            mixed[...] = jnp.zeros_like(mixed)
            for j in range(len(g0)):
                hidden[j], slope[j] = mlp_forward(
                    a2, wu_p[j][...], wd_p[j][...], smalls.at[j], mixed
                )

        near_up, near_down = [near[0], near_core[0]], [near[1], near_core[1]]
        x1, a2, a2t, mixed, hidden, slope = run(
            "mlp_near_forward",
            mlp_near_forward,
            [x, att0, att1, wo0, wo1, small0, norm_scale_pair, norm_offset_pair, out_bias]
            + near_up
            + near_down,
            [full, full_bf, turned, full]
            + [shape((len(g0), count, hid), BF16), shape((len(g0), count, hid), F32)],
        )

        cot_parts[2:], (a2,) = together(cot_parts[2:], [a2])
        cot_parts = cot_parts[:2] + pass_rows(cot_parts[2:])

        def mlp_near_backward(ins, outs, scratch):
            dpi = lax.axis_index("dp")
            (hidden, slope, a2t), dy_p, wu_p, wd_p = take(ins, [3, n_mp, len(g0), len(g0)])
            dy, dyt, d_mid = outs[:3]
            assemble(dy, dy_p)
            dyt[...] = dy[...].T
            d_mid[...] = jnp.zeros_like(d_mid)
            for j, k in enumerate(g0):
                mlp_backward(
                    hidden[j],
                    slope[j],
                    a2t,
                    dy,
                    dyt,
                    wu_p[j][...],
                    wd_p[j][...],
                    d_mid,
                    scratch[j],
                    outs[3 + k % 2],
                    0,
                    outs[5].at[j],
                    dpi,
                )

        dy, dyt, d_mid, keep0, send0, gub0 = run(
            "mlp_near_backward",
            mlp_near_backward,
            [hidden, slope, a2t] + cot_parts + near_up + near_down,
            [full_bf, turned, full] + mlp_outs(len(g0), 2),
            [pltpu.VMEM((2, width, hid), BF16)] * len(g0),
        )

        up_yc, up_x, down_yc, down_z, (gub0,) = together(up_yc, up_x, down_yc, down_z, [gub0])
        up_xc, down_zc = ([mp_swap(v, 1) for v in vs] for vs in (up_x, down_z))
        got0 = mp_swap(send0, 1)

        up1 = far(up_y, up_x, up_yc, up_xc)
        down1 = far(down_y, down_z, down_yc, down_zc)

        def mlp_far(j, last):
            ks = g1[j::2]
            n_w = 2 * len(ks)

            def fn(ins, outs, scratch):
                dpi = lax.axis_index("dp")
                lead, wu_p, wd_p = take(ins, [10, n_w, n_w])
                x1, a2, a2t, dy, dyt, mixed_in, d_mid_in, smalls, gains, ob = lead
                (mixed, d_mid), gs = (scratch[:2], scratch[2:]) if last else (outs[:2], scratch)
                mixed[...] = mixed_in[...]
                d_mid[...] = d_mid_in[...]
                grads, bias_sums = outs[-2:]
                for n in range(len(ks)):
                    wu = whole(wu_p[2 * n : 2 * n + 2], dpi & 1)
                    wd = whole(wd_p[2 * n : 2 * n + 2], (dpi >> 1) & 1)
                    hidden, slope = mlp_forward(a2, wu, wd, smalls.at[2 * n + j], mixed)
                    mlp_backward(
                        hidden,
                        slope,
                        a2t,
                        dy,
                        dyt,
                        wu,
                        wd,
                        d_mid,
                        gs[n],
                        grads,
                        n,
                        bias_sums.at[n],
                        dpi,
                    )
                if not last:
                    return
                output, dx1, d_att, vec = outs[:4]
                v = x1[...]
                output[...] = (v + (mixed[...] + ob[1:2])).astype(BF16)
                normed, rstd = normalize(v)
                g = d_mid[...]
                dyf = dy[...].astype(F32)
                d = dyf + norm_back(g, normed, rstd, gains[1:2])
                dx1[...] = d
                low = d.astype(BF16)
                d_att[...] = low
                vec[0:1] = jnp.sum(g * normed, 0, keepdims=True)
                vec[1:2] = jnp.sum(g, 0, keepdims=True)
                vec[2:3] = jnp.sum(low.astype(F32), 0, keepdims=True)
                vec[3:4] = jnp.sum(dyf, 0, keepdims=True)

            sums = [pltpu.VMEM((count, width), F32)] * 2
            return run(
                "mlp_far",
                fn,
                [x1, a2, a2t, dy, dyt, mixed, d_mid, small1, norm_scale_pair, out_bias]
                + [v for n in range(len(ks)) for v in up1[4 * n + 2 * j : 4 * n + 2 * j + 2]]
                + [v for n in range(len(ks)) for v in down1[4 * n + 2 * j : 4 * n + 2 * j + 2]],
                ([full_bf, full, full_bf, shape((4, width), F32)] if last else [full, full])
                + mlp_outs(len(ks), 1),
                (sums if last else []) + [pltpu.VMEM((2, width, hid), BF16)] * len(ks),
            )

        mixed, d_mid, send1, gub1_odd = mlp_far(1, False)
        send1, mixed = together([send1, mixed])[0]
        got1 = mp_swap(send1, 1)
        out_rows, dx1, d_att, vec, keep1, gub1_even = mlp_far(0, True)

        def add_all(values, vectors=False):
            total = values[0].astype(F32)
            for v in values[1:]:
                total = total + v.astype(F32)
            if not vectors:
                return total.astype(BF16)
            m = total.shape[-2]
            head = total[: m - 2 * VEC]
            v = total[m - 2 * VEC : m - VEC] + total[m - VEC :]
            high = v.astype(BF16).astype(F32)
            return jnp.concatenate([head, high, v - high], 0).astype(BF16)

        n_y = len(y_peers)

        def split(places, bit):
            return [i for i, p in enumerate(places) if not p & bit], [
                i for i, p in enumerate(places) if p & bit
            ]

        def add_split(parts, places, bit, vectors=False, after=(), two=False, halves=()):
            picks = split(places, bit)
            n_parts, n_half = len(parts), len(places) // 2

            def fn(ins, outs, _):
                for pick, dsts in zip(picks, (outs[:1], outs[1:])):
                    for at, i in enumerate(pick):
                        values = [v[i] for v in ins[:n_parts]]
                        if halves:
                            values.append(ins[n_parts + i // n_half][i % n_half])
                        size = dsts[0].shape[0]
                        dsts[at // size][at % size] = add_all(values, vectors)

            n, rest = len(picks[0]), parts[0].shape[1:]
            sizes = [n] + ([n // 2] * 2 if two else [n])
            kept, *sent = run(
                "add_split",
                fn,
                list(parts) + list(halves),
                [shape((k,) + rest, BF16) for k in sizes],
                after=after,
            )
            return kept, sent if two else sent[0], [places[i] for i in picks[0]]

        def add_whole(parts, vectors=False):
            def fn(ins, outs, _):
                for i in range(outs[0].shape[0]):
                    outs[0][i] = add_all([v[i] for v in ins], vectors)

            return run("add_whole", fn, parts, [shape(parts[0].shape, BF16)])[0]

        def meet(mine, got, places, bit, vectors):
            def fn(ins, outs, _):
                for i, p in enumerate(places):
                    outs[0][i] = add_all([ins[0][i], ins[1][places.index(p ^ bit)]], vectors)

            return run("meet", fn, [mine, got], [shape(mine.shape, BF16)])[0]

        every = list(range(n_dp))
        no_x, with_x = split(every, 1)
        last_bits = [b for b in bits_of(n_dp) if b > 2]

        def add_core_mlp(ins, outs, _):
            keep0, got0, keep1, got1 = ins
            kept, sent, mine = outs[:3]
            for n in range(1 + n_y):
                a, b, i = (keep0, got0, 0) if n == 0 else (keep1, got1, n - 1)
                for dst, pick in ((kept, no_x), (sent, with_x)):
                    for at, p in enumerate(pick):
                        dst[n, at] = add_all([a[i, 0, p], b[i, 0, p]])
                up = mine if n == 0 else outs[3 + n - 1]
                for p in every:
                    up[p] = add_all([a[i, 1, p], b[i, 1, p]])

        kept_d, sent_d, mine_u, *others_u = run(
            "add_core_mlp",
            add_core_mlp,
            [keep0, got0, keep1, got1],
            [shape((1 + n_y, n_dp // 2, sub, hid), BF16)] * 2
            + [shape((n_dp, sub, hid), BF16)] * (1 + n_y),
        )
        (sent_d, d_att), others_u = together([sent_d, d_att], others_u)
        got_d = dp_swap(sent_d, 1)
        got_u = spread_y(others_u)

        vec_rows = n_dp * VEC
        chunk = 4 * sub + 2 * VEC

        def attend_back(ins, outs, scratch):
            me, dpi = lax.axis_index("mp"), lax.axis_index("dp")
            (lens, om, gains), fulls, qkvs, ps, atts, wqs, wos, vecs = take(
                ins, [3, 5, 2, 2, 2, 2, 2, 4]
            )
            x_ref, a1_ref, dx1, d_att, out_ref = fulls
            vec, gub_near, gub_even, gub_odd = vecs
            parts, grads = outs[:-4], outs[-4:]
            dqkvs, gqs = scratch[:2], scratch[2:4]
            d_in, vec_f, shared = scratch[4:]
            a1t = a1_ref[...].T
            d_att_v = d_att[...]
            d_att_t = d_att_v.T
            d_in[...] = jnp.zeros_like(d_in)
            cut_slots(parts, 0, out_ref[...])
            order_sums = {}
            for gi, group in enumerate(groups):
                wide = lane * len(group)
                heads = wide // HD
                qkv_ref, p_ref, att_ref = qkvs[gi], ps[gi], atts[gi]
                wq, wo, dqkv, gq = wqs[gi], wos[gi], dqkvs[gi], gqs[gi]
                d_o = dot_nt(d_att_v, wo[...]).astype(BF16)
                for r in range(own):
                    length = lens[me * own + r]
                    order = order_row(om, me, r)
                    kept = keep_row(me, length)
                    column = keep_column(me, length).astype(BF16)
                    here = slice(r * slots, (r + 1) * slots)
                    for pair in range(heads // 2):
                        at = slice(pair * PAIR, (pair + 1) * PAIR)
                        q = qkv_ref[0, here, at] * jnp.asarray(factor, BF16)
                        key = qkv_ref[1, here, at] * jnp.asarray(factor, BF16)
                        val = qkv_ref[2, here, at]
                        do = d_o[here, at] * column
                        dq = dk = dv = 0.0
                        for h in (2 * pair, 2 * pair + 1):
                            p_low = p_ref[r * heads + h]
                            p = p_low.astype(F32)
                            do_h = head_mask(do, h)
                            d_p = dot_nt(do_h, val)
                            inner = jnp.sum(p * d_p, -1, keepdims=True)
                            d_s = jnp.where(kept, p * (d_p - inner), 0.0).astype(BF16)
                            sums = dot(jnp.ones((8, slots), BF16), d_s)[:1] * order
                            name = (group[h // per], h % per)
                            old = order_sums.get(name)
                            order_sums[name] = sums if old is None else old + sums
                            dq = dq + dot(d_s, head_mask(key, h))
                            dk = dk + dot_tn(d_s, head_mask(q, h))
                            dv = dv + dot_tn(p_low, do_h)
                        dqkv[0, here, at] = dq.astype(BF16)
                        dqkv[1, here, at] = dk.astype(BF16)
                        dqkv[2, here, at] = dv.astype(BF16)
                total = None
                for t in range(3):
                    g = dqkv[t]
                    gq[t] = dot(a1t, g).astype(BF16)
                    term = dot_nt(g, wq[t * width : (t + 1) * width])
                    total = term if total is None else total + term
                d_in[...] += total
                gq[3] = dot(d_att_t, att_ref[...]).astype(BF16)
                for j, k in enumerate(group):
                    dst = grads[2 * gi + k % 2]
                    at = slice(j * lane, (j + 1) * lane)
                    for p in range(n_dp):
                        here = rows_of(dpi ^ p, sub)
                        for t in range(4):
                            dst[j // 2, p, t * sub : (t + 1) * sub] = gq[t, here, at]
                    vec_f[k] = jnp.zeros((vec_rows, lane), F32)
                    base = 6 * cols
                    for n, t in enumerate((0, 2)):
                        vec_f[k, base + n : base + n + 1] = jnp.sum(
                            dqkv[t, :, at].astype(F32), 0, keepdims=True
                        )
                    gub = gub_near[j] if gi == 0 else (gub_even, gub_odd)[j % 2][j // 2]
                    for i in range(hid_rows):
                        vec_f[k, base + 2 + i : base + 3 + i] = gub[:, i * lane : (i + 1) * lane]
                    lanes = lax.broadcasted_iota(jnp.int32, (1, lane), 1)
                    row = jnp.zeros((1, lane), F32)
                    for i in range(per):
                        row = row + jnp.where(
                            lanes == i, jnp.sum(order_sums[(k, i)], -1, keepdims=True), 0.0
                        )
                    vec_f[k, base + 2 + hid_rows : base + 3 + hid_rows] = row
            normed, rstd = normalize(x_ref[...].astype(F32))
            g = d_in[...]
            cut_slots(
                parts, own, (dx1[...] + norm_back(g, normed, rstd, gains[0:1])).astype(BF16)
            )
            shared[0:1] = jnp.sum(g * normed, 0, keepdims=True)
            shared[1:2] = vec[0:1]
            shared[2:3] = jnp.sum(g, 0, keepdims=True)
            shared[3:4] = vec[1:2]
            shared[4:5] = vec[2:3]
            shared[5:6] = vec[3:4]
            for gi, group in enumerate(groups):
                for j, k in enumerate(group):
                    for i in range(6):
                        for c in range(cols):
                            at = i * cols + c
                            vec_f[k, at : at + 1] = shared[i : i + 1, c * lane : (c + 1) * lane]
                    dst = grads[2 * gi + k % 2]
                    for p in range(n_dp):
                        v = vec_f[k, rows_of(dpi ^ p, VEC)]
                        dst[j // 2, p, 4 * sub :] = two_parts(v)

        def grad_shapes(n_blocks):
            return [shape((n_blocks // 2, n_dp, chunk, lane), BF16)] * 2

        back = run(
            "attend_back",
            attend_back,
            [lengths, order_mask, norm_scale_pair]
            + [x, a1, dx1, d_att, out_rows]
            + [qkv0, qkv1, p0, p1, att0, att1, wq0, wq1, wo0, wo1]
            + [vec, gub0, gub1_even, gub1_odd],
            [shape((2 * s.shape[0],) + s.shape[1:], BF16) for s in row_shapes]
            + grad_shapes(len(g0))
            + grad_shapes(len(g1)),
            [
                *[pltpu.VMEM((3, count, lane * len(g)), BF16) for g in groups],
                *[pltpu.VMEM((4, width, lane * len(g)), BF16) for g in groups],
                pltpu.VMEM((count, width), F32),
                pltpu.VMEM((n_mp, vec_rows, lane), F32),
                pltpu.VMEM((8, width), F32),
            ],
            smem=(0,),
        )
        row_parts, (ka0, sa0, ka1, sa1) = back[:-4], back[-4:]

        def add_x(ins, outs, _):
            for n in range(1 + n_y):
                for i in range(n_dp // 2):
                    outs[n][i] = add_all([ins[0][n, i], ins[1][n, i]])

        mine_d, *others_d = run(
            "add_x", add_x, [kept_d, got_d], [shape((n_dp // 2, sub, hid), BF16)] * (1 + n_y)
        )
        kept_u, sent_u, at_u = add_split([mine_u] + got_u, every, 2)
        others_d, (sent_u,), sends = together(others_d, [sent_u], [sa0, sa1])
        got_d = spread_y(others_d)
        got_u = dp_swap(sent_u, 2)
        ga0, ga1 = (mp_swap(v, 1) for v in sends)

        def add_core_att(ins, outs, _):
            keep0, got0, keep1, got1 = ins
            for n in range(1 + n_y):
                a, b, i = (keep0, got0, 0) if n == 0 else (keep1, got1, n - 1)
                for p in every:
                    outs[n][p] = add_all([a[i, p], b[i, p]], True)

        mine_a, *others_a = run(
            "add_core_att",
            add_core_att,
            [ka0, ga0, ka1, ga1],
            [shape((n_dp, chunk, lane), BF16)] * (1 + n_y),
        )
        kept_d, sent_d, at_d = add_split([mine_d] + got_d, no_x, 2)
        kept_u, sent_u, at_u = add_split([kept_u, got_u], at_u, 1)
        (sent_d, sent_u), others_a = together([sent_d, sent_u], others_a)
        got_d, got_u, got_a = dp_swap(sent_d, 2), dp_swap(sent_u, 1), spread_y(others_a)

        def join(ins, outs, _):
            for n, mine in enumerate((ins[:2], ins[2:])):
                for i in range(outs[0].shape[0]):
                    outs[0][i, n] = add_all([v[i] for v in mine])

        (both,) = run(
            "join",
            join,
            [kept_d, got_d, kept_u, got_u],
            [shape((len(at_d), 2, sub, hid), BF16)],
        )
        at_both = at_d
        for bit in last_bits[:-1]:
            kept, sent, at_both = add_split([both], at_both, bit)
            both = add_whole([kept, dp_swap(sent, bit)])
        got = dp_swap(both, last_bits[-1])
        kept_a, sent_a, at_a = add_split([mine_a] + got_a, every, 1, True, two=True)
        got_a = [dp_swap(v, 1) for v in sent_a]
        both = meet(both, got, at_both, last_bits[-1], False)
        for bit in reversed(last_bits[:-1]):
            both, at_both = jnp.concatenate([both, dp_swap(both, bit)]), at_both + [
                p ^ bit for p in at_both
            ]

        def part(ins, outs, _):
            for n, o in enumerate(outs):
                for i in range(len(at_both)):
                    o[i] = ins[0][i, n]

        down, up = run("part", part, [both], [shape((len(at_both), sub, hid), BF16)] * 2)
        kept_a, sent_a, at_a = add_split([kept_a], at_a, 2, True, [down], halves=got_a)

        row_parts = list(row_parts)
        row_parts[1:] = send_rows(row_parts[1], row_parts[2:])
        down, up, sent_a = together([down, up, sent_a])[0]
        got_d, got_u, got_a = dp_swap(down, 2), dp_swap(up, 1), dp_swap(sent_a, 2)
        down, at_down = jnp.concatenate([down, got_d]), at_both + [p ^ 2 for p in at_both]
        up, at_up = jnp.concatenate([up, got_u]), at_both + [p ^ 1 for p in at_both]
        if len(last_bits) > 1:
            kept_a, sent_a, at_a = add_split([kept_a, got_a], at_a, last_bits[0], True)
        else:
            kept_a = sent_a = add_whole([kept_a, got_a], True)
        got_d, got_u, got_a = dp_swap(down, 1), dp_swap(up, 2), dp_swap(sent_a, last_bits[0])
        for bit in last_bits[1:]:
            if bit != last_bits[-1]:
                kept_a, sent_a, at_a = add_split([kept_a, got_a], at_a, bit, True)
            else:
                kept_a = sent_a = add_whole([kept_a, got_a], True)
            got_a = dp_swap(sent_a, bit)
        att = meet(kept_a, got_a, at_a, last_bits[-1], True)
        for bit in [*reversed(last_bits[:-1]), 2]:
            if bit == 2:
                (att, got_d, got_u), row_parts = together([att, got_d, got_u], row_parts)
                row_parts = row_parts[:2] + pass_rows(row_parts[2:])
            att = jnp.concatenate([att, dp_swap(att, bit)])
            at_a = at_a + [p ^ bit for p in at_a]
        got_a = dp_swap(att, 1)

        def finish_mlp(ins, outs, scratch):
            dpi = lax.axis_index("dp")
            for n, p in enumerate(at_down):
                for v, at in zip(ins[:2], (p, p ^ 1)):
                    scratch[0][rows_of(dpi ^ at, sub)] = v[n].astype(F32)
            for n, p in enumerate(at_up):
                for v, at in zip(ins[2:], (p, p ^ 2)):
                    outs[1][rows_of(dpi ^ at, sub)] = v[n].astype(F32)
            outs[0][...] = scratch[0][...].T
            outs[2][...] = jnp.zeros((8, LANES), F32)

        mark = shape((8, LANES), F32)
        r_down, r_up, mlp_mark = run(
            "finish_mlp",
            finish_mlp,
            [down, got_d, up, got_u],
            [shape((hid, width), F32), shape((width, hid), F32), mark],
            [pltpu.VMEM((width, hid), F32)],
        )

        def finish_att(ins, outs, scratch):
            r_qkv, r_out, gain, shift, outb, qvb, upb, order = outs
            turned_out, vec_f = scratch
            dpi = lax.axis_index("dp")
            for src, n, p in [(0, n, p) for n, p in enumerate(at_a)] + [
                (1, n, p ^ 1) for n, p in enumerate(at_a)
            ]:
                v = ins[src][n]
                at = dpi ^ p
                here = rows_of(at, sub)
                for t in range(3):
                    r_qkv[t, here] = v[t * sub : (t + 1) * sub].astype(F32)
                turned_out[here] = v[3 * sub : 4 * sub].astype(F32)
                pairs = v[4 * sub :].astype(F32)
                vec_f[rows_of(at, VEC)] = pairs[:VEC] + pairs[VEC:]
            r_out[...] = turned_out[...].T
            for i in range(6):
                dst = (gain, shift, outb)[i // 2]
                dst[i % 2 : i % 2 + 1] = jnp.concatenate(
                    [vec_f[i * cols + c : i * cols + c + 1] for c in range(cols)], 1
                )
            base = 6 * cols
            qvb[...] = vec_f[base : base + 2]
            upb[...] = jnp.concatenate(
                [vec_f[base + 2 + i : base + 3 + i] for i in range(hid_rows)], 1
            )
            order[...] = vec_f[base + 2 + hid_rows : base + 3 + hid_rows, :per]

        pair_shape = shape((2, width), F32)
        def gather_rows(ins, outs, _):
            me = lax.axis_index("mp")
            for k in range(n_mp):
                here = pl.ds((me ^ k) * own, own)
                outs[0][here] = ins[k][:own]
                outs[1][here] = ins[k][own : 2 * own].astype(F32)
            outs[2][...] = jnp.zeros((8, LANES), F32)

        output, token_gradient, rows_mark = run(
            "gather_rows",
            gather_rows,
            row_parts,
            [shape((rows, share, width), BF16), shape((rows, share, width), F32), mark],
        )
        r_qkv, r_out, gain, shift, outb, qvb, upb, order = run(
            "finish_att",
            finish_att,
            [att, got_a],
            [
                shape((3, width, lane), F32),
                shape((lane, width), F32),
                pair_shape,
                pair_shape,
                pair_shape,
                shape((2, lane), F32),
                shape((1, hid), F32),
                shape((1, per), F32),
            ],
            [pltpu.VMEM((width, lane), F32), pltpu.VMEM((vec_rows, lane), F32)],
            after=[mlp_mark, rows_mark],
        )

        return (
            output,
            token_gradient,
            gain,
            shift,
            r_qkv,
            qvb,
            order.reshape(per),
            r_out,
            outb,
            r_up,
            upb.reshape(hid),
            r_down,
        )

    return body


def solution(mesh):
    return jax.shard_map(
        make_body(mesh.shape["dp"], mesh.shape["mp"]),
        mesh=mesh,
        in_specs=(
            P("dp", "mp", None),
            P("dp"),
            P("dp", None),
            P(),
            P(),
            P(None, None, "mp"),
            P(None, "mp"),
            P("mp"),
            P("mp", None),
            P(),
            P(None, "mp"),
            P("mp"),
            P("mp", None),
            P("dp", "mp", None),
        ),
        out_specs=(
            P("dp", "mp", None),
            P("dp", "mp", None),
            P(),
            P(),
            P(None, None, "mp"),
            P(None, "mp"),
            P("mp"),
            P("mp", None),
            P(),
            P(None, "mp"),
            P("mp"),
            P("mp", None),
        ),
        check_vma=False,
    )
```

```python
import jax
import jax.numpy as jnp
from jax import lax
from jax.experimental import pallas as pl
from jax.experimental.pallas import tpu as pltpu
from jax.sharding import PartitionSpec as P

HD = 64
PAIR = 2 * HD
LANES = 128
F32 = jnp.float32
BF16 = jnp.bfloat16
VMEM_LIMIT = 28 * 2**20
VMEM_MOST = 60 * 2**20
GELU_C = 0.7978845608028654
GELU_A = 0.044715
VEC = 8


def swap(v, axis, bit, size):
    return lax.ppermute(v, axis, [(i, i ^ bit) for i in range(size)])


def bits_of(size):
    return [1 << b for b in range(size.bit_length() - 1)]


def shape(dims, kind):
    return jax.ShapeDtypeStruct(tuple(dims), kind)


def together(*lists):
    out = lax.optimization_barrier(tuple(tuple(v) for v in lists))
    return [list(v) for v in out]


def run(name, fn, ins, outs, scratch=(), smem=(), after=(), hbm=(), limit=VMEM_LIMIT):
    n_in, n_out, n_all = len(ins), len(outs), len(ins) + len(after)

    def kernel(*refs):
        fn(refs[:n_in], refs[n_all : n_all + n_out], refs[n_all + n_out :])

    return pl.pallas_call(
        kernel,
        out_shape=tuple(outs),
        in_specs=[
            pl.BlockSpec(
                memory_space=pltpu.SMEM if i in smem else pl.ANY if i in hbm else pltpu.VMEM
            )
            for i in range(n_in)
        ]
        + [pl.BlockSpec(memory_space=pl.ANY) for _ in after],
        out_specs=tuple(pl.BlockSpec(memory_space=pltpu.VMEM) for _ in outs),
        scratch_shapes=list(scratch),
        compiler_params=pltpu.CompilerParams(vmem_limit_bytes=limit),
        cost_estimate=pl.CostEstimate(flops=1, bytes_accessed=1, transcendentals=0),
        name=name,
    )(*ins, *after)


def dot(a, b):
    return jnp.dot(a, b, preferred_element_type=F32)


def dot_nt(a, b):
    return lax.dot_general(a, b, (((1,), (1,)), ((), ())), preferred_element_type=F32)


def dot_tn(a, b):
    return lax.dot_general(a, b, (((0,), (0,)), ((), ())), preferred_element_type=F32)


def normalize(v):
    centre = v - jnp.mean(v, -1, keepdims=True)
    rstd = lax.rsqrt(jnp.mean(centre * centre, -1, keepdims=True) + 1e-05)
    return centre * rstd, rstd


def norm_back(g, normed, rstd, gain):
    e = g * gain
    return rstd * (
        e - jnp.mean(e, -1, keepdims=True) - normed * jnp.mean(e * normed, -1, keepdims=True)
    )


def rows_of(start, size):
    return pl.ds(pl.multiple_of(start * size, size), size)


def whole(pieces, x_bit):
    if len(pieces) == 1:
        return pieces[0][...]
    a, b = pieces[0][...], pieces[1][...]
    first = x_bit == 0
    return jnp.concatenate([jnp.where(first, a, b), jnp.where(first, b, a)], 0)


def take(refs, counts):
    out, at = [], 0
    for c in counts:
        out.append(refs[at : at + c])
        at += c
    assert at == len(refs)
    return out


def three_parts(v):
    high = v.astype(BF16).astype(F32)
    rest = v - high
    middle = rest.astype(BF16).astype(F32)
    return jnp.concatenate([high, middle, rest - middle, jnp.zeros_like(v)], 0).astype(BF16)


def two_parts(v):
    high = v.astype(BF16).astype(F32)
    return jnp.concatenate([high, v - high], 0).astype(BF16)


def make_body(n_dp, n_mp):
    groups = [[0, 1], list(range(2, n_mp))]
    y_peers = list(range(2, n_mp, 2))
    def body(
        tokens,
        lengths,
        order_mask,
        norm_scale_pair,
        norm_offset_pair,
        w_qkv,
        qv_bias,
        order_bias,
        w_out,
        out_bias,
        w_up,
        up_bias,
        w_down,
        cotangent,
    ):
        rows, share, width = tokens.shape
        slots = order_mask.shape[1]
        own = rows // n_mp
        count = own * slots
        lane = qv_bias.shape[1]
        per = order_bias.shape[0]
        hid = up_bias.shape[0]
        hid_rows = hid // lane
        cols = width // lane
        piece = shape((own, share, width), BF16)
        sub = width // n_dp
        factor = HD**-0.5
        o_at, s_at = 3 * width, 4 * width
        bundle_rows = 4 * width + 4 * VEC

        def mp_swap(v, bit):
            return swap(v, "mp", bit, n_mp)

        def dp_swap(v, bit):
            return swap(v, "dp", bit, n_dp)

        def send_rows(core, pairs):
            return [mp_swap(core, 1)] + spread_y(pairs)

        def pass_rows(pairs):
            half = pairs[0].shape[0] // 2
            passed = [mp_swap(v[half:], 1) for v in pairs]
            return [p for pair in zip(pairs, passed) for p in pair]

        def over_y(v):
            return [mp_swap(v, k) for k in y_peers]

        def spread_y(parts):
            return [mp_swap(v, k) for k, v in zip(y_peers, parts)]

        row_shapes = [piece] * 2 + [shape((2 * own, share, width), BF16)] * len(y_peers)

        def cut_copies(src, outs, sems):
            me = lax.axis_index("mp")
            copies = []
            for k in range(n_mp):
                dst = outs[k] if k < 2 else outs[k // 2 + 1].at[pl.ds((k % 2) * own, own)]
                here = src.at[pl.ds((me ^ k) * own, own)]
                copies.append(pltpu.make_async_copy(here, dst, sems.at[k]))
            for c in copies:
                c.start()
            return copies

        def begin(ins, outs, scratch):
            x_bit = lax.axis_index("dp") & 1
            bundle, half = outs[-2:]
            copies = cut_copies(ins[0], outs, scratch[0])
            copies.append(
                pltpu.make_async_copy(ins[1], bundle.at[pl.ds(0, o_at)], scratch[1])
            )
            copies[-1].start()
            for c in range(cols):
                bundle[o_at + c * lane : o_at + (c + 1) * lane] = ins[2][
                    :, c * lane : (c + 1) * lane
                ]
            small = jnp.concatenate(
                [
                    ins[3][...],
                    ins[4][...],
                    jnp.concatenate([ins[5][...], jnp.zeros((1, lane - per), F32)], 1),
                    jnp.zeros((VEC - 3 - hid_rows, lane), F32),
                ],
                0,
            )
            bundle[s_at:] = three_parts(small)
            for c in copies:
                c.wait()
            half[...] = bundle[rows_of(x_bit, bundle_rows // 2)]

        *token_parts, bundle, bundle_half = run(
            "begin",
            begin,
            [
                tokens,
                w_qkv.reshape(-1, lane),
                w_out,
                qv_bias,
                up_bias.reshape(hid_rows, lane),
                order_bias.reshape(1, per),
            ],
            row_shapes
            + [shape((bundle_rows, lane), BF16), shape((bundle_rows // 2, lane), BF16)],
            [pltpu.SemaphoreType.DMA((n_mp,)), pltpu.SemaphoreType.DMA(())],
            hbm=(0, 1),
            limit=VMEM_MOST,
        )

        def cut_rest(ins, outs, scratch):
            dpi = lax.axis_index("dp")
            copies = cut_copies(ins[0], outs, scratch[0])
            halves = outs[len(row_shapes) :]
            for n, (src, bit) in enumerate(zip(ins[1:], (dpi & 1, (dpi >> 1) & 1))):
                here = src.at[rows_of(bit, src.shape[0] // 2)]
                dst = halves[0].at[n] if joined else halves[n]
                copies.append(pltpu.make_async_copy(here, dst, scratch[1].at[n]))
                copies[-1].start()
            for c in copies:
                c.wait()

        joined = w_up.shape == w_down.shape
        half_shapes = [shape((v.shape[0] // 2, v.shape[1]), BF16) for v in (w_up, w_down)]
        rest = run(
            "cut_rest",
            cut_rest,
            [cotangent, w_up, w_down],
            row_shapes
            + ([shape((2,) + half_shapes[0].shape, BF16)] if joined else half_shapes),
            [pltpu.SemaphoreType.DMA((n_mp,)), pltpu.SemaphoreType.DMA((2,))],
            hbm=(0, 1, 2),
            after=[bundle_half],
        )
        cot_parts, half_parts = list(rest[: len(row_shapes)]), rest[len(row_shapes) :]

        sends, (bundle, bundle_half) = together(token_parts[1:], [bundle, bundle_half])
        token_parts = token_parts[:1] + send_rows(sends[0], sends[1:])
        bundle_core, bundle_y = mp_swap(bundle, 1), over_y(bundle_half)

        near = [w_up, w_down]
        near_core = [mp_swap(v, 1) for v in near]
        bundle_y, (bundle_core,), token_parts[:2], half_parts, cot_parts, near_core = together(
            bundle_y, [bundle_core], token_parts[:2], half_parts, cot_parts, near_core
        )
        halves_y = [over_y(v) for v in half_parts]
        bundle_x = [dp_swap(v, 1) for v in bundle_y]
        bundle_yc = [mp_swap(v, 1) for v in bundle_y]
        token_parts = token_parts[:2] + pass_rows(token_parts[2:])

        def far(first, second, first_core, second_core):
            return [
                v
                for n in range(len(y_peers))
                for v in (first[n], second[n], first_core[n], second_core[n])
            ]

        def order_row(om_ref, me, r):
            v = om_ref[pl.ds(me * own + r, 1), :].astype(F32)
            v = jnp.broadcast_to(v, (8, slots))
            at = lax.broadcasted_iota(jnp.int32, (8, slots), 1)
            step = share
            while step < slots:
                turned = jnp.where(
                    (at & step) == 0, pltpu.roll(v, slots - step, 1), pltpu.roll(v, step, 1)
                )
                v = jnp.where((me * share) & step, turned, v)
                step *= 2
            return v[:1]

        def keep_row(me, length):
            at = lax.broadcasted_iota(jnp.int32, (1, slots), 1)
            return (at ^ (me * share)) < length

        def keep_column(me, length):
            at = lax.broadcasted_iota(jnp.int32, (slots, 1), 0)
            return ((at ^ (me * share)) < length).astype(F32)

        def head_mask(pair_value, h):
            at = lax.broadcasted_iota(jnp.int32, pair_value.shape, 1)
            return jnp.where((at >= HD) == (h % 2 == 1), pair_value, jnp.zeros_like(pair_value))

        def assemble(dst, parts):
            for r in range(own):
                for k in range(n_mp):
                    dst[r * slots + k * share : r * slots + (k + 1) * share] = parts[k][r]

        def cut_slots(dst, lead, value):
            for r in range(own):
                for k in range(n_mp):
                    at = r * slots + k * share
                    to, first = (dst[k], 0) if k < 2 else (dst[k // 2 + 1], (k % 2) * 2 * own)
                    to[first + lead + r] = value[at : at + share]

        def attend(group, first, pieces):
            wide = lane * len(group)
            heads = wide // HD
            counts = [len(pieces) // len(group)] * len(group)

            def fn(ins, outs, scratch):
                me, x_bit = lax.axis_index("mp"), lax.axis_index("dp") & 1
                qkv_ref, p_ref, att_ref, weights, wo, smalls = outs[-6:]
                if first:
                    lens, om, gains, shifts = ins[n_mp : n_mp + 4]
                    x_ref, a1_ref = outs[:2]
                    assemble(x_ref, ins[:n_mp])
                    normed, _ = normalize(x_ref[...].astype(F32))
                    a1_ref[...] = (normed * gains[0:1] + shifts[0:1]).astype(BF16)
                else:
                    lens, om, a1_ref = ins[:3]
                for j, ps in enumerate(take(ins[-len(pieces) :], counts)):
                    v = whole(ps, x_bit)
                    weights[:, j * lane : (j + 1) * lane] = v[:o_at]
                    for c in range(cols):
                        wo[j * lane : (j + 1) * lane, c * lane : (c + 1) * lane] = v[
                            o_at + c * lane : o_at + (c + 1) * lane
                        ]
                    parts = v[s_at:].astype(F32)
                    smalls[j] = parts[:VEC] + parts[VEC : 2 * VEC] + parts[2 * VEC : 3 * VEC]
                a1 = a1_ref[...]
                for t in range(3):
                    y = dot(a1, weights[t * width : (t + 1) * width])
                    if t != 1:
                        i = t // 2
                        y = y + jnp.concatenate(
                            [smalls[j, i : i + 1] for j in range(len(group))], 1
                        )
                    qkv_ref[t] = y.astype(BF16)
                for r in range(own):
                    length = lens[me * own + r]
                    order = order_row(om, me, r)
                    kept = keep_row(me, length)
                    column = keep_column(me, length)
                    here = slice(r * slots, (r + 1) * slots)
                    for pair in range(heads // 2):
                        at = slice(pair * PAIR, (pair + 1) * PAIR)
                        q = qkv_ref[0, here, at] * jnp.asarray(factor, BF16)
                        key = qkv_ref[1, here, at]
                        val = qkv_ref[2, here, at]
                        acc = None
                        for h in (2 * pair, 2 * pair + 1):
                            o = 2 + hid_rows
                            ob = smalls[h // per, o : o + 1, h % per : h % per + 1]
                            row = jnp.where(kept, ob * order, -1e30)
                            s = dot_nt(head_mask(q, h), key) + row
                            e = jnp.exp(s - jnp.max(s, -1, keepdims=True))
                            p = (e * (1.0 / jnp.sum(e, -1, keepdims=True))).astype(BF16)
                            p_ref[r * heads + h] = p
                            term = dot(p, head_mask(val, h))
                            acc = term if acc is None else acc + term
                        att_ref[here, at] = (acc * column).astype(BF16)

            ins = (
                token_parts + [lengths, order_mask, norm_scale_pair, norm_offset_pair]
                if first
                else [lengths, order_mask, a1]
            )
            lead = [shape((count, width), BF16)] * 2 if first else []
            return run(
                "attend",
                fn,
                ins + pieces,
                lead
                + [
                    shape((3, count, wide), BF16),
                    shape((own * heads, slots, slots), BF16),
                    shape((count, wide), BF16),
                    shape((3 * width, wide), BF16),
                    shape((wide, width), BF16),
                    shape((len(group), VEC, lane), F32),
                ],
                smem=(n_mp if first else 0,),
            )

        x, a1, qkv0, p0, att0, wq0, wo0, small0 = attend(groups[0], True, [bundle, bundle_core])

        bundle_x, (att0,), sends = together(bundle_x, [att0], cot_parts[1:])
        cot_parts = cot_parts[:1] + send_rows(sends[0], sends[1:])
        bundle_xc = [mp_swap(v, 1) for v in bundle_x]
        qkv1, p1, att1, wq1, wo1, small1 = attend(
            groups[1], False, far(bundle_y, bundle_x, bundle_yc, bundle_xc)
        )

        def take_apart(ins, outs, _):
            for n, o in enumerate(outs):
                o[...] = ins[0][n]

        if joined:
            pairs = [run("take_apart", take_apart, [v], half_shapes, after=[att1]) for v in halves_y[0]]
            halves_y = list(zip(*pairs))
        up_y, down_y, (att1,), cot_parts[1:2] = together(*halves_y, [att1], cot_parts[1:2])
        up_x, down_z = [dp_swap(v, 1) for v in up_y], [dp_swap(v, 2) for v in down_y]
        up_yc, down_yc = ([mp_swap(v, 1) for v in vs] for vs in (up_y, down_y))

        def scatter(dst, src, block, which, dpi):
            for p in range(n_dp):
                dst[block, which, p] = src[rows_of(dpi ^ p, sub), :]

        def mlp_forward(a2, wu, wd, bias, mixed):
            up = jnp.concatenate([bias[2 + i : 3 + i] for i in range(hid_rows)], 1)
            pre = dot(a2[...], wu) + up
            square = pre * pre
            t = jnp.tanh(pre * (GELU_C + (GELU_C * GELU_A) * square))
            half = 0.5 + 0.5 * t
            hidden = (pre * half).astype(BF16)
            slope = half + (pre * (1.0 - t * t)) * (
                0.5 * GELU_C + (1.5 * GELU_C * GELU_A) * square
            )
            mixed[...] += dot(hidden, wd)
            return hidden, slope

        def mlp_backward(hidden, slope, a2t, dy, dyt, wu, wd, d_mid, gs, dst, block, bias_sum, dpi):
            d_hidden = dot_nt(dy[...], wd)
            d_pre = (slope * d_hidden).astype(BF16)
            d_mid[...] += dot_nt(d_pre, wu)
            g_down, g_up = gs.at[0], gs.at[1]
            g_down[...] = dot(dyt[...], hidden).astype(BF16)
            scatter(dst, g_down, block, 0, dpi)
            g_up[...] = dot(a2t[...], d_pre).astype(BF16)
            scatter(dst, g_up, block, 1, dpi)
            bias_sum[...] = jnp.sum(d_pre.astype(F32), 0, keepdims=True)

        def mlp_outs(n_blocks, n_arrays):
            both = shape((n_blocks // n_arrays, 2, n_dp, sub, hid), BF16)
            return [both] * n_arrays + [shape((n_blocks, 1, hid), F32)]

        full = shape((count, width), F32)
        full_bf = shape((count, width), BF16)
        turned = shape((width, count), BF16)
        g0, g1 = groups

        def mlp_near_forward(ins, outs, _):
            lead, wu_p, wd_p = take(ins, [9, len(g0), len(g0)])
            x_ref, att0_ref, att1_ref, wo0_ref, wo1_ref, smalls, gains, shifts, ob = lead
            x1, a2, a2t, mixed, hidden, slope = outs
            v = x_ref[...].astype(F32) + (
                dot(att0_ref[...], wo0_ref[...]) + dot(att1_ref[...], wo1_ref[...]) + ob[0:1]
            )
            x1[...] = v
            normed, _ = normalize(v)
            act = (normed * gains[1:2] + shifts[1:2]).astype(BF16)
            a2[...] = act
            a2t[...] = act.T
            mixed[...] = jnp.zeros_like(mixed)
            for j in range(len(g0)):
                hidden[j], slope[j] = mlp_forward(
                    a2, wu_p[j][...], wd_p[j][...], smalls.at[j], mixed
                )

        near_up, near_down = [near[0], near_core[0]], [near[1], near_core[1]]
        x1, a2, a2t, mixed, hidden, slope = run(
            "mlp_near_forward",
            mlp_near_forward,
            [x, att0, att1, wo0, wo1, small0, norm_scale_pair, norm_offset_pair, out_bias]
            + near_up
            + near_down,
            [full, full_bf, turned, full]
            + [shape((len(g0), count, hid), BF16), shape((len(g0), count, hid), F32)],
        )

        cot_parts[2:], (a2,) = together(cot_parts[2:], [a2])
        cot_parts = cot_parts[:2] + pass_rows(cot_parts[2:])

        def mlp_near_backward(ins, outs, scratch):
            dpi = lax.axis_index("dp")
            (hidden, slope, a2t), dy_p, wu_p, wd_p = take(ins, [3, n_mp, len(g0), len(g0)])
            dy, dyt, d_mid = outs[:3]
            assemble(dy, dy_p)
            dyt[...] = dy[...].T
            d_mid[...] = jnp.zeros_like(d_mid)
            for j, k in enumerate(g0):
                mlp_backward(
                    hidden[j],
                    slope[j],
                    a2t,
                    dy,
                    dyt,
                    wu_p[j][...],
                    wd_p[j][...],
                    d_mid,
                    scratch[j],
                    outs[3 + k % 2],
                    0,
                    outs[5].at[j],
                    dpi,
                )

        dy, dyt, d_mid, keep0, send0, gub0 = run(
            "mlp_near_backward",
            mlp_near_backward,
            [hidden, slope, a2t] + cot_parts + near_up + near_down,
            [full_bf, turned, full] + mlp_outs(len(g0), 2),
            [pltpu.VMEM((2, width, hid), BF16)] * len(g0),
        )

        up_yc, up_x, down_yc, down_z, (gub0,) = together(up_yc, up_x, down_yc, down_z, [gub0])
        up_xc, down_zc = ([mp_swap(v, 1) for v in vs] for vs in (up_x, down_z))
        got0 = mp_swap(send0, 1)

        up1 = far(up_y, up_x, up_yc, up_xc)
        down1 = far(down_y, down_z, down_yc, down_zc)

        def mlp_far(j, last):
            ks = g1[j::2]
            n_w = 2 * len(ks)

            def fn(ins, outs, scratch):
                dpi = lax.axis_index("dp")
                lead, wu_p, wd_p = take(ins, [10, n_w, n_w])
                x1, a2, a2t, dy, dyt, mixed_in, d_mid_in, smalls, gains, ob = lead
                (mixed, d_mid), gs = (scratch[:2], scratch[2:]) if last else (outs[:2], scratch)
                mixed[...] = mixed_in[...]
                d_mid[...] = d_mid_in[...]
                grads, bias_sums = outs[-2:]
                for n in range(len(ks)):
                    wu = whole(wu_p[2 * n : 2 * n + 2], dpi & 1)
                    wd = whole(wd_p[2 * n : 2 * n + 2], (dpi >> 1) & 1)
                    hidden, slope = mlp_forward(a2, wu, wd, smalls.at[2 * n + j], mixed)
                    mlp_backward(
                        hidden,
                        slope,
                        a2t,
                        dy,
                        dyt,
                        wu,
                        wd,
                        d_mid,
                        gs[n],
                        grads,
                        n,
                        bias_sums.at[n],
                        dpi,
                    )
                if not last:
                    return
                output, dx1, d_att, vec = outs[:4]
                v = x1[...]
                output[...] = (v + (mixed[...] + ob[1:2])).astype(BF16)
                normed, rstd = normalize(v)
                g = d_mid[...]
                dyf = dy[...].astype(F32)
                d = dyf + norm_back(g, normed, rstd, gains[1:2])
                dx1[...] = d
                low = d.astype(BF16)
                d_att[...] = low
                vec[0:1] = jnp.sum(g * normed, 0, keepdims=True)
                vec[1:2] = jnp.sum(g, 0, keepdims=True)
                vec[2:3] = jnp.sum(low.astype(F32), 0, keepdims=True)
                vec[3:4] = jnp.sum(dyf, 0, keepdims=True)

            sums = [pltpu.VMEM((count, width), F32)] * 2
            return run(
                "mlp_far",
                fn,
                [x1, a2, a2t, dy, dyt, mixed, d_mid, small1, norm_scale_pair, out_bias]
                + [v for n in range(len(ks)) for v in up1[4 * n + 2 * j : 4 * n + 2 * j + 2]]
                + [v for n in range(len(ks)) for v in down1[4 * n + 2 * j : 4 * n + 2 * j + 2]],
                ([full_bf, full, full_bf, shape((4, width), F32)] if last else [full, full])
                + mlp_outs(len(ks), 1),
                (sums if last else []) + [pltpu.VMEM((2, width, hid), BF16)] * len(ks),
            )

        mixed, d_mid, send1, gub1_odd = mlp_far(1, False)
        send1, mixed = together([send1, mixed])[0]
        got1 = mp_swap(send1, 1)
        out_rows, dx1, d_att, vec, keep1, gub1_even = mlp_far(0, True)

        def add_all(values, vectors=False):
            total = values[0].astype(F32)
            for v in values[1:]:
                total = total + v.astype(F32)
            if not vectors:
                return total.astype(BF16)
            m = total.shape[-2]
            head = total[: m - 2 * VEC]
            v = total[m - 2 * VEC : m - VEC] + total[m - VEC :]
            high = v.astype(BF16).astype(F32)
            return jnp.concatenate([head, high, v - high], 0).astype(BF16)

        n_y = len(y_peers)

        def split(places, bit):
            return [i for i, p in enumerate(places) if not p & bit], [
                i for i, p in enumerate(places) if p & bit
            ]

        def add_split(parts, places, bit, vectors=False, after=(), two=False, halves=()):
            picks = split(places, bit)
            n_parts, n_half = len(parts), len(places) // 2

            def fn(ins, outs, _):
                for pick, dsts in zip(picks, (outs[:1], outs[1:])):
                    for at, i in enumerate(pick):
                        values = [v[i] for v in ins[:n_parts]]
                        if halves:
                            values.append(ins[n_parts + i // n_half][i % n_half])
                        size = dsts[0].shape[0]
                        dsts[at // size][at % size] = add_all(values, vectors)

            n, rest = len(picks[0]), parts[0].shape[1:]
            sizes = [n] + ([n // 2] * 2 if two else [n])
            kept, *sent = run(
                "add_split",
                fn,
                list(parts) + list(halves),
                [shape((k,) + rest, BF16) for k in sizes],
                after=after,
            )
            return kept, sent if two else sent[0], [places[i] for i in picks[0]]

        def add_parts(parts, picks, after=()):
            counts = [len(p) for p in parts]

            def fn(ins, outs, _):
                for dst, pick in zip(outs, picks):
                    for at, i in enumerate(pick):
                        values = []
                        for refs in take(ins, counts):
                            n = refs[0].shape[0]
                            values.append(refs[i // n][i % n])
                        dst[at] = add_all(values, True)

            flat_parts = [v for p in parts for v in p]
            rest = flat_parts[0].shape[1:]
            outs = [shape((len(p),) + rest, BF16) for p in picks]
            return run("add_parts", fn, flat_parts, outs, after=after)

        def add_whole(parts, vectors=False):
            def fn(ins, outs, _):
                for i in range(outs[0].shape[0]):
                    outs[0][i] = add_all([v[i] for v in ins], vectors)

            return run("add_whole", fn, parts, [shape(parts[0].shape, BF16)])[0]

        def meet(mine, got, places, bit, vectors):
            def fn(ins, outs, _):
                for i, p in enumerate(places):
                    outs[0][i] = add_all([ins[0][i], ins[1][places.index(p ^ bit)]], vectors)

            return run("meet", fn, [mine, got], [shape(mine.shape, BF16)])[0]

        every = list(range(n_dp))
        no_x, with_x = split(every, 1)
        last_bits = [b for b in bits_of(n_dp) if b > 2]

        def add_core_mlp(ins, outs, _):
            keep0, got0, keep1, got1 = ins
            kept, sent, mine = outs[:3]
            for n in range(1 + n_y):
                a, b, i = (keep0, got0, 0) if n == 0 else (keep1, got1, n - 1)
                for dst, pick in ((kept, no_x), (sent, with_x)):
                    for at, p in enumerate(pick):
                        dst[n, at] = add_all([a[i, 0, p], b[i, 0, p]])
                up = mine if n == 0 else outs[3 + n - 1]
                for p in every:
                    up[p] = add_all([a[i, 1, p], b[i, 1, p]])

        kept_d, sent_d, mine_u, *others_u = run(
            "add_core_mlp",
            add_core_mlp,
            [keep0, got0, keep1, got1],
            [shape((1 + n_y, n_dp // 2, sub, hid), BF16)] * 2
            + [shape((n_dp, sub, hid), BF16)] * (1 + n_y),
        )
        (sent_d, d_att), others_u = together([sent_d, d_att], others_u)
        got_d = dp_swap(sent_d, 1)
        got_u = spread_y(others_u)

        vec_rows = n_dp * VEC
        chunk = 4 * sub + 2 * VEC

        half_dp = n_dp // 2

        def place_of(gi, k, p, grads):
            if gi == 1 and k % 2:
                return grads[3 + p // half_dp], p % half_dp
            return grads[2 * gi + k % 2], p

        def attend_back(ins, outs, scratch):
            me, dpi = lax.axis_index("mp"), lax.axis_index("dp")
            (lens, om, gains), fulls, qkvs, ps, atts, wqs, wos, vecs = take(
                ins, [3, 5, 2, 2, 2, 2, 2, 4]
            )
            x_ref, a1_ref, dx1, d_att, out_ref = fulls
            vec, gub_near, gub_even, gub_odd = vecs
            parts, grads = outs[:-5], outs[-5:]
            dqkvs, gqs = scratch[:2], scratch[2:4]
            d_in, vec_f, shared = scratch[4:]
            a1t = a1_ref[...].T
            d_att_v = d_att[...]
            d_att_t = d_att_v.T
            d_in[...] = jnp.zeros_like(d_in)
            cut_slots(parts, 0, out_ref[...])
            order_sums = {}
            for gi, group in enumerate(groups):
                wide = lane * len(group)
                heads = wide // HD
                qkv_ref, p_ref, att_ref = qkvs[gi], ps[gi], atts[gi]
                wq, wo, dqkv, gq = wqs[gi], wos[gi], dqkvs[gi], gqs[gi]
                d_o = dot_nt(d_att_v, wo[...]).astype(BF16)
                for r in range(own):
                    length = lens[me * own + r]
                    order = order_row(om, me, r)
                    kept = keep_row(me, length)
                    column = keep_column(me, length).astype(BF16)
                    here = slice(r * slots, (r + 1) * slots)
                    for pair in range(heads // 2):
                        at = slice(pair * PAIR, (pair + 1) * PAIR)
                        q = qkv_ref[0, here, at] * jnp.asarray(factor, BF16)
                        key = qkv_ref[1, here, at] * jnp.asarray(factor, BF16)
                        val = qkv_ref[2, here, at]
                        do = d_o[here, at] * column
                        dq = dk = dv = 0.0
                        for h in (2 * pair, 2 * pair + 1):
                            p_low = p_ref[r * heads + h]
                            p = p_low.astype(F32)
                            do_h = head_mask(do, h)
                            d_p = dot_nt(do_h, val)
                            inner = jnp.sum(p * d_p, -1, keepdims=True)
                            inner = inner / jnp.sum(p, -1, keepdims=True)
                            d_s = jnp.where(kept, p * (d_p - inner), 0.0).astype(BF16)
                            sums = dot(jnp.ones((8, slots), BF16), d_s)[:1] * order
                            name = (group[h // per], h % per)
                            old = order_sums.get(name)
                            order_sums[name] = sums if old is None else old + sums
                            dq = dq + dot(d_s, head_mask(key, h))
                            dk = dk + dot_tn(d_s, head_mask(q, h))
                            dv = dv + dot_tn(p_low, do_h)
                        dqkv[0, here, at] = dq.astype(BF16)
                        dqkv[1, here, at] = dk.astype(BF16)
                        dqkv[2, here, at] = dv.astype(BF16)
                total = None
                for t in range(3):
                    g = dqkv[t]
                    gq[t] = dot(a1t, g).astype(BF16)
                    term = dot_nt(g, wq[t * width : (t + 1) * width])
                    total = term if total is None else total + term
                d_in[...] += total
                gq[3] = dot(d_att_t, att_ref[...]).astype(BF16)
                for j, k in enumerate(group):
                    at = slice(j * lane, (j + 1) * lane)
                    for p in range(n_dp):
                        here = rows_of(dpi ^ p, sub)
                        to, q = place_of(gi, k, p, grads)
                        for t in range(4):
                            to[j // 2, q, t * sub : (t + 1) * sub] = gq[t, here, at]
                    vec_f[k] = jnp.zeros((vec_rows, lane), F32)
                    base = 6 * cols
                    for n, t in enumerate((0, 2)):
                        vec_f[k, base + n : base + n + 1] = jnp.sum(
                            dqkv[t, :, at].astype(F32), 0, keepdims=True
                        )
                    gub = gub_near[j] if gi == 0 else (gub_even, gub_odd)[j % 2][j // 2]
                    for i in range(hid_rows):
                        vec_f[k, base + 2 + i : base + 3 + i] = gub[:, i * lane : (i + 1) * lane]
                    lanes = lax.broadcasted_iota(jnp.int32, (1, lane), 1)
                    row = jnp.zeros((1, lane), F32)
                    for i in range(per):
                        row = row + jnp.where(
                            lanes == i, jnp.sum(order_sums[(k, i)], -1, keepdims=True), 0.0
                        )
                    vec_f[k, base + 2 + hid_rows : base + 3 + hid_rows] = row
            normed, rstd = normalize(x_ref[...].astype(F32))
            g = d_in[...]
            cut_slots(
                parts, own, (dx1[...] + norm_back(g, normed, rstd, gains[0:1])).astype(BF16)
            )
            shared[0:1] = jnp.sum(g * normed, 0, keepdims=True)
            shared[1:2] = vec[0:1]
            shared[2:3] = jnp.sum(g, 0, keepdims=True)
            shared[3:4] = vec[1:2]
            shared[4:5] = vec[2:3]
            shared[5:6] = vec[3:4]
            for gi, group in enumerate(groups):
                for j, k in enumerate(group):
                    for i in range(6):
                        for c in range(cols):
                            at = i * cols + c
                            vec_f[k, at : at + 1] = shared[i : i + 1, c * lane : (c + 1) * lane]
                    for p in range(n_dp):
                        v = vec_f[k, rows_of(dpi ^ p, VEC)]
                        to, q = place_of(gi, k, p, grads)
                        to[j // 2, q, 4 * sub :] = two_parts(v)

        back = run(
            "attend_back",
            attend_back,
            [lengths, order_mask, norm_scale_pair]
            + [x, a1, dx1, d_att, out_rows]
            + [qkv0, qkv1, p0, p1, att0, att1, wq0, wq1, wo0, wo1]
            + [vec, gub0, gub1_even, gub1_odd],
            [shape((2 * s.shape[0],) + s.shape[1:], BF16) for s in row_shapes]
            + [shape((len(g) // 2, n_dp, chunk, lane), BF16) for g in (g0, g0, g1)]
            + [shape((len(g1) // 2, half_dp, chunk, lane), BF16)] * 2,
            [
                *[pltpu.VMEM((3, count, lane * len(g)), BF16) for g in groups],
                *[pltpu.VMEM((4, width, lane * len(g)), BF16) for g in groups],
                pltpu.VMEM((count, width), F32),
                pltpu.VMEM((n_mp, vec_rows, lane), F32),
                pltpu.VMEM((8, width), F32),
            ],
            smem=(0,),
        )
        row_parts, (ka0, sa0, ka1, *sa1) = back[:-5], back[-5:]
        ga0, ga1 = mp_swap(sa0, 1), [mp_swap(v, 1) for v in sa1]

        def add_core_att(ins, outs, _):
            for n in range(n_y):
                for p in every:
                    got = ins[1 + p // half_dp][n, p % half_dp]
                    dst = outs[2 * n + p // half_dp]
                    dst[p % half_dp] = add_all([ins[0][n, p], got], True)

        others_a = run(
            "add_core_att",
            add_core_att,
            [ka1] + ga1,
            [shape((half_dp, chunk, lane), BF16)] * (2 * n_y),
        )

        def add_x(ins, outs, _):
            for n in range(1 + n_y):
                for i in range(n_dp // 2):
                    outs[n][i] = add_all([ins[0][n, i], ins[1][n, i]])

        mine_d, *others_d = run(
            "add_x", add_x, [kept_d, got_d], [shape((n_dp // 2, sub, hid), BF16)] * (1 + n_y)
        )
        kept_u, sent_u, at_u = add_split([mine_u] + got_u, every, 2)
        others_d, (sent_u,), others_a = together(others_d, [sent_u], others_a)
        got_d = spread_y(others_d)
        got_u = dp_swap(sent_u, 2)
        got_a = [mp_swap(v, y_peers[n // 2]) for n, v in enumerate(others_a)]

        kept_d, sent_d, at_d = add_split([mine_d] + got_d, no_x, 2)
        kept_u, sent_u, at_u = add_split([kept_u, got_u], at_u, 1)
        sent_d, sent_u = together([sent_d, sent_u])[0]
        got_d, got_u = dp_swap(sent_d, 2), dp_swap(sent_u, 1)

        def join(ins, outs, _):
            for n, mine in enumerate((ins[:2], ins[2:])):
                for i in range(outs[0].shape[0]):
                    outs[0][i, n] = add_all([v[i] for v in mine])

        (both,) = run(
            "join",
            join,
            [kept_d, got_d, kept_u, got_u],
            [shape((len(at_d), 2, sub, hid), BF16)],
        )
        at_both = at_d
        for bit in last_bits[:-1]:
            kept, sent, at_both = add_split([both], at_both, bit)
            both = add_whole([kept, dp_swap(sent, bit)])
        got = dp_swap(both, last_bits[-1])
        mine_a = [v.reshape(v.shape[1:]) for v in (ka0, ga0)]
        at_a, with_x = split(every, 1)
        kept_a, *sent_a = add_parts(
            [[v] for v in mine_a] + [got_a[n : n + 2] for n in range(0, 2 * n_y, 2)],
            [at_a, with_x[: len(with_x) // 2], with_x[len(with_x) // 2 :]],
        )
        got_a = [dp_swap(v, 1) for v in sent_a]
        keep, send = split(at_a, 2)
        kept_a, *sent_a = add_parts(
            [[kept_a], got_a], [keep, send[: len(send) // 2], send[len(send) // 2 :]]
        )
        got_a = [dp_swap(v, 2) for v in sent_a]
        at_a = [at_a[i] for i in keep]
        both = meet(both, got, at_both, last_bits[-1], False)
        for bit in reversed(last_bits[:-1]):
            both, at_both = jnp.concatenate([both, dp_swap(both, bit)]), at_both + [
                p ^ bit for p in at_both
            ]

        def part(ins, outs, _):
            for n, o in enumerate(outs):
                for i in range(len(at_both)):
                    o[i] = ins[0][i, n]

        down, up = run("part", part, [both], [shape((len(at_both), sub, hid), BF16)] * 2)

        (sum_a,) = add_parts([[kept_a], got_a], [list(range(len(at_a)))], [down])

        row_parts = list(row_parts)
        row_parts[2:] = spread_y(row_parts[2:])
        down, up = together([down, up])[0]
        got_d, got_u = dp_swap(down, 2), dp_swap(up, 1)
        for bit in last_bits[:-1]:
            kept_a, sent_a, at_a = add_split([sum_a], at_a, bit, True)
            sum_a = add_whole([kept_a, dp_swap(sent_a, bit)], True)
        got_a = dp_swap(sum_a, last_bits[-1])
        down, at_down = jnp.concatenate([down, got_d]), at_both + [p ^ 2 for p in at_both]
        up, at_up = jnp.concatenate([up, got_u]), at_both + [p ^ 1 for p in at_both]
        att = meet(sum_a, got_a, at_a, last_bits[-1], True)
        got_d, got_u = dp_swap(down, 1), dp_swap(up, 2)
        for bit in [*reversed(last_bits[:-1]), 2]:
            att = jnp.concatenate([att, dp_swap(att, bit)])
            at_a = at_a + [p ^ bit for p in at_a]
        (att, got_d, got_u), row_parts = together([att, got_d, got_u], row_parts)
        row_parts = [row_parts[0], mp_swap(row_parts[1], 1)] + pass_rows(row_parts[2:])
        got_a = dp_swap(att, 1)

        def finish_mlp(ins, outs, scratch):
            dpi = lax.axis_index("dp")
            for n, p in enumerate(at_down):
                for v, at in zip(ins[:2], (p, p ^ 1)):
                    scratch[0][rows_of(dpi ^ at, sub)] = v[n].astype(F32)
            for n, p in enumerate(at_up):
                for v, at in zip(ins[2:], (p, p ^ 2)):
                    outs[1][rows_of(dpi ^ at, sub)] = v[n].astype(F32)
            outs[0][...] = scratch[0][...].T
            outs[2][...] = jnp.zeros((8, LANES), F32)

        mark = shape((8, LANES), F32)
        r_down, r_up, mlp_mark = run(
            "finish_mlp",
            finish_mlp,
            [down, got_d, up, got_u],
            [shape((hid, width), F32), shape((width, hid), F32), mark],
            [pltpu.VMEM((width, hid), F32)],
        )

        def finish_att(ins, outs, scratch):
            r_qkv, r_out, gain, shift, outb, qvb, upb, order = outs
            turned_out, vec_f = scratch
            dpi = lax.axis_index("dp")
            for src, n, p in [(0, n, p) for n, p in enumerate(at_a)] + [
                (1, n, p ^ 1) for n, p in enumerate(at_a)
            ]:
                v = ins[src][n]
                at = dpi ^ p
                here = rows_of(at, sub)
                for t in range(3):
                    r_qkv[t, here] = v[t * sub : (t + 1) * sub].astype(F32)
                turned_out[here] = v[3 * sub : 4 * sub].astype(F32)
                pairs = v[4 * sub :].astype(F32)
                vec_f[rows_of(at, VEC)] = pairs[:VEC] + pairs[VEC:]
            r_out[...] = turned_out[...].T
            for i in range(6):
                dst = (gain, shift, outb)[i // 2]
                dst[i % 2 : i % 2 + 1] = jnp.concatenate(
                    [vec_f[i * cols + c : i * cols + c + 1] for c in range(cols)], 1
                )
            base = 6 * cols
            qvb[...] = vec_f[base : base + 2]
            upb[...] = jnp.concatenate(
                [vec_f[base + 2 + i : base + 3 + i] for i in range(hid_rows)], 1
            )
            order[...] = vec_f[base + 2 + hid_rows : base + 3 + hid_rows, :per]

        pair_shape = shape((2, width), F32)
        def gather_rows(ins, outs, _):
            me = lax.axis_index("mp")
            for k in range(n_mp):
                here = pl.ds((me ^ k) * own, own)
                outs[0][here] = ins[k][:own]
                outs[1][here] = ins[k][own : 2 * own].astype(F32)
            outs[2][...] = jnp.zeros((8, LANES), F32)

        output, token_gradient, rows_mark = run(
            "gather_rows",
            gather_rows,
            row_parts,
            [shape((rows, share, width), BF16), shape((rows, share, width), F32), mark],
        )
        r_qkv, r_out, gain, shift, outb, qvb, upb, order = run(
            "finish_att",
            finish_att,
            [att, got_a],
            [
                shape((3, width, lane), F32),
                shape((lane, width), F32),
                pair_shape,
                pair_shape,
                pair_shape,
                shape((2, lane), F32),
                shape((1, hid), F32),
                shape((1, per), F32),
            ],
            [pltpu.VMEM((width, lane), F32), pltpu.VMEM((vec_rows, lane), F32)],
            after=[mlp_mark, rows_mark],
        )

        return (
            output,
            token_gradient,
            gain,
            shift,
            r_qkv,
            qvb,
            order.reshape(per),
            r_out,
            outb,
            r_up,
            upb.reshape(hid),
            r_down,
        )

    return body


def solution(mesh):
    return jax.shard_map(
        make_body(mesh.shape["dp"], mesh.shape["mp"]),
        mesh=mesh,
        in_specs=(
            P("dp", "mp", None),
            P("dp"),
            P("dp", None),
            P(),
            P(),
            P(None, None, "mp"),
            P(None, "mp"),
            P("mp"),
            P("mp", None),
            P(),
            P(None, "mp"),
            P("mp"),
            P("mp", None),
            P("dp", "mp", None),
        ),
        out_specs=(
            P("dp", "mp", None),
            P("dp", "mp", None),
            P(),
            P(),
            P(None, None, "mp"),
            P(None, "mp"),
            P("mp"),
            P("mp", None),
            P(),
            P(None, "mp"),
            P("mp"),
            P("mp", None),
        ),
        check_vma=False,
    )
```

```python
import jax
import jax.numpy as jnp
from jax import lax
from jax.experimental import pallas as pl
from jax.experimental.pallas import tpu as pltpu
from jax.sharding import PartitionSpec as P

HD = 64
PAIR = 2 * HD
LANES = 128
F32 = jnp.float32
BF16 = jnp.bfloat16
VMEM_LIMIT = 28 * 2**20
VMEM_MOST = 60 * 2**20
GELU_C = 0.7978845608028654
GELU_A = 0.044715
VEC = 8


def swap(v, axis, bit, size):
    return lax.ppermute(v, axis, [(i, i ^ bit) for i in range(size)])


def bits_of(size):
    return [1 << b for b in range(size.bit_length() - 1)]


def shape(dims, kind):
    return jax.ShapeDtypeStruct(tuple(dims), kind)


def together(*lists):
    out = lax.optimization_barrier(tuple(tuple(v) for v in lists))
    return [list(v) for v in out]


def run(name, fn, ins, outs, scratch=(), smem=(), after=(), hbm=(), limit=VMEM_LIMIT):
    n_in, n_out, n_all = len(ins), len(outs), len(ins) + len(after)

    def kernel(*refs):
        fn(refs[:n_in], refs[n_all : n_all + n_out], refs[n_all + n_out :])

    return pl.pallas_call(
        kernel,
        out_shape=tuple(outs),
        in_specs=[
            pl.BlockSpec(
                memory_space=pltpu.SMEM if i in smem else pl.ANY if i in hbm else pltpu.VMEM
            )
            for i in range(n_in)
        ]
        + [pl.BlockSpec(memory_space=pl.ANY) for _ in after],
        out_specs=tuple(pl.BlockSpec(memory_space=pltpu.VMEM) for _ in outs),
        scratch_shapes=list(scratch),
        compiler_params=pltpu.CompilerParams(vmem_limit_bytes=limit),
        cost_estimate=pl.CostEstimate(flops=1, bytes_accessed=1, transcendentals=0),
        name=name,
    )(*ins, *after)


def dot(a, b):
    return jnp.dot(a, b, preferred_element_type=F32)


def dot_nt(a, b):
    return lax.dot_general(a, b, (((1,), (1,)), ((), ())), preferred_element_type=F32)


def dot_tn(a, b):
    return lax.dot_general(a, b, (((0,), (0,)), ((), ())), preferred_element_type=F32)


def normalize(v):
    centre = v - jnp.mean(v, -1, keepdims=True)
    rstd = lax.rsqrt(jnp.mean(centre * centre, -1, keepdims=True) + 1e-05)
    return centre * rstd, rstd


def norm_back(g, normed, rstd, gain):
    e = g * gain
    return rstd * (
        e - jnp.mean(e, -1, keepdims=True) - normed * jnp.mean(e * normed, -1, keepdims=True)
    )


def rows_of(start, size):
    return pl.ds(pl.multiple_of(start * size, size), size)


def in_order(a, b, bit):
    first = bit == 0
    return jnp.concatenate([jnp.where(first, a, b), jnp.where(first, b, a)], 0)


def whole(pieces, x_bit, z_bit=None):
    values = [v[...] for v in pieces]
    if len(values) == 4:
        return in_order(in_order(*values[:2], x_bit), in_order(*values[2:], x_bit), z_bit)
    return in_order(*values, x_bit) if len(values) == 2 else values[0]


def take(refs, counts):
    out, at = [], 0
    for c in counts:
        out.append(refs[at : at + c])
        at += c
    assert at == len(refs)
    return out


def three_parts(v):
    high = v.astype(BF16).astype(F32)
    rest = v - high
    middle = rest.astype(BF16).astype(F32)
    zeros = jnp.zeros((5 * v.shape[0], v.shape[1]), F32)
    return jnp.concatenate([high, middle, rest - middle, zeros], 0).astype(BF16)


def two_parts(v):
    high = v.astype(BF16).astype(F32)
    return jnp.concatenate([high, v - high], 0).astype(BF16)


def make_body(n_dp, n_mp):
    groups = [[0, 1], list(range(2, n_mp))]
    y_peers = list(range(2, n_mp, 2))
    def body(
        tokens,
        lengths,
        order_mask,
        norm_scale_pair,
        norm_offset_pair,
        w_qkv,
        qv_bias,
        order_bias,
        w_out,
        out_bias,
        w_up,
        up_bias,
        w_down,
        cotangent,
    ):
        rows, share, width = tokens.shape
        slots = order_mask.shape[1]
        own = rows // n_mp
        count = own * slots
        lane = qv_bias.shape[1]
        per = order_bias.shape[0]
        hid = up_bias.shape[0]
        hid_rows = hid // lane
        cols = width // lane
        piece = shape((own, share, width), BF16)
        sub = width // n_dp
        factor = HD**-0.5
        o_at, s_at = 3 * width, 4 * width
        bundle_rows = 4 * width + 8 * VEC

        def mp_swap(v, bit):
            return swap(v, "mp", bit, n_mp)

        def dp_swap(v, bit):
            return swap(v, "dp", bit, n_dp)

        def send_rows(core, pairs):
            return [mp_swap(core, 1)] + spread_y(pairs)

        def pass_rows(pairs):
            half = pairs[0].shape[0] // 2
            passed = [mp_swap(v[half:], 1) for v in pairs]
            return [p for pair in zip(pairs, passed) for p in pair]

        def over_y(v):
            return [mp_swap(v, k) for k in y_peers]

        def spread_y(parts):
            return [mp_swap(v, k) for k, v in zip(y_peers, parts)]

        row_shapes = [piece] * 2 + [shape((2 * own, share, width), BF16)] * len(y_peers)

        def cut_copies(src, outs, sems):
            me = lax.axis_index("mp")
            copies = []
            for k in range(n_mp):
                dst = outs[k] if k < 2 else outs[k // 2 + 1].at[pl.ds((k % 2) * own, own)]
                here = src.at[pl.ds((me ^ k) * own, own)]
                copies.append(pltpu.make_async_copy(here, dst, sems.at[k]))
            for c in copies:
                c.start()
            return copies

        def begin(ins, outs, scratch):
            dpi = lax.axis_index("dp")
            bundle, quarter = outs[-2:]
            copies = cut_copies(ins[0], outs, scratch[0])
            copies.append(
                pltpu.make_async_copy(ins[1], bundle.at[pl.ds(0, o_at)], scratch[1])
            )
            copies[-1].start()
            for c in range(cols):
                bundle[o_at + c * lane : o_at + (c + 1) * lane] = ins[2][
                    :, c * lane : (c + 1) * lane
                ]
            small = jnp.concatenate(
                [
                    ins[3][...],
                    ins[4][...],
                    jnp.concatenate([ins[5][...], jnp.zeros((1, lane - per), F32)], 1),
                    jnp.zeros((VEC - 3 - hid_rows, lane), F32),
                ],
                0,
            )
            bundle[s_at:] = three_parts(small)
            for c in copies:
                c.wait()
            mine = 2 * ((dpi >> 1) & 1) + (dpi & 1)
            quarter[...] = bundle[rows_of(mine, bundle_rows // 4)]

        *token_parts, bundle, bundle_quarter = run(
            "begin",
            begin,
            [
                tokens,
                w_qkv.reshape(-1, lane),
                w_out,
                qv_bias,
                up_bias.reshape(hid_rows, lane),
                order_bias.reshape(1, per),
            ],
            row_shapes
            + [shape((bundle_rows, lane), BF16), shape((bundle_rows // 4, lane), BF16)],
            [pltpu.SemaphoreType.DMA((n_mp,)), pltpu.SemaphoreType.DMA(())],
            hbm=(0, 1),
            limit=VMEM_MOST,
        )

        def cut_rest(ins, outs, scratch):
            dpi = lax.axis_index("dp")
            copies = cut_copies(ins[0], outs, scratch[0])
            halves = outs[len(row_shapes) :]
            for n, (src, bit) in enumerate(zip(ins[1:], (dpi & 1, (dpi >> 1) & 1))):
                here = src.at[rows_of(bit, src.shape[0] // 2)]
                dst = halves[0].at[n] if joined else halves[n]
                copies.append(pltpu.make_async_copy(here, dst, scratch[1].at[n]))
                copies[-1].start()
            for c in copies:
                c.wait()

        joined = w_up.shape == w_down.shape
        half_shapes = [shape((v.shape[0] // 2, v.shape[1]), BF16) for v in (w_up, w_down)]
        rest = run(
            "cut_rest",
            cut_rest,
            [cotangent, w_up, w_down],
            row_shapes
            + ([shape((2,) + half_shapes[0].shape, BF16)] if joined else half_shapes),
            [pltpu.SemaphoreType.DMA((n_mp,)), pltpu.SemaphoreType.DMA((2,))],
            hbm=(0, 1, 2),
            after=[bundle_quarter],
            limit=VMEM_MOST,
        )
        cot_parts, half_parts = list(rest[: len(row_shapes)]), rest[len(row_shapes) :]

        sends, (bundle, bundle_quarter) = together(token_parts[1:], [bundle, bundle_quarter])
        token_parts = token_parts[:1] + send_rows(sends[0], sends[1:])
        bundle_core, bundle_y = mp_swap(bundle, 1), over_y(bundle_quarter)

        near = [w_up, w_down]
        near_core = [mp_swap(v, 1) for v in near]
        bundle_y, (bundle_core,), token_parts[:2], near_core = together(
            bundle_y, [bundle_core], token_parts[:2], near_core
        )
        halves_y = [over_y(v) for v in half_parts]
        bundle_x, bundle_z = ([dp_swap(v, bit) for v in bundle_y] for bit in (1, 2))
        bundle_xz = [dp_swap(v, 2) for v in bundle_x]
        bundle_yc = [mp_swap(v, 1) for v in bundle_y]
        token_parts = token_parts[:2] + pass_rows(token_parts[2:])

        def far(even, odd):
            return [v[n] for n in range(len(y_peers)) for vs in (even, odd) for v in vs]

        def order_row(om_ref, me, r):
            v = om_ref[pl.ds(me * own + r, 1), :].astype(F32)
            v = jnp.broadcast_to(v, (8, slots))
            at = lax.broadcasted_iota(jnp.int32, (8, slots), 1)
            step = share
            while step < slots:
                turned = jnp.where(
                    (at & step) == 0, pltpu.roll(v, slots - step, 1), pltpu.roll(v, step, 1)
                )
                v = jnp.where((me * share) & step, turned, v)
                step *= 2
            return v[:1]

        def keep_row(me, length):
            at = lax.broadcasted_iota(jnp.int32, (1, slots), 1)
            return (at ^ (me * share)) < length

        def keep_column(me, length):
            at = lax.broadcasted_iota(jnp.int32, (slots, 1), 0)
            return ((at ^ (me * share)) < length).astype(F32)

        def head_mask(pair_value, h):
            at = lax.broadcasted_iota(jnp.int32, pair_value.shape, 1)
            return jnp.where((at >= HD) == (h % 2 == 1), pair_value, jnp.zeros_like(pair_value))

        def assemble(dst, parts):
            for r in range(own):
                for k in range(n_mp):
                    dst[r * slots + k * share : r * slots + (k + 1) * share] = parts[k][r]

        def cut_slots(dst, lead, value):
            for r in range(own):
                for k in range(n_mp):
                    at = r * slots + k * share
                    to, first = (dst[k], 0) if k < 2 else (dst[k // 2 + 1], (k % 2) * 2 * own)
                    to[first + lead + r] = value[at : at + share]

        def attend(group, first, pieces):
            wide = lane * len(group)
            heads = wide // HD
            counts = [len(pieces) // len(group)] * len(group)

            def fn(ins, outs, scratch):
                me, dpi = lax.axis_index("mp"), lax.axis_index("dp")
                qkv_ref, p_ref, att_ref, weights, wo, smalls = outs[-6:]
                if first:
                    lens, om, gains, shifts = ins[n_mp : n_mp + 4]
                    x_ref, a1_ref = outs[:2]
                    assemble(x_ref, ins[:n_mp])
                    normed, _ = normalize(x_ref[...].astype(F32))
                    a1_ref[...] = (normed * gains[0:1] + shifts[0:1]).astype(BF16)
                else:
                    lens, om, a1_ref = ins[:3]
                for j, ps in enumerate(take(ins[-len(pieces) :], counts)):
                    v = whole(ps, dpi & 1, (dpi >> 1) & 1)
                    weights[:, j * lane : (j + 1) * lane] = v[:o_at]
                    for c in range(cols):
                        wo[j * lane : (j + 1) * lane, c * lane : (c + 1) * lane] = v[
                            o_at + c * lane : o_at + (c + 1) * lane
                        ]
                    parts = v[s_at:].astype(F32)
                    smalls[j] = parts[:VEC] + parts[VEC : 2 * VEC] + parts[2 * VEC : 3 * VEC]
                a1 = a1_ref[...]
                for t in range(3):
                    y = dot(a1, weights[t * width : (t + 1) * width])
                    if t != 1:
                        i = t // 2
                        y = y + jnp.concatenate(
                            [smalls[j, i : i + 1] for j in range(len(group))], 1
                        )
                    qkv_ref[t] = y.astype(BF16)
                for r in range(own):
                    length = lens[me * own + r]
                    order = order_row(om, me, r)
                    kept = keep_row(me, length)
                    column = keep_column(me, length)
                    here = slice(r * slots, (r + 1) * slots)
                    for pair in range(heads // 2):
                        at = slice(pair * PAIR, (pair + 1) * PAIR)
                        q = qkv_ref[0, here, at] * jnp.asarray(factor, BF16)
                        key = qkv_ref[1, here, at]
                        val = qkv_ref[2, here, at]
                        acc = None
                        for h in (2 * pair, 2 * pair + 1):
                            o = 2 + hid_rows
                            ob = smalls[h // per, o : o + 1, h % per : h % per + 1]
                            row = jnp.where(kept, ob * order, -1e30)
                            s = dot_nt(head_mask(q, h), key) + row
                            e = jnp.exp(s - jnp.max(s, -1, keepdims=True))
                            p = (e * (1.0 / jnp.sum(e, -1, keepdims=True))).astype(BF16)
                            p_ref[r * heads + h] = p
                            term = dot(p, head_mask(val, h))
                            acc = term if acc is None else acc + term
                        att_ref[here, at] = (acc * column).astype(BF16)

            ins = (
                token_parts + [lengths, order_mask, norm_scale_pair, norm_offset_pair]
                if first
                else [lengths, order_mask, a1]
            )
            lead = [shape((count, width), BF16)] * 2 if first else []
            return run(
                "attend",
                fn,
                ins + pieces,
                lead
                + [
                    shape((3, count, wide), BF16),
                    shape((own * heads, slots, slots), BF16),
                    shape((count, wide), BF16),
                    shape((3 * width, wide), BF16),
                    shape((wide, width), BF16),
                    shape((len(group), VEC, lane), F32),
                ],
                smem=(n_mp if first else 0,),
            )

        x, a1, qkv0, p0, att0, wq0, wo0, small0 = attend(groups[0], True, [bundle, bundle_core])

        bundle_x, bundle_z, bundle_xz, (att0,), sends = together(
            bundle_x, bundle_z, bundle_xz, [att0], cot_parts[1:]
        )
        cot_parts = cot_parts[:1] + send_rows(sends[0], sends[1:])
        bundle_xc, bundle_zc, bundle_xzc = (
            [mp_swap(v, 1) for v in vs] for vs in (bundle_x, bundle_z, bundle_xz)
        )
        qkv1, p1, att1, wq1, wo1, small1 = attend(
            groups[1], False, far(
                (bundle_y, bundle_x, bundle_z, bundle_xz),
                (bundle_yc, bundle_xc, bundle_zc, bundle_xzc),
            )
        )

        def take_apart(ins, outs, _):
            for n, o in enumerate(outs):
                o[...] = ins[0][n]

        if joined:
            pairs = [run("take_apart", take_apart, [v], half_shapes, after=[att1]) for v in halves_y[0]]
            halves_y = list(zip(*pairs))
        up_y, down_y, (att1,), cot_parts[1:2] = together(*halves_y, [att1], cot_parts[1:2])
        up_x, down_z = [dp_swap(v, 1) for v in up_y], [dp_swap(v, 2) for v in down_y]
        up_yc, down_yc = ([mp_swap(v, 1) for v in vs] for vs in (up_y, down_y))

        def scatter(dst, src, block, which, dpi):
            for p in range(n_dp):
                dst[block, which, p] = src[rows_of(dpi ^ p, sub), :]

        def mlp_forward(a2, wu, wd, bias, mixed):
            up = jnp.concatenate([bias[2 + i : 3 + i] for i in range(hid_rows)], 1)
            pre = dot(a2[...], wu) + up
            square = pre * pre
            t = jnp.tanh(pre * (GELU_C + (GELU_C * GELU_A) * square))
            half = 0.5 + 0.5 * t
            hidden = (pre * half).astype(BF16)
            slope = half + (pre * (1.0 - t * t)) * (
                0.5 * GELU_C + (1.5 * GELU_C * GELU_A) * square
            )
            mixed[...] += dot(hidden, wd)
            return hidden, slope

        def mlp_backward(hidden, slope, a2t, dy, dyt, wu, wd, d_mid, gs, dst, block, bias_sum, dpi):
            d_hidden = dot_nt(dy[...], wd)
            d_pre = (slope * d_hidden).astype(BF16)
            d_mid[...] += dot_nt(d_pre, wu)
            g_down, g_up = gs.at[0], gs.at[1]
            g_down[...] = dot(dyt[...], hidden).astype(BF16)
            scatter(dst, g_down, block, 0, dpi)
            g_up[...] = dot(a2t[...], d_pre).astype(BF16)
            scatter(dst, g_up, block, 1, dpi)
            bias_sum[...] = jnp.sum(d_pre.astype(F32), 0, keepdims=True)

        def mlp_outs(n_blocks, n_arrays):
            both = shape((n_blocks // n_arrays, 2, n_dp, sub, hid), BF16)
            return [both] * n_arrays + [shape((n_blocks, 1, hid), F32)]

        full = shape((count, width), F32)
        full_bf = shape((count, width), BF16)
        turned = shape((width, count), BF16)
        g0, g1 = groups

        def mlp_near_forward(ins, outs, _):
            lead, wu_p, wd_p = take(ins, [9, len(g0), len(g0)])
            x_ref, att0_ref, att1_ref, wo0_ref, wo1_ref, smalls, gains, shifts, ob = lead
            x1, a2, a2t, mixed, hidden, slope = outs
            v = x_ref[...].astype(F32) + (
                dot(att0_ref[...], wo0_ref[...]) + dot(att1_ref[...], wo1_ref[...]) + ob[0:1]
            )
            x1[...] = v
            normed, _ = normalize(v)
            act = (normed * gains[1:2] + shifts[1:2]).astype(BF16)
            a2[...] = act
            a2t[...] = act.T
            mixed[...] = jnp.zeros_like(mixed)
            for j in range(len(g0)):
                hidden[j], slope[j] = mlp_forward(
                    a2, wu_p[j][...], wd_p[j][...], smalls.at[j], mixed
                )

        near_up, near_down = [near[0], near_core[0]], [near[1], near_core[1]]
        x1, a2, a2t, mixed, hidden, slope = run(
            "mlp_near_forward",
            mlp_near_forward,
            [x, att0, att1, wo0, wo1, small0, norm_scale_pair, norm_offset_pair, out_bias]
            + near_up
            + near_down,
            [full, full_bf, turned, full]
            + [shape((len(g0), count, hid), BF16), shape((len(g0), count, hid), F32)],
        )

        cot_parts[2:], (a2,) = together(cot_parts[2:], [a2])
        cot_parts = cot_parts[:2] + pass_rows(cot_parts[2:])

        def mlp_near_backward(ins, outs, scratch):
            dpi = lax.axis_index("dp")
            (hidden, slope, a2t), dy_p, wu_p, wd_p = take(ins, [3, n_mp, len(g0), len(g0)])
            dy, dyt, d_mid = outs[:3]
            assemble(dy, dy_p)
            dyt[...] = dy[...].T
            d_mid[...] = jnp.zeros_like(d_mid)
            for j, k in enumerate(g0):
                mlp_backward(
                    hidden[j],
                    slope[j],
                    a2t,
                    dy,
                    dyt,
                    wu_p[j][...],
                    wd_p[j][...],
                    d_mid,
                    scratch[j],
                    outs[3 + k % 2],
                    0,
                    outs[5].at[j],
                    dpi,
                )

        dy, dyt, d_mid, keep0, send0, gub0 = run(
            "mlp_near_backward",
            mlp_near_backward,
            [hidden, slope, a2t] + cot_parts + near_up + near_down,
            [full_bf, turned, full] + mlp_outs(len(g0), 2),
            [pltpu.VMEM((2, width, hid), BF16)] * len(g0),
        )

        up_yc, up_x, down_yc, down_z, (gub0,) = together(up_yc, up_x, down_yc, down_z, [gub0])
        up_xc, down_zc = ([mp_swap(v, 1) for v in vs] for vs in (up_x, down_z))
        got0 = mp_swap(send0, 1)

        up1 = far((up_y, up_x), (up_yc, up_xc))
        down1 = far((down_y, down_z), (down_yc, down_zc))

        def mlp_far(j, last):
            ks = g1[j::2]
            n_w = 2 * len(ks)

            def fn(ins, outs, scratch):
                dpi = lax.axis_index("dp")
                lead, wu_p, wd_p, done = take(ins, [10, n_w, n_w, 2 if last else 0])
                x1, a2, a2t, dy, dyt, mixed_in, d_mid_in, smalls, gains, ob = lead
                (mixed, d_mid), gs = (scratch[:2], scratch[2:]) if last else (outs[:2], scratch)
                mixed[...] = mixed_in[...]
                d_mid[...] = d_mid_in[...]
                grads, bias_sums = outs[-2:]
                for n in range(len(ks)):
                    wu = whole(wu_p[2 * n : 2 * n + 2], dpi & 1)
                    wd = whole(wd_p[2 * n : 2 * n + 2], (dpi >> 1) & 1)
                    if last:
                        hidden, slope = done[0][n], done[1][n]
                    else:
                        hidden, slope = mlp_forward(a2, wu, wd, smalls.at[2 * n + j], mixed)
                    mlp_backward(
                        hidden,
                        slope,
                        a2t,
                        dy,
                        dyt,
                        wu,
                        wd,
                        d_mid,
                        gs[n],
                        grads,
                        n,
                        bias_sums.at[n],
                        dpi,
                    )
                if not last:
                    return
                output, dx1, d_att, vec = outs[:4]
                v = x1[...]
                output[...] = (v + (mixed[...] + ob[1:2])).astype(BF16)
                normed, rstd = normalize(v)
                g = d_mid[...]
                dyf = dy[...].astype(F32)
                d = dyf + norm_back(g, normed, rstd, gains[1:2])
                dx1[...] = d
                low = d.astype(BF16)
                d_att[...] = low
                vec[0:1] = jnp.sum(g * normed, 0, keepdims=True)
                vec[1:2] = jnp.sum(g, 0, keepdims=True)
                vec[2:3] = jnp.sum(low.astype(F32), 0, keepdims=True)
                vec[3:4] = jnp.sum(dyf, 0, keepdims=True)

            sums = [pltpu.VMEM((count, width), F32)] * 2
            return run(
                "mlp_far",
                fn,
                [x1, a2, a2t, dy, dyt, mixed, d_mid, small1, norm_scale_pair, out_bias]
                + [v for n in range(len(ks)) for v in up1[4 * n + 2 * j : 4 * n + 2 * j + 2]]
                + [v for n in range(len(ks)) for v in down1[4 * n + 2 * j : 4 * n + 2 * j + 2]]
                + ([far_hidden, far_slope] if last else []),
                ([full_bf, full, full_bf, shape((4, width), F32)] if last else [full, full])
                + mlp_outs(len(ks), 1),
                (sums if last else []) + [pltpu.VMEM((2, width, hid), BF16)] * len(ks),
            )

        def mlp_even_forward(ins, outs, _):
            dpi = lax.axis_index("dp")
            n_w = 2 * len(y_peers)
            (a2, mixed_in, smalls), wu_p, wd_p = take(ins, [3, n_w, n_w])
            mixed, hidden, slope = outs
            mixed[...] = mixed_in[...]
            for n in range(len(y_peers)):
                wu = whole(wu_p[2 * n : 2 * n + 2], dpi & 1)
                wd = whole(wd_p[2 * n : 2 * n + 2], (dpi >> 1) & 1)
                hidden[n], slope[n] = mlp_forward(a2, wu, wd, smalls.at[2 * n], mixed)

        mixed, far_hidden, far_slope = run(
            "mlp_even_forward",
            mlp_even_forward,
            [a2, mixed, small1]
            + [v for pair in zip(up_y, up_x) for v in pair]
            + [v for pair in zip(down_y, down_z) for v in pair],
            [full]
            + [shape((len(y_peers), count, hid), kind) for kind in (BF16, F32)],
        )
        mixed, d_mid, send1, gub1_odd = mlp_far(1, False)
        send1, mixed = together([send1, mixed])[0]
        got1 = mp_swap(send1, 1)
        out_rows, dx1, d_att, vec, keep1, gub1_even = mlp_far(0, True)

        def add_all(values, vectors=False):
            total = values[0].astype(F32)
            for v in values[1:]:
                total = total + v.astype(F32)
            if not vectors:
                return total.astype(BF16)
            m = total.shape[-2]
            head = total[: m - 2 * VEC]
            v = total[m - 2 * VEC : m - VEC] + total[m - VEC :]
            high = v.astype(BF16).astype(F32)
            return jnp.concatenate([head, high, v - high], 0).astype(BF16)

        n_y = len(y_peers)

        def split(places, bit):
            return [i for i, p in enumerate(places) if not p & bit], [
                i for i, p in enumerate(places) if p & bit
            ]

        def add_split(parts, places, bit, vectors=False, after=(), two=False, halves=()):
            picks = split(places, bit)
            n_parts, n_half = len(parts), len(places) // 2

            def fn(ins, outs, _):
                for pick, dsts in zip(picks, (outs[:1], outs[1:])):
                    for at, i in enumerate(pick):
                        values = [v[i] for v in ins[:n_parts]]
                        if halves:
                            values.append(ins[n_parts + i // n_half][i % n_half])
                        size = dsts[0].shape[0]
                        dsts[at // size][at % size] = add_all(values, vectors)

            n, rest = len(picks[0]), parts[0].shape[1:]
            sizes = [n] + ([n // 2] * 2 if two else [n])
            kept, *sent = run(
                "add_split",
                fn,
                list(parts) + list(halves),
                [shape((k,) + rest, BF16) for k in sizes],
                after=after,
            )
            return kept, sent if two else sent[0], [places[i] for i in picks[0]]

        def add_parts(parts, picks, after=()):
            counts = [len(p) for p in parts]

            def fn(ins, outs, _):
                for dst, pick in zip(outs, picks):
                    for at, i in enumerate(pick):
                        values = []
                        for refs in take(ins, counts):
                            n = refs[0].shape[0]
                            values.append(refs[i // n][i % n])
                        dst[at] = add_all(values, True)

            flat_parts = [v for p in parts for v in p]
            rest = flat_parts[0].shape[1:]
            outs = [shape((len(p),) + rest, BF16) for p in picks]
            return run("add_parts", fn, flat_parts, outs, after=after)

        def add_whole(parts, vectors=False):
            def fn(ins, outs, _):
                for i in range(outs[0].shape[0]):
                    outs[0][i] = add_all([v[i] for v in ins], vectors)

            return run("add_whole", fn, parts, [shape(parts[0].shape, BF16)])[0]

        def meet(mine, got, places, bit, vectors):
            def fn(ins, outs, _):
                for i, p in enumerate(places):
                    outs[0][i] = add_all([ins[0][i], ins[1][places.index(p ^ bit)]], vectors)

            return run("meet", fn, [mine, got], [shape(mine.shape, BF16)])[0]

        every = list(range(n_dp))
        no_x, with_x = split(every, 1)
        last_bits = [b for b in bits_of(n_dp) if b > 2]

        def add_core_mlp(ins, outs, _):
            keep0, got0, keep1, got1 = ins
            kept, sent, mine = outs[:3]
            for n in range(1 + n_y):
                a, b, i = (keep0, got0, 0) if n == 0 else (keep1, got1, n - 1)
                for dst, pick in ((kept, no_x), (sent, with_x)):
                    for at, p in enumerate(pick):
                        dst[n, at] = add_all([a[i, 0, p], b[i, 0, p]])
                up = mine if n == 0 else outs[3 + n - 1]
                for p in every:
                    up[p] = add_all([a[i, 1, p], b[i, 1, p]])

        kept_d, sent_d, mine_u, *others_u = run(
            "add_core_mlp",
            add_core_mlp,
            [keep0, got0, keep1, got1],
            [shape((1 + n_y, n_dp // 2, sub, hid), BF16)] * 2
            + [shape((n_dp, sub, hid), BF16)] * (1 + n_y),
        )
        (sent_d, d_att), others_u = together([sent_d, d_att], others_u)
        got_d = dp_swap(sent_d, 1)
        got_u = spread_y(others_u)

        vec_rows = n_dp * VEC
        chunk = 4 * sub + 2 * VEC

        half_dp = n_dp // 2

        def place_of(gi, k, p, grads):
            if gi == 1 and k % 2:
                return grads[3 + p // half_dp], p % half_dp
            return grads[2 * gi + k % 2], p

        def attend_back(ins, outs, scratch):
            me, dpi = lax.axis_index("mp"), lax.axis_index("dp")
            (lens, om, gains), fulls, qkvs, ps, atts, wqs, wos, vecs = take(
                ins, [3, 5, 2, 2, 2, 2, 2, 4]
            )
            x_ref, a1_ref, dx1, d_att, out_ref = fulls
            vec, gub_near, gub_even, gub_odd = vecs
            parts, grads = outs[:-5], outs[-5:]
            dqkvs, gqs = scratch[:2], scratch[2:4]
            d_in, vec_f, shared = scratch[4:]
            a1t = a1_ref[...].T
            d_att_v = d_att[...]
            d_att_t = d_att_v.T
            d_in[...] = jnp.zeros_like(d_in)
            cut_slots(parts, 0, out_ref[...])
            order_sums = {}
            for gi, group in enumerate(groups):
                wide = lane * len(group)
                heads = wide // HD
                qkv_ref, p_ref, att_ref = qkvs[gi], ps[gi], atts[gi]
                wq, wo, dqkv, gq = wqs[gi], wos[gi], dqkvs[gi], gqs[gi]
                d_o = dot_nt(d_att_v, wo[...]).astype(BF16)
                for r in range(own):
                    length = lens[me * own + r]
                    order = order_row(om, me, r)
                    kept = keep_row(me, length)
                    column = keep_column(me, length).astype(BF16)
                    here = slice(r * slots, (r + 1) * slots)
                    for pair in range(heads // 2):
                        at = slice(pair * PAIR, (pair + 1) * PAIR)
                        q = qkv_ref[0, here, at] * jnp.asarray(factor, BF16)
                        key = qkv_ref[1, here, at] * jnp.asarray(factor, BF16)
                        val = qkv_ref[2, here, at]
                        do = d_o[here, at] * column
                        dq = dk = dv = 0.0
                        for h in (2 * pair, 2 * pair + 1):
                            p_low = p_ref[r * heads + h]
                            p = p_low.astype(F32)
                            do_h = head_mask(do, h)
                            d_p = dot_nt(do_h, val)
                            inner = jnp.sum(p * d_p, -1, keepdims=True)
                            inner = inner / jnp.sum(p, -1, keepdims=True)
                            d_s = jnp.where(kept, p * (d_p - inner), 0.0).astype(BF16)
                            sums = dot(jnp.ones((8, slots), BF16), d_s)[:1] * order
                            name = (group[h // per], h % per)
                            old = order_sums.get(name)
                            order_sums[name] = sums if old is None else old + sums
                            dq = dq + dot(d_s, head_mask(key, h))
                            dk = dk + dot_tn(d_s, head_mask(q, h))
                            dv = dv + dot_tn(p_low, do_h)
                        dqkv[0, here, at] = dq.astype(BF16)
                        dqkv[1, here, at] = dk.astype(BF16)
                        dqkv[2, here, at] = dv.astype(BF16)
                total = None
                for t in range(3):
                    g = dqkv[t]
                    gq[t] = dot(a1t, g).astype(BF16)
                    term = dot_nt(g, wq[t * width : (t + 1) * width])
                    total = term if total is None else total + term
                d_in[...] += total
                gq[3] = dot(d_att_t, att_ref[...]).astype(BF16)
                for j, k in enumerate(group):
                    at = slice(j * lane, (j + 1) * lane)
                    for p in range(n_dp):
                        here = rows_of(dpi ^ p, sub)
                        to, q = place_of(gi, k, p, grads)
                        for t in range(4):
                            to[j // 2, q, t * sub : (t + 1) * sub] = gq[t, here, at]
                    vec_f[k] = jnp.zeros((vec_rows, lane), F32)
                    base = 6 * cols
                    for n, t in enumerate((0, 2)):
                        vec_f[k, base + n : base + n + 1] = jnp.sum(
                            dqkv[t, :, at].astype(F32), 0, keepdims=True
                        )
                    gub = gub_near[j] if gi == 0 else (gub_even, gub_odd)[j % 2][j // 2]
                    for i in range(hid_rows):
                        vec_f[k, base + 2 + i : base + 3 + i] = gub[:, i * lane : (i + 1) * lane]
                    lanes = lax.broadcasted_iota(jnp.int32, (1, lane), 1)
                    row = jnp.zeros((1, lane), F32)
                    for i in range(per):
                        row = row + jnp.where(
                            lanes == i, jnp.sum(order_sums[(k, i)], -1, keepdims=True), 0.0
                        )
                    vec_f[k, base + 2 + hid_rows : base + 3 + hid_rows] = row
            normed, rstd = normalize(x_ref[...].astype(F32))
            g = d_in[...]
            cut_slots(
                parts, own, (dx1[...] + norm_back(g, normed, rstd, gains[0:1])).astype(BF16)
            )
            shared[0:1] = jnp.sum(g * normed, 0, keepdims=True)
            shared[1:2] = vec[0:1]
            shared[2:3] = jnp.sum(g, 0, keepdims=True)
            shared[3:4] = vec[1:2]
            shared[4:5] = vec[2:3]
            shared[5:6] = vec[3:4]
            for gi, group in enumerate(groups):
                for j, k in enumerate(group):
                    for i in range(6):
                        for c in range(cols):
                            at = i * cols + c
                            vec_f[k, at : at + 1] = shared[i : i + 1, c * lane : (c + 1) * lane]
                    for p in range(n_dp):
                        v = vec_f[k, rows_of(dpi ^ p, VEC)]
                        to, q = place_of(gi, k, p, grads)
                        to[j // 2, q, 4 * sub :] = two_parts(v)

        back = run(
            "attend_back",
            attend_back,
            [lengths, order_mask, norm_scale_pair]
            + [x, a1, dx1, d_att, out_rows]
            + [qkv0, qkv1, p0, p1, att0, att1, wq0, wq1, wo0, wo1]
            + [vec, gub0, gub1_even, gub1_odd],
            [shape((2 * s.shape[0],) + s.shape[1:], BF16) for s in row_shapes]
            + [shape((len(g) // 2, n_dp, chunk, lane), BF16) for g in (g0, g0, g1)]
            + [shape((len(g1) // 2, half_dp, chunk, lane), BF16)] * 2,
            [
                *[pltpu.VMEM((3, count, lane * len(g)), BF16) for g in groups],
                *[pltpu.VMEM((4, width, lane * len(g)), BF16) for g in groups],
                pltpu.VMEM((count, width), F32),
                pltpu.VMEM((n_mp, vec_rows, lane), F32),
                pltpu.VMEM((8, width), F32),
            ],
            smem=(0,),
        )
        row_parts, (ka0, sa0, ka1, *sa1) = back[:-5], back[-5:]
        ga0, ga1 = mp_swap(sa0, 1), [mp_swap(v, 1) for v in sa1]

        def add_core_att(ins, outs, _):
            for n in range(n_y):
                for p in every:
                    got = ins[1 + p // half_dp][n, p % half_dp]
                    dst = outs[2 * n + p // half_dp]
                    dst[p % half_dp] = add_all([ins[0][n, p], got], True)

        others_a = run(
            "add_core_att",
            add_core_att,
            [ka1] + ga1,
            [shape((half_dp, chunk, lane), BF16)] * (2 * n_y),
        )

        def add_x(ins, outs, _):
            for n in range(1 + n_y):
                for i in range(n_dp // 2):
                    outs[n][i] = add_all([ins[0][n, i], ins[1][n, i]])

        mine_d, *others_d = run(
            "add_x", add_x, [kept_d, got_d], [shape((n_dp // 2, sub, hid), BF16)] * (1 + n_y)
        )
        kept_u, sent_u, at_u = add_split([mine_u] + got_u, every, 2)
        others_d, (sent_u,), others_a = together(others_d, [sent_u], others_a)
        got_d = spread_y(others_d)
        got_u = dp_swap(sent_u, 2)
        got_a = [mp_swap(v, y_peers[n // 2]) for n, v in enumerate(others_a)]

        kept_d, sent_d, at_d = add_split([mine_d] + got_d, no_x, 2)
        kept_u, sent_u, at_u = add_split([kept_u, got_u], at_u, 1)
        sent_d, sent_u = together([sent_d, sent_u])[0]
        got_d, got_u = dp_swap(sent_d, 2), dp_swap(sent_u, 1)

        def join(ins, outs, _):
            for n, mine in enumerate((ins[:2], ins[2:])):
                for i in range(outs[0].shape[0]):
                    outs[0][i, n] = add_all([v[i] for v in mine])

        (both,) = run(
            "join",
            join,
            [kept_d, got_d, kept_u, got_u],
            [shape((len(at_d), 2, sub, hid), BF16)],
        )
        at_both = at_d
        for bit in last_bits[:-1]:
            kept, sent, at_both = add_split([both], at_both, bit)
            both = add_whole([kept, dp_swap(sent, bit)])
        got = dp_swap(both, last_bits[-1])
        mine_a = [v.reshape(v.shape[1:]) for v in (ka0, ga0)]
        at_a, with_x = split(every, 1)
        kept_a, *sent_a = add_parts(
            [[v] for v in mine_a] + [got_a[n : n + 2] for n in range(0, 2 * n_y, 2)],
            [at_a, with_x[: len(with_x) // 2], with_x[len(with_x) // 2 :]],
        )
        got_a = [dp_swap(v, 1) for v in sent_a]
        keep, send = split(at_a, 2)
        kept_a, *sent_a = add_parts(
            [[kept_a], got_a], [keep, send[: len(send) // 2], send[len(send) // 2 :]]
        )
        got_a = [dp_swap(v, 2) for v in sent_a]
        at_a = [at_a[i] for i in keep]
        both = meet(both, got, at_both, last_bits[-1], False)
        for bit in reversed(last_bits[:-1]):
            both, at_both = jnp.concatenate([both, dp_swap(both, bit)]), at_both + [
                p ^ bit for p in at_both
            ]

        def part(ins, outs, _):
            for n, o in enumerate(outs):
                for i in range(len(at_both)):
                    o[i] = ins[0][i, n]

        down, up = run("part", part, [both], [shape((len(at_both), sub, hid), BF16)] * 2)

        (sum_a,) = add_parts([[kept_a], got_a], [list(range(len(at_a)))], [down])

        row_parts = list(row_parts)
        row_parts[2:] = spread_y(row_parts[2:])
        down, up = together([down, up])[0]
        got_d, got_u = dp_swap(down, 2), dp_swap(up, 1)
        for bit in last_bits[:-1]:
            kept_a, sent_a, at_a = add_split([sum_a], at_a, bit, True)
            sum_a = add_whole([kept_a, dp_swap(sent_a, bit)], True)
        got_a = dp_swap(sum_a, last_bits[-1])
        down, at_down = jnp.concatenate([down, got_d]), at_both + [p ^ 2 for p in at_both]
        up, at_up = jnp.concatenate([up, got_u]), at_both + [p ^ 1 for p in at_both]
        att = meet(sum_a, got_a, at_a, last_bits[-1], True)
        got_d, got_u = dp_swap(down, 1), dp_swap(up, 2)
        for bit in [*reversed(last_bits[:-1]), 2]:
            att = jnp.concatenate([att, dp_swap(att, bit)])
            at_a = at_a + [p ^ bit for p in at_a]
        (att, got_d, got_u), row_parts = together([att, got_d, got_u], row_parts)
        row_parts = [row_parts[0], mp_swap(row_parts[1], 1)] + pass_rows(row_parts[2:])
        got_a = dp_swap(att, 1)

        def finish_mlp(ins, outs, scratch):
            dpi = lax.axis_index("dp")
            for n, p in enumerate(at_down):
                for v, at in zip(ins[:2], (p, p ^ 1)):
                    scratch[0][rows_of(dpi ^ at, sub)] = v[n].astype(F32)
            for n, p in enumerate(at_up):
                for v, at in zip(ins[2:], (p, p ^ 2)):
                    outs[1][rows_of(dpi ^ at, sub)] = v[n].astype(F32)
            outs[0][...] = scratch[0][...].T
            outs[2][...] = jnp.zeros((8, LANES), F32)

        mark = shape((8, LANES), F32)
        r_down, r_up, mlp_mark = run(
            "finish_mlp",
            finish_mlp,
            [down, got_d, up, got_u],
            [shape((hid, width), F32), shape((width, hid), F32), mark],
            [pltpu.VMEM((width, hid), F32)],
        )

        def finish_att(ins, outs, scratch):
            r_qkv, r_out, gain, shift, outb, qvb, upb, order = outs
            turned_out, vec_f = scratch
            dpi = lax.axis_index("dp")
            for src, n, p in [(0, n, p) for n, p in enumerate(at_a)] + [
                (1, n, p ^ 1) for n, p in enumerate(at_a)
            ]:
                v = ins[src][n]
                at = dpi ^ p
                here = rows_of(at, sub)
                for t in range(3):
                    r_qkv[t, here] = v[t * sub : (t + 1) * sub].astype(F32)
                turned_out[here] = v[3 * sub : 4 * sub].astype(F32)
                pairs = v[4 * sub :].astype(F32)
                vec_f[rows_of(at, VEC)] = pairs[:VEC] + pairs[VEC:]
            r_out[...] = turned_out[...].T
            for i in range(6):
                dst = (gain, shift, outb)[i // 2]
                dst[i % 2 : i % 2 + 1] = jnp.concatenate(
                    [vec_f[i * cols + c : i * cols + c + 1] for c in range(cols)], 1
                )
            base = 6 * cols
            qvb[...] = vec_f[base : base + 2]
            upb[...] = jnp.concatenate(
                [vec_f[base + 2 + i : base + 3 + i] for i in range(hid_rows)], 1
            )
            order[...] = vec_f[base + 2 + hid_rows : base + 3 + hid_rows, :per]

        pair_shape = shape((2, width), F32)
        def gather_rows(ins, outs, _):
            me = lax.axis_index("mp")
            for k in range(n_mp):
                here = pl.ds((me ^ k) * own, own)
                outs[0][here] = ins[k][:own]
                outs[1][here] = ins[k][own : 2 * own].astype(F32)
            outs[2][...] = jnp.zeros((8, LANES), F32)

        output, token_gradient, rows_mark = run(
            "gather_rows",
            gather_rows,
            row_parts,
            [shape((rows, share, width), BF16), shape((rows, share, width), F32), mark],
        )
        r_qkv, r_out, gain, shift, outb, qvb, upb, order = run(
            "finish_att",
            finish_att,
            [att, got_a],
            [
                shape((3, width, lane), F32),
                shape((lane, width), F32),
                pair_shape,
                pair_shape,
                pair_shape,
                shape((2, lane), F32),
                shape((1, hid), F32),
                shape((1, per), F32),
            ],
            [pltpu.VMEM((width, lane), F32), pltpu.VMEM((vec_rows, lane), F32)],
            after=[mlp_mark, rows_mark],
        )

        return (
            output,
            token_gradient,
            gain,
            shift,
            r_qkv,
            qvb,
            order.reshape(per),
            r_out,
            outb,
            r_up,
            upb.reshape(hid),
            r_down,
        )

    return body


def solution(mesh):
    return jax.shard_map(
        make_body(mesh.shape["dp"], mesh.shape["mp"]),
        mesh=mesh,
        in_specs=(
            P("dp", "mp", None),
            P("dp"),
            P("dp", None),
            P(),
            P(),
            P(None, None, "mp"),
            P(None, "mp"),
            P("mp"),
            P("mp", None),
            P(),
            P(None, "mp"),
            P("mp"),
            P("mp", None),
            P("dp", "mp", None),
        ),
        out_specs=(
            P("dp", "mp", None),
            P("dp", "mp", None),
            P(),
            P(),
            P(None, None, "mp"),
            P(None, "mp"),
            P("mp"),
            P("mp", None),
            P(),
            P(None, "mp"),
            P("mp"),
            P("mp", None),
        ),
        check_vma=False,
    )
```

```python
import jax
import jax.numpy as jnp
from jax import lax
from jax.experimental import pallas as pl
from jax.experimental.pallas import tpu as pltpu
from jax.sharding import PartitionSpec as P

HD = 64
PAIR = 2 * HD
LANES = 128
F32 = jnp.float32
BF16 = jnp.bfloat16
VMEM_LIMIT = 28 * 2**20
VMEM_MOST = 60 * 2**20
GELU_C = 0.7978845608028654
GELU_A = 0.044715
VEC = 8


def swap(v, axis, bit, size):
    return lax.ppermute(v, axis, [(i, i ^ bit) for i in range(size)])


def bits_of(size):
    return [1 << b for b in range(size.bit_length() - 1)]


def shape(dims, kind):
    return jax.ShapeDtypeStruct(tuple(dims), kind)


def together(*lists):
    out = lax.optimization_barrier(tuple(tuple(v) for v in lists))
    return [list(v) for v in out]


def run(name, fn, ins, outs, scratch=(), smem=(), after=(), hbm=(), limit=VMEM_LIMIT):
    n_in, n_out, n_all = len(ins), len(outs), len(ins) + len(after)

    def kernel(*refs):
        fn(refs[:n_in], refs[n_all : n_all + n_out], refs[n_all + n_out :])

    return pl.pallas_call(
        kernel,
        out_shape=tuple(outs),
        in_specs=[
            pl.BlockSpec(
                memory_space=pltpu.SMEM if i in smem else pl.ANY if i in hbm else pltpu.VMEM
            )
            for i in range(n_in)
        ]
        + [pl.BlockSpec(memory_space=pl.ANY) for _ in after],
        out_specs=tuple(pl.BlockSpec(memory_space=pltpu.VMEM) for _ in outs),
        scratch_shapes=list(scratch),
        compiler_params=pltpu.CompilerParams(vmem_limit_bytes=limit),
        cost_estimate=pl.CostEstimate(flops=1, bytes_accessed=1, transcendentals=0),
        name=name,
    )(*ins, *after)


def dot(a, b):
    return jnp.dot(a, b, preferred_element_type=F32)


def dot_nt(a, b):
    return lax.dot_general(a, b, (((1,), (1,)), ((), ())), preferred_element_type=F32)


def dot_tn(a, b):
    return lax.dot_general(a, b, (((0,), (0,)), ((), ())), preferred_element_type=F32)


def normalize(v):
    centre = v - jnp.mean(v, -1, keepdims=True)
    rstd = lax.rsqrt(jnp.mean(centre * centre, -1, keepdims=True) + 1e-05)
    return centre * rstd, rstd


def norm_back(g, normed, rstd, gain):
    e = g * gain
    return rstd * (
        e - jnp.mean(e, -1, keepdims=True) - normed * jnp.mean(e * normed, -1, keepdims=True)
    )


def rows_of(start, size):
    return pl.ds(pl.multiple_of(start * size, size), size)


def in_order(a, b, bit):
    first = bit == 0
    return jnp.concatenate([jnp.where(first, a, b), jnp.where(first, b, a)], 0)


def whole(pieces, x_bit, z_bit=None):
    values = [v[...] for v in pieces]
    if len(values) == 4:
        return in_order(in_order(*values[:2], x_bit), in_order(*values[2:], x_bit), z_bit)
    return in_order(*values, x_bit) if len(values) == 2 else values[0]


def take(refs, counts):
    out, at = [], 0
    for c in counts:
        out.append(refs[at : at + c])
        at += c
    assert at == len(refs)
    return out


def three_parts(v):
    high = v.astype(BF16).astype(F32)
    rest = v - high
    middle = rest.astype(BF16).astype(F32)
    zeros = jnp.zeros((5 * v.shape[0], v.shape[1]), F32)
    return jnp.concatenate([high, middle, rest - middle, zeros], 0).astype(BF16)


def two_parts(v):
    high = v.astype(BF16).astype(F32)
    return jnp.concatenate([high, v - high], 0).astype(BF16)


def make_body(n_dp, n_mp):
    groups = [[0, 1], list(range(2, n_mp))]
    y_peers = list(range(2, n_mp, 2))
    def body(
        tokens,
        lengths,
        order_mask,
        norm_scale_pair,
        norm_offset_pair,
        w_qkv,
        qv_bias,
        order_bias,
        w_out,
        out_bias,
        w_up,
        up_bias,
        w_down,
        cotangent,
    ):
        rows, share, width = tokens.shape
        slots = order_mask.shape[1]
        own = rows // n_mp
        count = own * slots
        lane = qv_bias.shape[1]
        per = order_bias.shape[0]
        hid = up_bias.shape[0]
        hid_rows = hid // lane
        cols = width // lane
        piece = shape((own, share, width), BF16)
        sub = width // n_dp
        factor = HD**-0.5
        o_at, s_at = 3 * width, 4 * width
        bundle_rows = 4 * width + 8 * VEC

        def mp_swap(v, bit):
            return swap(v, "mp", bit, n_mp)

        def dp_swap(v, bit):
            return swap(v, "dp", bit, n_dp)

        def send_rows(core, pairs):
            return [mp_swap(core, 1)] + spread_y(pairs)

        def pass_rows(pairs):
            half = pairs[0].shape[0] // 2
            passed = [mp_swap(v[half:], 1) for v in pairs]
            return [p for pair in zip(pairs, passed) for p in pair]

        def over_y(v):
            return [mp_swap(v, k) for k in y_peers]

        def spread_y(parts):
            return [mp_swap(v, k) for k, v in zip(y_peers, parts)]

        row_shapes = [piece] * 2 + [shape((2 * own, share, width), BF16)] * len(y_peers)

        def cut_copies(src, outs, sems):
            me = lax.axis_index("mp")
            copies = []
            for k in range(n_mp):
                dst = outs[k] if k < 2 else outs[k // 2 + 1].at[pl.ds((k % 2) * own, own)]
                here = src.at[pl.ds((me ^ k) * own, own)]
                copies.append(pltpu.make_async_copy(here, dst, sems.at[k]))
            for c in copies:
                c.start()
            return copies

        def begin(ins, outs, scratch):
            dpi = lax.axis_index("dp")
            bundle, quarter = outs[-2:]
            copies = cut_copies(ins[0], outs, scratch[0])
            copies.append(
                pltpu.make_async_copy(ins[1], bundle.at[pl.ds(0, o_at)], scratch[1])
            )
            copies[-1].start()
            for c in range(cols):
                bundle[o_at + c * lane : o_at + (c + 1) * lane] = ins[2][
                    :, c * lane : (c + 1) * lane
                ]
            small = jnp.concatenate(
                [
                    ins[3][...],
                    ins[4][...],
                    jnp.concatenate([ins[5][...], jnp.zeros((1, lane - per), F32)], 1),
                    jnp.zeros((VEC - 3 - hid_rows, lane), F32),
                ],
                0,
            )
            bundle[s_at:] = three_parts(small)
            for c in copies:
                c.wait()
            mine = 2 * ((dpi >> 1) & 1) + (dpi & 1)
            quarter[...] = bundle[rows_of(mine, bundle_rows // 4)]

        *token_parts, bundle, bundle_quarter = run(
            "begin",
            begin,
            [
                tokens,
                w_qkv.reshape(-1, lane),
                w_out,
                qv_bias,
                up_bias.reshape(hid_rows, lane),
                order_bias.reshape(1, per),
            ],
            row_shapes
            + [shape((bundle_rows, lane), BF16), shape((bundle_rows // 4, lane), BF16)],
            [pltpu.SemaphoreType.DMA((n_mp,)), pltpu.SemaphoreType.DMA(())],
            hbm=(0, 1),
            limit=VMEM_MOST,
        )

        def cut_rest(ins, outs, scratch):
            dpi = lax.axis_index("dp")
            copies = cut_copies(ins[0], outs, scratch[0])
            halves = outs[len(row_shapes) :]
            for n, (src, bit) in enumerate(zip(ins[1:], (dpi & 1, (dpi >> 1) & 1))):
                here = src.at[rows_of(bit, src.shape[0] // 2)]
                dst = halves[0].at[n] if joined else halves[n]
                copies.append(pltpu.make_async_copy(here, dst, scratch[1].at[n]))
                copies[-1].start()
            for c in copies:
                c.wait()

        joined = w_up.shape == w_down.shape
        half_shapes = [shape((v.shape[0] // 2, v.shape[1]), BF16) for v in (w_up, w_down)]
        rest = run(
            "cut_rest",
            cut_rest,
            [cotangent, w_up, w_down],
            row_shapes
            + ([shape((2,) + half_shapes[0].shape, BF16)] if joined else half_shapes),
            [pltpu.SemaphoreType.DMA((n_mp,)), pltpu.SemaphoreType.DMA((2,))],
            hbm=(0, 1, 2),
            after=[bundle_quarter],
            limit=VMEM_MOST,
        )
        cot_parts, half_parts = list(rest[: len(row_shapes)]), rest[len(row_shapes) :]

        sends, (bundle, bundle_quarter) = together(token_parts[1:], [bundle, bundle_quarter])
        token_parts = token_parts[:1] + send_rows(sends[0], sends[1:])
        bundle_core, bundle_y = mp_swap(bundle, 1), over_y(bundle_quarter)

        near = [w_up, w_down]
        near_core = [mp_swap(v, 1) for v in near]
        bundle_y, (bundle_core,), token_parts[:2], near_core = together(
            bundle_y, [bundle_core], token_parts[:2], near_core
        )
        halves_y = [over_y(v) for v in half_parts]
        bundle_x, bundle_z = ([dp_swap(v, bit) for v in bundle_y] for bit in (1, 2))
        bundle_xz = [dp_swap(v, 2) for v in bundle_x]
        bundle_yc = [mp_swap(v, 1) for v in bundle_y]
        def unpacked(n):
            return [
                shape((3 * width, lane * n), BF16),
                shape((lane * n, width), BF16),
                shape((n, VEC, lane), F32),
            ]

        def unpack(pieces, outs, n):
            dpi = lax.axis_index("dp")
            weights, wo, smalls = outs
            for j, ps in enumerate(take(pieces, [len(pieces) // n] * n)):
                v = whole(ps, dpi & 1, (dpi >> 1) & 1)
                weights[:, j * lane : (j + 1) * lane] = v[:o_at]
                for c in range(cols):
                    wo[j * lane : (j + 1) * lane, c * lane : (c + 1) * lane] = v[
                        o_at + c * lane : o_at + (c + 1) * lane
                    ]
                parts = v[s_at:].astype(F32)
                smalls[j] = parts[:VEC] + parts[VEC : 2 * VEC] + parts[2 * VEC : 3 * VEC]

        near_unpacked = run(
            "unpack",
            lambda ins, outs, _: unpack(ins, outs, 2),
            [bundle, bundle_core],
            unpacked(2),
        )

        token_parts[2:], near_unpacked = together(token_parts[2:], near_unpacked)
        token_parts = token_parts[:2] + pass_rows(token_parts[2:])

        def far(even, odd):
            return [v[n] for n in range(len(y_peers)) for vs in (even, odd) for v in vs]

        def order_row(om_ref, me, r):
            v = om_ref[pl.ds(me * own + r, 1), :].astype(F32)
            v = jnp.broadcast_to(v, (8, slots))
            at = lax.broadcasted_iota(jnp.int32, (8, slots), 1)
            step = share
            while step < slots:
                turned = jnp.where(
                    (at & step) == 0, pltpu.roll(v, slots - step, 1), pltpu.roll(v, step, 1)
                )
                v = jnp.where((me * share) & step, turned, v)
                step *= 2
            return v[:1]

        def keep_row(me, length):
            at = lax.broadcasted_iota(jnp.int32, (1, slots), 1)
            return (at ^ (me * share)) < length

        def keep_column(me, length):
            at = lax.broadcasted_iota(jnp.int32, (slots, 1), 0)
            return ((at ^ (me * share)) < length).astype(F32)

        def head_mask(pair_value, h):
            at = lax.broadcasted_iota(jnp.int32, pair_value.shape, 1)
            return jnp.where((at >= HD) == (h % 2 == 1), pair_value, jnp.zeros_like(pair_value))

        def assemble(dst, parts):
            for r in range(own):
                for k in range(n_mp):
                    dst[r * slots + k * share : r * slots + (k + 1) * share] = parts[k][r]

        def cut_slots(dst, lead, value):
            for r in range(own):
                for k in range(n_mp):
                    at = r * slots + k * share
                    to, first = (dst[k], 0) if k < 2 else (dst[k // 2 + 1], (k % 2) * 2 * own)
                    to[first + lead + r] = value[at : at + share]

        def attend(group, first, pieces, ready=()):
            wide = lane * len(group)
            heads = wide // HD

            def fn(ins, outs, scratch):
                me, dpi = lax.axis_index("mp"), lax.axis_index("dp")
                if ready:
                    (weights, wo, smalls), (qkv_ref, p_ref, att_ref) = ins[-3:], outs[-3:]
                else:
                    qkv_ref, p_ref, att_ref, weights, wo, smalls = outs[-6:]
                if first:
                    lens, om, gains, shifts = ins[n_mp : n_mp + 4]
                    x_ref, a1_ref = outs[:2]
                    assemble(x_ref, ins[:n_mp])
                    normed, _ = normalize(x_ref[...].astype(F32))
                    a1_ref[...] = (normed * gains[0:1] + shifts[0:1]).astype(BF16)
                else:
                    lens, om, a1_ref = ins[:3]
                if not ready:
                    unpack(ins[-len(pieces) :], (weights, wo, smalls), len(group))
                a1 = a1_ref[...]
                for t in range(3):
                    y = dot(a1, weights[t * width : (t + 1) * width])
                    if t != 1:
                        i = t // 2
                        y = y + jnp.concatenate(
                            [smalls[j, i : i + 1] for j in range(len(group))], 1
                        )
                    qkv_ref[t] = y.astype(BF16)
                for r in range(own):
                    length = lens[me * own + r]
                    order = order_row(om, me, r)
                    kept = keep_row(me, length)
                    column = keep_column(me, length)
                    here = slice(r * slots, (r + 1) * slots)
                    for pair in range(heads // 2):
                        at = slice(pair * PAIR, (pair + 1) * PAIR)
                        q = qkv_ref[0, here, at] * jnp.asarray(factor, BF16)
                        key = qkv_ref[1, here, at]
                        val = qkv_ref[2, here, at]
                        acc = None
                        for h in (2 * pair, 2 * pair + 1):
                            o = 2 + hid_rows
                            ob = smalls[h // per, o : o + 1, h % per : h % per + 1]
                            row = jnp.where(kept, ob * order, -1e30)
                            s = dot_nt(head_mask(q, h), key) + row
                            e = jnp.exp(s - jnp.max(s, -1, keepdims=True))
                            p = (e * (1.0 / jnp.sum(e, -1, keepdims=True))).astype(BF16)
                            p_ref[r * heads + h] = p
                            term = dot(p, head_mask(val, h))
                            acc = term if acc is None else acc + term
                        att_ref[here, at] = (acc * column).astype(BF16)

            ins = (
                token_parts + [lengths, order_mask, norm_scale_pair, norm_offset_pair]
                if first
                else [lengths, order_mask, a1]
            )
            lead = [shape((count, width), BF16)] * 2 if first else []
            return run(
                "attend",
                fn,
                ins + (list(ready) or pieces),
                lead
                + [
                    shape((3, count, wide), BF16),
                    shape((own * heads, slots, slots), BF16),
                    shape((count, wide), BF16),
                ]
                + ([] if ready else unpacked(len(group))),
                smem=(n_mp if first else 0,),
            )

        x, a1, qkv0, p0, att0 = attend(groups[0], True, [], near_unpacked)
        wq0, wo0, small0 = near_unpacked

        bundle_x, bundle_z, bundle_xz, (att0,), sends = together(
            bundle_x, bundle_z, bundle_xz, [att0], cot_parts[1:]
        )
        cot_parts = cot_parts[:1] + send_rows(sends[0], sends[1:])
        bundle_xc, bundle_zc, bundle_xzc = (
            [mp_swap(v, 1) for v in vs] for vs in (bundle_x, bundle_z, bundle_xz)
        )
        qkv1, p1, att1, wq1, wo1, small1 = attend(
            groups[1], False, far(
                (bundle_y, bundle_x, bundle_z, bundle_xz),
                (bundle_yc, bundle_xc, bundle_zc, bundle_xzc),
            )
        )

        def take_apart(ins, outs, _):
            for n, o in enumerate(outs):
                o[...] = ins[0][n]

        if joined:
            pairs = [run("take_apart", take_apart, [v], half_shapes, after=[att1]) for v in halves_y[0]]
            halves_y = list(zip(*pairs))
        up_y, down_y, (att1,), cot_parts[1:2] = together(*halves_y, [att1], cot_parts[1:2])
        up_x, down_z = [dp_swap(v, 1) for v in up_y], [dp_swap(v, 2) for v in down_y]
        up_yc, down_yc = ([mp_swap(v, 1) for v in vs] for vs in (up_y, down_y))

        def scatter(dst, src, block, which, dpi):
            for p in range(n_dp):
                dst[block, which, p] = src[rows_of(dpi ^ p, sub), :]

        def mlp_forward(a2, wu, wd, bias, mixed):
            up = jnp.concatenate([bias[2 + i : 3 + i] for i in range(hid_rows)], 1)
            pre = dot(a2[...], wu) + up
            square = pre * pre
            t = jnp.tanh(pre * (GELU_C + (GELU_C * GELU_A) * square))
            half = 0.5 + 0.5 * t
            hidden = (pre * half).astype(BF16)
            slope = half + (pre * (1.0 - t * t)) * (
                0.5 * GELU_C + (1.5 * GELU_C * GELU_A) * square
            )
            mixed[...] += dot(hidden, wd)
            return hidden, slope

        def mlp_backward(hidden, slope, a2t, dy, dyt, wu, wd, d_mid, gs, dst, block, bias_sum, dpi):
            d_hidden = dot_nt(dy[...], wd)
            d_pre = (slope * d_hidden).astype(BF16)
            d_mid[...] += dot_nt(d_pre, wu)
            g_down, g_up = gs.at[0], gs.at[1]
            g_down[...] = dot(dyt[...], hidden).astype(BF16)
            scatter(dst, g_down, block, 0, dpi)
            g_up[...] = dot(a2t[...], d_pre).astype(BF16)
            scatter(dst, g_up, block, 1, dpi)
            bias_sum[...] = jnp.sum(d_pre.astype(F32), 0, keepdims=True)

        def mlp_outs(n_blocks, n_arrays):
            both = shape((n_blocks // n_arrays, 2, n_dp, sub, hid), BF16)
            return [both] * n_arrays + [shape((n_blocks, 1, hid), F32)]

        full = shape((count, width), F32)
        full_bf = shape((count, width), BF16)
        turned = shape((width, count), BF16)
        g0, g1 = groups

        def mlp_near_forward(ins, outs, _):
            lead, wu_p, wd_p = take(ins, [9, len(g0), len(g0)])
            x_ref, att0_ref, att1_ref, wo0_ref, wo1_ref, smalls, gains, shifts, ob = lead
            x1, a2, a2t, mixed, hidden, slope = outs
            v = x_ref[...].astype(F32) + (
                dot(att0_ref[...], wo0_ref[...]) + dot(att1_ref[...], wo1_ref[...]) + ob[0:1]
            )
            x1[...] = v
            normed, _ = normalize(v)
            act = (normed * gains[1:2] + shifts[1:2]).astype(BF16)
            a2[...] = act
            a2t[...] = act.T
            mixed[...] = jnp.zeros_like(mixed)
            for j in range(len(g0)):
                hidden[j], slope[j] = mlp_forward(
                    a2, wu_p[j][...], wd_p[j][...], smalls.at[j], mixed
                )

        near_up, near_down = [near[0], near_core[0]], [near[1], near_core[1]]
        x1, a2, a2t, mixed, hidden, slope = run(
            "mlp_near_forward",
            mlp_near_forward,
            [x, att0, att1, wo0, wo1, small0, norm_scale_pair, norm_offset_pair, out_bias]
            + near_up
            + near_down,
            [full, full_bf, turned, full]
            + [shape((len(g0), count, hid), BF16), shape((len(g0), count, hid), F32)],
        )

        cot_parts[2:], (a2,) = together(cot_parts[2:], [a2])
        cot_parts = cot_parts[:2] + pass_rows(cot_parts[2:])

        def mlp_near_backward(ins, outs, scratch):
            dpi = lax.axis_index("dp")
            (hidden, slope, a2t), dy_p, wu_p, wd_p = take(ins, [3, n_mp, len(g0), len(g0)])
            dy, dyt, d_mid = outs[:3]
            assemble(dy, dy_p)
            dyt[...] = dy[...].T
            d_mid[...] = jnp.zeros_like(d_mid)
            for j, k in enumerate(g0):
                mlp_backward(
                    hidden[j],
                    slope[j],
                    a2t,
                    dy,
                    dyt,
                    wu_p[j][...],
                    wd_p[j][...],
                    d_mid,
                    scratch[j],
                    outs[3 + k % 2],
                    0,
                    outs[5].at[j],
                    dpi,
                )

        dy, dyt, d_mid, keep0, send0, gub0 = run(
            "mlp_near_backward",
            mlp_near_backward,
            [hidden, slope, a2t] + cot_parts + near_up + near_down,
            [full_bf, turned, full] + mlp_outs(len(g0), 2),
            [pltpu.VMEM((2, width, hid), BF16)] * len(g0),
        )

        up_yc, up_x, down_yc, down_z, (gub0,) = together(up_yc, up_x, down_yc, down_z, [gub0])
        up_xc, down_zc = ([mp_swap(v, 1) for v in vs] for vs in (up_x, down_z))
        got0 = mp_swap(send0, 1)

        up1 = far((up_y, up_x), (up_yc, up_xc))
        down1 = far((down_y, down_z), (down_yc, down_zc))

        def mlp_far(j, last):
            ks = g1[j::2]
            n_w = 2 * len(ks)

            def fn(ins, outs, scratch):
                dpi = lax.axis_index("dp")
                lead, wu_p, wd_p, done = take(ins, [10, n_w, n_w, 2 if last else 0])
                x1, a2, a2t, dy, dyt, mixed_in, d_mid_in, smalls, gains, ob = lead
                (mixed, d_mid), gs = (scratch[:2], scratch[2:]) if last else (outs[:2], scratch)
                mixed[...] = mixed_in[...]
                d_mid[...] = d_mid_in[...]
                grads, bias_sums = outs[-2:]
                for n in range(len(ks)):
                    wu = whole(wu_p[2 * n : 2 * n + 2], dpi & 1)
                    wd = whole(wd_p[2 * n : 2 * n + 2], (dpi >> 1) & 1)
                    if last:
                        hidden, slope = done[0][n], done[1][n]
                    else:
                        hidden, slope = mlp_forward(a2, wu, wd, smalls.at[2 * n + j], mixed)
                    mlp_backward(
                        hidden,
                        slope,
                        a2t,
                        dy,
                        dyt,
                        wu,
                        wd,
                        d_mid,
                        gs[n],
                        grads,
                        n,
                        bias_sums.at[n],
                        dpi,
                    )
                if not last:
                    return
                output, dx1, d_att, vec = outs[:4]
                v = x1[...]
                output[...] = (v + (mixed[...] + ob[1:2])).astype(BF16)
                normed, rstd = normalize(v)
                g = d_mid[...]
                dyf = dy[...].astype(F32)
                d = dyf + norm_back(g, normed, rstd, gains[1:2])
                dx1[...] = d
                low = d.astype(BF16)
                d_att[...] = low
                vec[0:1] = jnp.sum(g * normed, 0, keepdims=True)
                vec[1:2] = jnp.sum(g, 0, keepdims=True)
                vec[2:3] = jnp.sum(low.astype(F32), 0, keepdims=True)
                vec[3:4] = jnp.sum(dyf, 0, keepdims=True)

            sums = [pltpu.VMEM((count, width), F32)] * 2
            return run(
                "mlp_far",
                fn,
                [x1, a2, a2t, dy, dyt, mixed, d_mid, small1, norm_scale_pair, out_bias]
                + [v for n in range(len(ks)) for v in up1[4 * n + 2 * j : 4 * n + 2 * j + 2]]
                + [v for n in range(len(ks)) for v in down1[4 * n + 2 * j : 4 * n + 2 * j + 2]]
                + ([far_hidden, far_slope] if last else []),
                ([full_bf, full, full_bf, shape((4, width), F32)] if last else [full, full])
                + mlp_outs(len(ks), 1),
                (sums if last else []) + [pltpu.VMEM((2, width, hid), BF16)] * len(ks),
            )

        def mlp_even_forward(ins, outs, _):
            dpi = lax.axis_index("dp")
            n_w = 2 * len(y_peers)
            (a2, mixed_in, smalls), wu_p, wd_p = take(ins, [3, n_w, n_w])
            mixed, hidden, slope = outs
            mixed[...] = mixed_in[...]
            for n in range(len(y_peers)):
                wu = whole(wu_p[2 * n : 2 * n + 2], dpi & 1)
                wd = whole(wd_p[2 * n : 2 * n + 2], (dpi >> 1) & 1)
                hidden[n], slope[n] = mlp_forward(a2, wu, wd, smalls.at[2 * n], mixed)

        mixed, far_hidden, far_slope = run(
            "mlp_even_forward",
            mlp_even_forward,
            [a2, mixed, small1]
            + [v for pair in zip(up_y, up_x) for v in pair]
            + [v for pair in zip(down_y, down_z) for v in pair],
            [full]
            + [shape((len(y_peers), count, hid), kind) for kind in (BF16, F32)],
        )
        mixed, d_mid, send1, gub1_odd = mlp_far(1, False)
        send1, mixed = together([send1, mixed])[0]
        got1 = mp_swap(send1, 1)
        out_rows, dx1, d_att, vec, keep1, gub1_even = mlp_far(0, True)

        def add_all(values, vectors=False):
            total = values[0].astype(F32)
            for v in values[1:]:
                total = total + v.astype(F32)
            if not vectors:
                return total.astype(BF16)
            m = total.shape[-2]
            head = total[: m - 2 * VEC]
            v = total[m - 2 * VEC : m - VEC] + total[m - VEC :]
            high = v.astype(BF16).astype(F32)
            return jnp.concatenate([head, high, v - high], 0).astype(BF16)

        n_y = len(y_peers)

        def split(places, bit):
            return [i for i, p in enumerate(places) if not p & bit], [
                i for i, p in enumerate(places) if p & bit
            ]

        def add_split(parts, places, bit, vectors=False, after=(), two=False, halves=()):
            picks = split(places, bit)
            n_parts, n_half = len(parts), len(places) // 2

            def fn(ins, outs, _):
                for pick, dsts in zip(picks, (outs[:1], outs[1:])):
                    for at, i in enumerate(pick):
                        values = [v[i] for v in ins[:n_parts]]
                        if halves:
                            values.append(ins[n_parts + i // n_half][i % n_half])
                        size = dsts[0].shape[0]
                        dsts[at // size][at % size] = add_all(values, vectors)

            n, rest = len(picks[0]), parts[0].shape[1:]
            sizes = [n] + ([n // 2] * 2 if two else [n])
            kept, *sent = run(
                "add_split",
                fn,
                list(parts) + list(halves),
                [shape((k,) + rest, BF16) for k in sizes],
                after=after,
            )
            return kept, sent if two else sent[0], [places[i] for i in picks[0]]

        def add_parts(parts, picks, after=()):
            counts = [len(p) for p in parts]

            def fn(ins, outs, _):
                for dst, pick in zip(outs, picks):
                    for at, i in enumerate(pick):
                        values = []
                        for refs in take(ins, counts):
                            n = refs[0].shape[0]
                            values.append(refs[i // n][i % n])
                        dst[at] = add_all(values, True)

            flat_parts = [v for p in parts for v in p]
            rest = flat_parts[0].shape[1:]
            outs = [shape((len(p),) + rest, BF16) for p in picks]
            return run("add_parts", fn, flat_parts, outs, after=after)

        def add_whole(parts, vectors=False):
            def fn(ins, outs, _):
                for i in range(outs[0].shape[0]):
                    outs[0][i] = add_all([v[i] for v in ins], vectors)

            return run("add_whole", fn, parts, [shape(parts[0].shape, BF16)])[0]

        def meet(mine, got, places, bit, vectors):
            def fn(ins, outs, _):
                for i, p in enumerate(places):
                    outs[0][i] = add_all([ins[0][i], ins[1][places.index(p ^ bit)]], vectors)

            return run("meet", fn, [mine, got], [shape(mine.shape, BF16)])[0]

        every = list(range(n_dp))
        no_x, with_x = split(every, 1)
        last_bits = [b for b in bits_of(n_dp) if b > 2]

        def add_core_mlp(ins, outs, _):
            keep0, got0, keep1, got1 = ins
            kept, sent, mine = outs[:3]
            for n in range(1 + n_y):
                a, b, i = (keep0, got0, 0) if n == 0 else (keep1, got1, n - 1)
                for dst, pick in ((kept, no_x), (sent, with_x)):
                    for at, p in enumerate(pick):
                        dst[n, at] = add_all([a[i, 0, p], b[i, 0, p]])
                up = mine if n == 0 else outs[3 + n - 1]
                for p in every:
                    up[p] = add_all([a[i, 1, p], b[i, 1, p]])

        kept_d, sent_d, mine_u, *others_u = run(
            "add_core_mlp",
            add_core_mlp,
            [keep0, got0, keep1, got1],
            [shape((1 + n_y, n_dp // 2, sub, hid), BF16)] * 2
            + [shape((n_dp, sub, hid), BF16)] * (1 + n_y),
        )
        (sent_d, d_att), others_u = together([sent_d, d_att], others_u)
        got_d = dp_swap(sent_d, 1)
        got_u = spread_y(others_u)

        vec_rows = n_dp * VEC
        chunk = 4 * sub + 2 * VEC

        half_dp = n_dp // 2

        def place_of(gi, k, p, grads):
            if gi == 1 and k % 2:
                return grads[3 + p // half_dp], p % half_dp
            return grads[2 * gi + k % 2], p

        def attend_back(ins, outs, scratch):
            me, dpi = lax.axis_index("mp"), lax.axis_index("dp")
            (lens, om, gains), fulls, qkvs, ps, atts, wqs, wos, vecs = take(
                ins, [3, 5, 2, 2, 2, 2, 2, 4]
            )
            x_ref, a1_ref, dx1, d_att, out_ref = fulls
            vec, gub_near, gub_even, gub_odd = vecs
            parts, grads = outs[:-5], outs[-5:]
            dqkvs, gqs = scratch[:2], scratch[2:4]
            d_in, vec_f, shared = scratch[4:]
            a1t = a1_ref[...].T
            d_att_v = d_att[...]
            d_att_t = d_att_v.T
            d_in[...] = jnp.zeros_like(d_in)
            cut_slots(parts, 0, out_ref[...])
            order_sums = {}
            for gi, group in enumerate(groups):
                wide = lane * len(group)
                heads = wide // HD
                qkv_ref, p_ref, att_ref = qkvs[gi], ps[gi], atts[gi]
                wq, wo, dqkv, gq = wqs[gi], wos[gi], dqkvs[gi], gqs[gi]
                d_o = dot_nt(d_att_v, wo[...]).astype(BF16)
                for r in range(own):
                    length = lens[me * own + r]
                    order = order_row(om, me, r)
                    kept = keep_row(me, length)
                    column = keep_column(me, length).astype(BF16)
                    here = slice(r * slots, (r + 1) * slots)
                    for pair in range(heads // 2):
                        at = slice(pair * PAIR, (pair + 1) * PAIR)
                        q = qkv_ref[0, here, at] * jnp.asarray(factor, BF16)
                        key = qkv_ref[1, here, at] * jnp.asarray(factor, BF16)
                        val = qkv_ref[2, here, at]
                        do = d_o[here, at] * column
                        dq = dk = dv = 0.0
                        for h in (2 * pair, 2 * pair + 1):
                            p_low = p_ref[r * heads + h]
                            p = p_low.astype(F32)
                            do_h = head_mask(do, h)
                            d_p = dot_nt(do_h, val)
                            inner = jnp.sum(p * d_p, -1, keepdims=True)
                            inner = inner / jnp.sum(p, -1, keepdims=True)
                            d_s = jnp.where(kept, p * (d_p - inner), 0.0).astype(BF16)
                            sums = dot(jnp.ones((8, slots), BF16), d_s)[:1] * order
                            name = (group[h // per], h % per)
                            old = order_sums.get(name)
                            order_sums[name] = sums if old is None else old + sums
                            dq = dq + dot(d_s, head_mask(key, h))
                            dk = dk + dot_tn(d_s, head_mask(q, h))
                            dv = dv + dot_tn(p_low, do_h)
                        dqkv[0, here, at] = dq.astype(BF16)
                        dqkv[1, here, at] = dk.astype(BF16)
                        dqkv[2, here, at] = dv.astype(BF16)
                total = None
                for t in range(3):
                    g = dqkv[t]
                    gq[t] = dot(a1t, g).astype(BF16)
                    term = dot_nt(g, wq[t * width : (t + 1) * width])
                    total = term if total is None else total + term
                d_in[...] += total
                gq[3] = dot(d_att_t, att_ref[...]).astype(BF16)
                for j, k in enumerate(group):
                    at = slice(j * lane, (j + 1) * lane)
                    for p in range(n_dp):
                        here = rows_of(dpi ^ p, sub)
                        to, q = place_of(gi, k, p, grads)
                        for t in range(4):
                            to[j // 2, q, t * sub : (t + 1) * sub] = gq[t, here, at]
                    vec_f[k] = jnp.zeros((vec_rows, lane), F32)
                    base = 6 * cols
                    for n, t in enumerate((0, 2)):
                        vec_f[k, base + n : base + n + 1] = jnp.sum(
                            dqkv[t, :, at].astype(F32), 0, keepdims=True
                        )
                    gub = gub_near[j] if gi == 0 else (gub_even, gub_odd)[j % 2][j // 2]
                    for i in range(hid_rows):
                        vec_f[k, base + 2 + i : base + 3 + i] = gub[:, i * lane : (i + 1) * lane]
                    lanes = lax.broadcasted_iota(jnp.int32, (1, lane), 1)
                    row = jnp.zeros((1, lane), F32)
                    for i in range(per):
                        row = row + jnp.where(
                            lanes == i, jnp.sum(order_sums[(k, i)], -1, keepdims=True), 0.0
                        )
                    vec_f[k, base + 2 + hid_rows : base + 3 + hid_rows] = row
            normed, rstd = normalize(x_ref[...].astype(F32))
            g = d_in[...]
            cut_slots(
                parts, own, (dx1[...] + norm_back(g, normed, rstd, gains[0:1])).astype(BF16)
            )
            shared[0:1] = jnp.sum(g * normed, 0, keepdims=True)
            shared[1:2] = vec[0:1]
            shared[2:3] = jnp.sum(g, 0, keepdims=True)
            shared[3:4] = vec[1:2]
            shared[4:5] = vec[2:3]
            shared[5:6] = vec[3:4]
            for gi, group in enumerate(groups):
                for j, k in enumerate(group):
                    for i in range(6):
                        for c in range(cols):
                            at = i * cols + c
                            vec_f[k, at : at + 1] = shared[i : i + 1, c * lane : (c + 1) * lane]
                    for p in range(n_dp):
                        v = vec_f[k, rows_of(dpi ^ p, VEC)]
                        to, q = place_of(gi, k, p, grads)
                        to[j // 2, q, 4 * sub :] = two_parts(v)

        back = run(
            "attend_back",
            attend_back,
            [lengths, order_mask, norm_scale_pair]
            + [x, a1, dx1, d_att, out_rows]
            + [qkv0, qkv1, p0, p1, att0, att1, wq0, wq1, wo0, wo1]
            + [vec, gub0, gub1_even, gub1_odd],
            [shape((2 * s.shape[0],) + s.shape[1:], BF16) for s in row_shapes]
            + [shape((len(g) // 2, n_dp, chunk, lane), BF16) for g in (g0, g0, g1)]
            + [shape((len(g1) // 2, half_dp, chunk, lane), BF16)] * 2,
            [
                *[pltpu.VMEM((3, count, lane * len(g)), BF16) for g in groups],
                *[pltpu.VMEM((4, width, lane * len(g)), BF16) for g in groups],
                pltpu.VMEM((count, width), F32),
                pltpu.VMEM((n_mp, vec_rows, lane), F32),
                pltpu.VMEM((8, width), F32),
            ],
            smem=(0,),
        )
        row_parts, (ka0, sa0, ka1, *sa1) = back[:-5], back[-5:]
        ga0, ga1 = mp_swap(sa0, 1), [mp_swap(v, 1) for v in sa1]

        def add_core_att(ins, outs, _):
            for n in range(n_y):
                for p in every:
                    got = ins[1 + p // half_dp][n, p % half_dp]
                    dst = outs[2 * n + p // half_dp]
                    dst[p % half_dp] = add_all([ins[0][n, p], got], True)

        others_a = run(
            "add_core_att",
            add_core_att,
            [ka1] + ga1,
            [shape((half_dp, chunk, lane), BF16)] * (2 * n_y),
        )

        def add_x(ins, outs, _):
            for n in range(1 + n_y):
                for i in range(n_dp // 2):
                    outs[n][i] = add_all([ins[0][n, i], ins[1][n, i]])

        mine_d, *others_d = run(
            "add_x", add_x, [kept_d, got_d], [shape((n_dp // 2, sub, hid), BF16)] * (1 + n_y)
        )
        kept_u, sent_u, at_u = add_split([mine_u] + got_u, every, 2)
        others_d, (sent_u,), others_a = together(others_d, [sent_u], others_a)
        got_d = spread_y(others_d)
        got_u = dp_swap(sent_u, 2)
        got_a = [mp_swap(v, y_peers[n // 2]) for n, v in enumerate(others_a)]

        kept_d, sent_d, at_d = add_split([mine_d] + got_d, no_x, 2)
        kept_u, sent_u, at_u = add_split([kept_u, got_u], at_u, 1)
        sent_d, sent_u = together([sent_d, sent_u])[0]
        got_d, got_u = dp_swap(sent_d, 2), dp_swap(sent_u, 1)

        def join(ins, outs, _):
            for n, mine in enumerate((ins[:2], ins[2:])):
                for i in range(outs[0].shape[0]):
                    outs[0][i, n] = add_all([v[i] for v in mine])

        (both,) = run(
            "join",
            join,
            [kept_d, got_d, kept_u, got_u],
            [shape((len(at_d), 2, sub, hid), BF16)],
        )
        at_both = at_d
        for bit in last_bits[:-1]:
            kept, sent, at_both = add_split([both], at_both, bit)
            both = add_whole([kept, dp_swap(sent, bit)])
        got = dp_swap(both, last_bits[-1])
        mine_a = [v.reshape(v.shape[1:]) for v in (ka0, ga0)]
        at_a, with_x = split(every, 1)
        kept_a, *sent_a = add_parts(
            [[v] for v in mine_a] + [got_a[n : n + 2] for n in range(0, 2 * n_y, 2)],
            [at_a, with_x[: len(with_x) // 2], with_x[len(with_x) // 2 :]],
        )
        got_a = [dp_swap(v, 1) for v in sent_a]
        keep, send = split(at_a, 2)
        kept_a, *sent_a = add_parts(
            [[kept_a], got_a], [keep, send[: len(send) // 2], send[len(send) // 2 :]]
        )
        got_a = [dp_swap(v, 2) for v in sent_a]
        at_a = [at_a[i] for i in keep]
        both = meet(both, got, at_both, last_bits[-1], False)
        for bit in reversed(last_bits[:-1]):
            both, at_both = jnp.concatenate([both, dp_swap(both, bit)]), at_both + [
                p ^ bit for p in at_both
            ]

        def part(ins, outs, _):
            for n, o in enumerate(outs):
                for i in range(len(at_both)):
                    o[i] = ins[0][i, n]

        down, up = run("part", part, [both], [shape((len(at_both), sub, hid), BF16)] * 2)

        (sum_a,) = add_parts([[kept_a], got_a], [list(range(len(at_a)))], [down])

        row_parts = list(row_parts)
        row_parts[2:] = spread_y(row_parts[2:])
        down, up = together([down, up])[0]
        got_d, got_u = dp_swap(down, 2), dp_swap(up, 1)
        for bit in last_bits[:-1]:
            kept_a, sent_a, at_a = add_split([sum_a], at_a, bit, True)
            sum_a = add_whole([kept_a, dp_swap(sent_a, bit)], True)
        got_a = dp_swap(sum_a, last_bits[-1])
        down, at_down = jnp.concatenate([down, got_d]), at_both + [p ^ 2 for p in at_both]
        up, at_up = jnp.concatenate([up, got_u]), at_both + [p ^ 1 for p in at_both]
        att = meet(sum_a, got_a, at_a, last_bits[-1], True)
        got_d, got_u = dp_swap(down, 1), dp_swap(up, 2)
        for bit in [*reversed(last_bits[:-1]), 2]:
            att = jnp.concatenate([att, dp_swap(att, bit)])
            at_a = at_a + [p ^ bit for p in at_a]
        (att, got_d, got_u), row_parts = together([att, got_d, got_u], row_parts)
        row_parts = [row_parts[0], mp_swap(row_parts[1], 1)] + pass_rows(row_parts[2:])
        got_a = dp_swap(att, 1)

        def finish_mlp(ins, outs, scratch):
            dpi = lax.axis_index("dp")
            for n, p in enumerate(at_down):
                for v, at in zip(ins[:2], (p, p ^ 1)):
                    scratch[0][rows_of(dpi ^ at, sub)] = v[n].astype(F32)
            for n, p in enumerate(at_up):
                for v, at in zip(ins[2:], (p, p ^ 2)):
                    outs[1][rows_of(dpi ^ at, sub)] = v[n].astype(F32)
            outs[0][...] = scratch[0][...].T
            outs[2][...] = jnp.zeros((8, LANES), F32)

        mark = shape((8, LANES), F32)
        r_down, r_up, mlp_mark = run(
            "finish_mlp",
            finish_mlp,
            [down, got_d, up, got_u],
            [shape((hid, width), F32), shape((width, hid), F32), mark],
            [pltpu.VMEM((width, hid), F32)],
        )

        def finish_att(ins, outs, scratch):
            r_qkv, r_out, gain, shift, outb, qvb, upb, order = outs
            turned_out, vec_f = scratch
            dpi = lax.axis_index("dp")
            for src, n, p in [(0, n, p) for n, p in enumerate(at_a)] + [
                (1, n, p ^ 1) for n, p in enumerate(at_a)
            ]:
                v = ins[src][n]
                at = dpi ^ p
                here = rows_of(at, sub)
                for t in range(3):
                    r_qkv[t, here] = v[t * sub : (t + 1) * sub].astype(F32)
                turned_out[here] = v[3 * sub : 4 * sub].astype(F32)
                pairs = v[4 * sub :].astype(F32)
                vec_f[rows_of(at, VEC)] = pairs[:VEC] + pairs[VEC:]
            r_out[...] = turned_out[...].T
            for i in range(6):
                dst = (gain, shift, outb)[i // 2]
                dst[i % 2 : i % 2 + 1] = jnp.concatenate(
                    [vec_f[i * cols + c : i * cols + c + 1] for c in range(cols)], 1
                )
            base = 6 * cols
            qvb[...] = vec_f[base : base + 2]
            upb[...] = jnp.concatenate(
                [vec_f[base + 2 + i : base + 3 + i] for i in range(hid_rows)], 1
            )
            order[...] = vec_f[base + 2 + hid_rows : base + 3 + hid_rows, :per]

        pair_shape = shape((2, width), F32)
        def gather_rows(ins, outs, _):
            me = lax.axis_index("mp")
            for k in range(n_mp):
                here = pl.ds((me ^ k) * own, own)
                outs[0][here] = ins[k][:own]
                outs[1][here] = ins[k][own : 2 * own].astype(F32)
            outs[2][...] = jnp.zeros((8, LANES), F32)

        output, token_gradient, rows_mark = run(
            "gather_rows",
            gather_rows,
            row_parts,
            [shape((rows, share, width), BF16), shape((rows, share, width), F32), mark],
        )
        r_qkv, r_out, gain, shift, outb, qvb, upb, order = run(
            "finish_att",
            finish_att,
            [att, got_a],
            [
                shape((3, width, lane), F32),
                shape((lane, width), F32),
                pair_shape,
                pair_shape,
                pair_shape,
                shape((2, lane), F32),
                shape((1, hid), F32),
                shape((1, per), F32),
            ],
            [pltpu.VMEM((width, lane), F32), pltpu.VMEM((vec_rows, lane), F32)],
            after=[mlp_mark, rows_mark],
        )

        return (
            output,
            token_gradient,
            gain,
            shift,
            r_qkv,
            qvb,
            order.reshape(per),
            r_out,
            outb,
            r_up,
            upb.reshape(hid),
            r_down,
        )

    return body


def solution(mesh):
    return jax.shard_map(
        make_body(mesh.shape["dp"], mesh.shape["mp"]),
        mesh=mesh,
        in_specs=(
            P("dp", "mp", None),
            P("dp"),
            P("dp", None),
            P(),
            P(),
            P(None, None, "mp"),
            P(None, "mp"),
            P("mp"),
            P("mp", None),
            P(),
            P(None, "mp"),
            P("mp"),
            P("mp", None),
            P("dp", "mp", None),
        ),
        out_specs=(
            P("dp", "mp", None),
            P("dp", "mp", None),
            P(),
            P(),
            P(None, None, "mp"),
            P(None, "mp"),
            P("mp"),
            P("mp", None),
            P(),
            P(None, "mp"),
            P("mp"),
            P("mp", None),
        ),
        check_vma=False,
    )
```
